256 devices in a mesh: dp: 64 (over z, x, core), mp: 4 (over y).
Axes of the slice: x: 4, y: 4, z: 8, core: 2. Of those that a mesh axis runs over, the one named last changes fastest.
Arguments:
- imp_x: bfloat16 [8192, 512], P('dp'), may hold values from -6 to 6
- imp_hist: int32 [8192, 1], P('dp'), may hold values from 0 to 63; in each aligned block of 128 rows (0 to 127, 128 to 255, ...) at most 8 rows name the same one
- imp_len: int32 [8192], P('dp'), may hold values from 512 to 2048, as said below
- owner_map: int32 [64], replicated, may hold values from 0 to 63, each once
- hist_x: bfloat16 [64, 2048, 512], P('dp'), may hold values from -6 to 6
- w_in: bfloat16 [4, 512, 512], P(None, None, 'mp'), may hold values from -0.25 to 0.25
- w_out: bfloat16 [512, 512], P('mp'), may hold values from -0.25 to 0.25
- grad_y: bfloat16 [8192, 512], P('dp'), may hold values from -6 to 6
Outputs:
- grad_x: bfloat16 [8192, 512], P(('dp', 'mp'))
- grad_kv: bfloat16 [64, 2048, 2, 512], P('dp', None, None, 'mp')
- grad_w_in: float32 [4, 512, 512], P(None, None, 'mp')
- grad_w_out: float32 [512, 512], P('mp')
The draws below stay inside these ranges and needn't reach their ends.
Inputs may be any that keep to these rules, and one draw needn't show every extreme that they name: `imp_hist`: row i names the history of impression i. Among the 128 impressions of one log shard no history is named more than 8 times. `imp_len`: every device's block of impressions holds one that sees all 2048 events. A permutation: history h is held by device owner_map[h] of dp, as row owner_map[h] of hist_x.
All inputs are finite; a program needn't handle non-finite values.
Results may differ from the reference program's by a relative error of at most 0.01.
Values may be sent and summed in bfloat16 or wider, within the bound.
No kernel may reach another device: no remote copies, remote signals or barrier semaphores. Data moves between devices by JAX's collectives and lax.ppermute only.
A program may use at most 64 MiB of HBM per device.

```python
import math
import jax
import jax.numpy as jnp
import numpy as np
from jax import lax

D = 512
DH = 64
HD = 512
L = 2048
IMP_DEV = 128
HISTS = 64
IMPS = 8192
CAP = 8
N_DP = 64


def draw_imp_len(key, part):
    key = jax.random.fold_in(key, 7)
    length_key, anchor_key = jax.random.split(key)
    lengths = jax.random.randint(length_key, (IMPS,), L // 4, L + 1, dtype=jnp.int32)
    anchors = jax.random.randint(anchor_key, (N_DP,), 0, IMP_DEV, dtype=jnp.int32)
    anchors = anchors + jnp.arange(N_DP, dtype=jnp.int32) * IMP_DEV
    return lengths.at[anchors].set(L)


def levels(rng, shape, cuts, smallest, high):
    factor_of, own = 1.0, jax.random.fold_in(rng, 6)
    for dim, blocks in cuts:
        heights = jnp.exp(jax.random.uniform(jax.random.fold_in(own, dim), (blocks,), jnp.float32, smallest / len(cuts), high / len(cuts)))
        factor_of = factor_of * jnp.repeat(heights, shape[dim] // blocks).reshape([-1 if axis == dim else 1 for axis in range(len(shape))])
    return factor_of


def shared_out(own_key, own, number, rows, count, top, reach, lean):
    sequence = jax.random.permutation(own_key, count)
    packed, common = portions_of(count, rows * top, reach, lean, True), portions_of(count, rows * top, reach, lean, False)
    places = jnp.arange(count)

    def named(tallies, turn):
        used = int((tallies > 0).sum())
        fixed = max(1, used // 4)
        passed = fixed + (places - fixed + turn * (used - fixed)) % max(1, count - fixed)
        return jnp.zeros((count,), jnp.int32).at[sequence[jnp.where(places < fixed, places, passed)]].set(jnp.asarray(tallies, jnp.int32))

    tallies = jnp.where(number % 4 == 0, named(packed, number // 4), named(common, number - number // 4 - 1))
    mixed = jax.random.permutation(jax.random.fold_in(own, 3), count)
    source_of, sink = mixed[0:count // 2 * 2:2], mixed[1:count // 2 * 2:2]
    slack = jnp.minimum(tallies[source_of] - 1, reach - tallies[sink]) // 2
    slack = jnp.where((source_of == sequence[0]) | (sink == sequence[0]) | (tallies[sink] == 0), 0, jnp.maximum(slack, 0))
    passed = jax.random.randint(jax.random.fold_in(own, 4), (count // 2,), 0, 1 << 20) % (slack + 1)
    tallies = tallies.at[source_of].add(-passed).at[sink].add(passed)
    items = jnp.searchsorted(jnp.cumsum(tallies), jnp.arange(rows * top), side="right").astype(jnp.int32)
    grid = items.reshape(top, rows).T
    grid = grid[jax.random.permutation(jax.random.fold_in(own, 1), rows)]
    turn = jax.random.randint(jax.random.fold_in(own, 2), (rows, 1), 0, top)
    return jnp.take_along_axis(grid, (jnp.arange(top)[None, :] + turn) % top, axis=1)


def portions_of(count, total, most, slope, full):
    portions = [(1 << 20) // math.isqrt(standing ** slope) + 1 for standing in range(1, count + 1)]
    largest = most if full else min(most, max(-(-total // count), total * portions[0] // sum(portions)))
    least = 1 if total - largest >= count - 1 else 0
    given, rest = [largest] + [least] * (count - 1), total - largest - least * (count - 1)
    while rest > 0:
        movable = [i for i in range(1, count) if given[i] < largest] or [i for i in range(1, count) if given[i] < most]
        whole, budget = sum([portions[i] for i in movable]), rest
        for i in movable:
            extra = min(most - given[i], max(1, budget * portions[i] // whole), rest)
            given[i] = given[i] + extra
            rest = rest - extra
    return np.array(given)


def noise(stream_key, shape, deviation, most, cuts=(), held_as=jnp.bfloat16):
    level = levels(stream_key, shape, cuts, -0.22, 0.18) if cuts else 1.0
    entries = jax.random.normal(stream_key, shape, jnp.float32) * deviation * level
    return jnp.minimum(jnp.maximum(entries, -most), most).astype(held_as)


def setup_inputs(seed: int = 0) -> dict:
    key_list = jax.random.split(jax.random.key(seed), 9)
    imp_x = noise(key_list[0], (IMPS, D), 1.0, 6.0, ((0, 64),))
    imp_hist_keys = jax.random.split(jax.random.fold_in(key_list[1], 1), IMPS // IMP_DEV)
    imp_hist_turns = jax.random.permutation(jax.random.fold_in(key_list[1], 3), IMPS // IMP_DEV)
    imp_hist = jax.vmap(lambda own, number: shared_out(jax.random.fold_in(key_list[1], 2), own, number, IMP_DEV, HISTS, 1, CAP, 2))(imp_hist_keys, imp_hist_turns).reshape((IMPS, 1))
    imp_len = draw_imp_len(jax.random.fold_in(key_list[8], 71), 0)
    owner_map = jax.random.permutation(key_list[3], HISTS).astype(jnp.int32)
    hist_x = noise(key_list[4], (HISTS, L, D), 1.0, 6.0, ((0, 64),))
    w_in = noise(key_list[5], (4, D, HD), D ** -0.5, 0.25, ((2, 4),))
    w_out = noise(key_list[6], (HD, D), HD ** -0.5, 0.25, ((0, 4),))
    grad_y = noise(key_list[7], (IMPS, D), 1.0, 6.0, ((0, 64),))
    return dict(imp_x=imp_x, imp_hist=imp_hist, imp_len=imp_len, owner_map=owner_map, hist_x=hist_x, w_in=w_in, w_out=w_out, grad_y=grad_y)


EPSILON = 1e-05

def silu_slope(pre_act):
    sigmoid_v = jax.nn.sigmoid(pre_act)
    return sigmoid_v * (1.0 + pre_act * (1.0 - sigmoid_v))

def owner_pass(query_rows, gate_rows, cotangent, length_rows, events, w_key, w_value):
    row_count = query_rows.shape[0]
    col_width = query_rows.shape[1]
    head_count = col_width // DH
    event_count = events.shape[0]
    block_len = min(1024, event_count)
    block_count = event_count // block_len
    factor = DH ** (-0.5)
    key_pre = jnp.dot(events, w_key, preferred_element_type=jnp.float32)
    key_rows = jax.nn.silu(key_pre).astype(jnp.bfloat16)
    value_rows = jnp.dot(events, w_value, preferred_element_type=jnp.float32).astype(jnp.bfloat16)
    key_blocks = key_rows.reshape(block_count, block_len, head_count, DH)
    value_blocks = value_rows.reshape(block_count, block_len, head_count, DH)
    query_heads = query_rows.reshape(row_count, head_count, DH).astype(jnp.float32)
    positions = jnp.arange(block_count, dtype=jnp.int32)

    def scores_of(position, key_block):
        scores = jnp.einsum('rhd,khd->hrk', query_heads, key_block.astype(jnp.float32)) * factor
        event_ids = position * block_len + jnp.arange(block_len, dtype=jnp.int32)
        visible = event_ids[None, :] < length_rows[:, None]
        return (scores, visible[None])

    def forward(running, pieces):
        position, key_block, value_block = pieces
        scores, visible = scores_of(position, key_block)
        weights = jnp.where(visible, jax.nn.silu(scores), 0.0).astype(jnp.bfloat16)
        running = running + jnp.einsum('hrk,khd->rhd', weights.astype(jnp.float32), value_block.astype(jnp.float32))
        return (running, None)
    attended, unused = lax.scan(forward, jnp.zeros((row_count, head_count, DH), jnp.float32), (positions, key_blocks, value_blocks))
    inverse = lax.rsqrt(lax.optimization_barrier(jnp.mean(attended * attended, axis=-1, keepdims=True)) + EPSILON)
    normed = attended * inverse
    gate_heads = gate_rows.reshape(row_count, head_count, DH).astype(jnp.float32)
    cot_heads = cotangent.reshape(row_count, head_count, DH).astype(jnp.float32)
    gated = (normed * gate_heads).astype(jnp.bfloat16)
    d_normed = cot_heads * gate_heads
    d_gate = (cot_heads * normed).astype(jnp.bfloat16)
    d_att = (inverse * (d_normed - normed * lax.optimization_barrier(jnp.mean(d_normed * normed, axis=-1, keepdims=True)))).astype(jnp.bfloat16)
    d_att_wide = d_att.astype(jnp.float32)

    def backward(partial_value, pieces):
        position, key_block, value_block = pieces
        scores, visible = scores_of(position, key_block)
        weights = jnp.where(visible, jax.nn.silu(scores), 0.0).astype(jnp.bfloat16)
        d_weights = jnp.einsum('rhd,khd->hrk', d_att_wide, value_block.astype(jnp.float32))
        d_scores = jnp.where(visible, d_weights * silu_slope(scores) * factor, 0.0).astype(jnp.bfloat16)
        d_scores_wide = d_scores.astype(jnp.float32)
        partial_value = partial_value + jnp.einsum('hrk,khd->rhd', d_scores_wide, key_block.astype(jnp.float32))
        d_key = jnp.einsum('hrk,rhd->khd', d_scores_wide, query_heads)
        d_value = jnp.einsum('hrk,rhd->khd', weights.astype(jnp.float32), d_att_wide)
        return (partial_value, (d_key, d_value))
    d_query, (d_keys, d_values) = lax.scan(backward, jnp.zeros((row_count, head_count, DH), jnp.float32), (positions, key_blocks, value_blocks))
    d_keys = d_keys.reshape(event_count, col_width)
    d_values = d_values.reshape(event_count, col_width)
    grad_key = d_keys.astype(jnp.bfloat16)
    grad_value = d_values.astype(jnp.bfloat16)
    key_term = (d_keys * silu_slope(key_pre)).astype(jnp.bfloat16)
    grad_wk = jnp.dot(events.T, key_term, preferred_element_type=jnp.float32)
    grad_wv = jnp.dot(events.T, grad_value, preferred_element_type=jnp.float32)
    return (d_query.reshape(row_count, col_width).astype(jnp.bfloat16), d_gate.reshape(row_count, col_width), gated.reshape(row_count, col_width), grad_key, grad_value, grad_wk, grad_wv)

def reference(imp_x, imp_hist, imp_len, owner_map, hist_x, w_in, w_out, grad_y):
    histories = imp_hist[:, 0]
    target_dev = owner_map[histories]
    by_shard = target_dev.reshape(N_DP, IMP_DEV)
    one_hot = (by_shard[:, :, None] == jnp.arange(N_DP, dtype=jnp.int32)[None, None, :]).astype(jnp.int32)
    prior_hits = jnp.cumsum(one_hot, axis=1) - one_hot
    slot_index = lax.optimization_barrier(jnp.sum(prior_hits * one_hot, axis=2)).reshape(IMPS)
    source_dev = (jnp.arange(IMPS, dtype=jnp.int32) // IMP_DEV).astype(jnp.int32)
    slot_table = jnp.full((N_DP, N_DP, CAP), IMPS, jnp.int32)
    slot_table = slot_table.at[target_dev, source_dev, slot_index].set(jnp.arange(IMPS, dtype=jnp.int32))
    slot_table = slot_table.reshape(N_DP, N_DP * CAP)
    query_pre = jnp.dot(imp_x, w_in[0], preferred_element_type=jnp.float32)
    gate_pre = jnp.dot(imp_x, w_in[1], preferred_element_type=jnp.float32)
    queries = jax.nn.silu(query_pre).astype(jnp.bfloat16)
    gate_rows = jax.nn.silu(gate_pre).astype(jnp.bfloat16)
    cotangent = jnp.dot(grad_y, w_out.T, preferred_element_type=jnp.float32).astype(jnp.bfloat16)

    def per_owner(pieces):
        owner_slot, slot_rows = pieces
        occupied = slot_rows < IMPS
        safe_index = jnp.minimum(slot_rows, IMPS - 1)
        q_rows = jnp.where(occupied[:, None], queries[safe_index], jnp.zeros((), queries.dtype))
        u_rows = jnp.where(occupied[:, None], gate_rows[safe_index], jnp.zeros((), gate_rows.dtype))
        c_rows = jnp.where(occupied[:, None], cotangent[safe_index], jnp.zeros((), cotangent.dtype))
        l_rows = jnp.where(occupied, imp_len[safe_index], 0).astype(jnp.int32)
        return owner_pass(q_rows, u_rows, c_rows, l_rows, hist_x[owner_slot], w_in[2], w_in[3])
    results = lax.map(per_owner, (jnp.arange(N_DP, dtype=jnp.int32), slot_table))
    d_query_rows, d_gate_rows, gated_rows, grad_key, grad_value, grad_wk, grad_wv = results
    flat_slots = slot_table.reshape(-1)

    def to_impressions(stacked):
        flat_rows = stacked.reshape(N_DP * N_DP * CAP, HD)
        return jnp.zeros((IMPS, HD), stacked.dtype).at[flat_slots].set(flat_rows, mode='drop')
    d_query = to_impressions(d_query_rows)
    d_gate = to_impressions(d_gate_rows)
    gated = to_impressions(gated_rows)
    query_term = (d_query.astype(jnp.float32) * silu_slope(query_pre)).astype(jnp.bfloat16)
    gate_term = (d_gate.astype(jnp.float32) * silu_slope(gate_pre)).astype(jnp.bfloat16)
    grad_x = (jnp.dot(query_term, w_in[0].T, preferred_element_type=jnp.float32) + jnp.dot(gate_term, w_in[1].T, preferred_element_type=jnp.float32)).astype(jnp.bfloat16)
    factor = IMPS ** (-0.5)
    grad_wq = jnp.dot(imp_x.T, query_term, preferred_element_type=jnp.float32)
    grad_wu = jnp.dot(imp_x.T, gate_term, preferred_element_type=jnp.float32)
    grad_w_in = jnp.stack([grad_wq, grad_wu, lax.optimization_barrier(jnp.sum(grad_wk, axis=0)), lax.optimization_barrier(jnp.sum(grad_wv, axis=0))]) * factor
    grad_w_out = jnp.dot(gated.T, grad_y, preferred_element_type=jnp.float32) * factor
    grad_kv = jnp.stack([grad_key, grad_value], axis=2)
    return (grad_x, grad_kv, grad_w_in, grad_w_out)
```

```python
import jax
import jax.numpy as jnp
from jax import lax
from jax.experimental import pallas as pl
from jax.experimental.pallas import tpu as pltpu
from jax.sharding import PartitionSpec as P

DH = 64
EPSILON = 1e-05
CAP = 8
BLOCK = 256
F32 = jnp.float32
BF16 = jnp.bfloat16
VMEM = pl.BlockSpec(memory_space=pltpu.VMEM)
SMEM = pl.BlockSpec(memory_space=pltpu.SMEM)
PARAMS = pltpu.CompilerParams(vmem_limit_bytes=48 * 1024 * 1024)


def nn(a, b):
    return lax.dot_general(a, b, (((1,), (0,)), ((), ())), preferred_element_type=F32)


def nt(a, b):
    return lax.dot_general(a, b, (((1,), (1,)), ((), ())), preferred_element_type=F32)


def tn(a, b):
    return lax.dot_general(a, b, (((0,), (0,)), ((), ())), preferred_element_type=F32)


def sigmoid(v):
    return 0.5 * jnp.tanh(0.5 * v) + 0.5


def silu_and_slope(v):
    s = sigmoid(v)
    return v * s, s * (1.0 + v * (1.0 - s))


def iota(shape, dim):
    return lax.broadcasted_iota(jnp.int32, shape, dim)


def spread(parts):
    count = parts[0].shape[0] // 8
    cut = [p.reshape(count, 8, p.shape[1]) for p in parts]
    joined = jnp.concatenate(cut, axis=1)
    return joined.reshape(count * 8 * len(parts), parts[0].shape[1])


def pre_kernel(x_ref, hist_ref, len_ref, owner_ref, w_ref, wo_ref, gy_ref, send_ref, aux_ref, place_ref):
    rows = x_ref.shape[0]
    owners = owner_ref.shape[1]
    x = x_ref[...]
    queries, slope_q = silu_and_slope(nn(x, w_ref[0]))
    gates, slope_g = silu_and_slope(nn(x, w_ref[1]))
    cot = nt(gy_ref[...], wo_ref[...]).astype(BF16).astype(F32)
    gates = gates.astype(BF16).astype(F32)
    aux_ref[0] = slope_q
    aux_ref[1] = slope_g
    aux_ref[2] = gates
    aux_ref[3] = cot
    named = hist_ref[...] == iota((rows, owners), 1)
    target = jnp.sum(jnp.where(named, owner_ref[...].astype(F32), 0.0), axis=1, keepdims=True)
    target = jnp.transpose(jnp.broadcast_to(target, (rows, rows)))
    hit = target[:owners] == iota((owners, rows), 0).astype(F32)
    hit = jnp.where(hit, 1.0, 0.0)
    earlier = jnp.where(iota((rows, rows), 0) < iota((rows, rows), 1), 1.0, 0.0)
    before = nn(hit.astype(BF16), earlier.astype(BF16))
    rank = jnp.sum(before * hit, axis=0, keepdims=True)
    slot = target[:1] * float(CAP) + rank
    slots = owners * CAP
    place = jnp.where(iota((slots, rows), 0).astype(F32) == slot, 1.0, 0.0).astype(BF16)
    place_ref[...] = place
    length = len_ref[...].astype(F32)
    high = jnp.floor(length * (1.0 / 256.0))
    low = length - 256.0 * high
    digits = jnp.where(iota((rows, rows), 0) == 0, high, low)
    digits = jnp.transpose(digits)
    payload = jnp.concatenate(
        [queries.astype(BF16), (cot * gates).astype(BF16), digits.astype(BF16)], axis=1
    )
    packed = nn(place, payload)
    width = queries.shape[1]
    send_ref[...] = spread(
        [packed[:, :width], packed[:, width : 2 * width], packed[:, 2 * width :]]
    ).astype(BF16)


def project_kernel(ev_ref, w_ref, k_ref, v_ref, kt_ref, vt_ref, slope_ref):
    def step(b, carry):
        at = pl.ds(pl.multiple_of(b * 512, 512), 512)
        ev = ev_ref[at, :]
        keys, slope = silu_and_slope(nn(ev, w_ref[2]))
        values = nn(ev, w_ref[3])
        k_ref[at, :] = keys.astype(BF16)
        v_ref[at, :] = values.astype(BF16)
        slope_ref[at, :] = slope
        kt_ref[:, at] = jnp.transpose(keys.astype(BF16))
        vt_ref[:, at] = jnp.transpose(values.astype(BF16))
        return carry

    lax.fori_loop(0, ev_ref.shape[0] // 512, step, 0)


def attend_kernel(
    recv_ref, k_ref, v_ref, kt_ref, vt_ref, slope_ref,
    back_ref, gkv_ref, term_ref,
    w_scr, s_scr, att_scr, dq_scr,
):
    slots = recv_ref.shape[0] // 3
    events, width = k_ref.shape
    heads = width // DH
    got = recv_ref[...].astype(F32).reshape(slots // CAP, 3 * CAP, width)
    q = got[:, :CAP].reshape(slots, width)
    dn = got[:, CAP : 2 * CAP].reshape(slots, width)
    digits = got[:, 2 * CAP :].reshape(slots, width)
    digits = jnp.transpose(digits)
    length = digits[0:1] * 256.0 + digits[1:2]
    qt = jnp.transpose(q)
    head_row = iota((width, slots), 0) // DH
    head_col = iota((slots, width), 1) // DH
    qt_half = (qt * (0.5 * DH ** (-0.5))).astype(BF16)
    zero = jnp.zeros((), BF16)
    qt_of = [jnp.where(head_row == h, qt_half, zero) for h in range(heads)]
    att_scr[...] = jnp.zeros_like(att_scr)

    def forward(b, carry):
        start = pl.multiple_of(b * BLOCK, BLOCK)
        at = pl.ds(start, BLOCK)
        visible = (iota((BLOCK, slots), 0) + start).astype(F32) < length
        for h in range(heads):
            half = nn(k_ref[at, :], qt_of[h])
            twice = jnp.where(visible, jnp.tanh(half) + 1.0, 0.0)
            weights = half * twice
            s_scr[h, at, :] = (twice + weights * (2.0 - twice)).astype(BF16)
            weights = weights.astype(BF16)
            w_scr[h, at, :] = weights
            mine = pl.ds(h * DH, DH)
            att_scr[mine, :] += nn(vt_ref[mine, at], weights)
        return carry

    lax.fori_loop(0, events // BLOCK, forward, 0)
    att = att_scr[...].reshape(heads, DH, slots)
    inverse = lax.rsqrt(jnp.mean(att * att, axis=1, keepdims=True) + EPSILON)
    normed = att * inverse
    dnt = jnp.transpose(dn).reshape(heads, DH, slots)
    d_att = inverse * (dnt - normed * jnp.mean(dnt * normed, axis=1, keepdims=True))
    d_att = d_att.reshape(width, slots)
    d_att_t = d_att.astype(BF16)
    d_att = jnp.transpose(d_att).astype(BF16)
    normed = jnp.transpose(normed.reshape(width, slots))
    q_bf = q.astype(BF16)
    dt_of = [jnp.where(head_row == h, d_att_t, zero) for h in range(heads)]
    d_of = [jnp.where(head_col == h, d_att, zero) for h in range(heads)]
    q_of = [jnp.where(head_col == h, q_bf, zero) for h in range(heads)]
    dq_scr[...] = jnp.zeros_like(dq_scr)

    def backward(b, carry):
        at = pl.ds(pl.multiple_of(b * BLOCK, BLOCK), BLOCK)
        d_keys = jnp.zeros((BLOCK, width), F32)
        d_values = jnp.zeros((BLOCK, width), F32)
        for h in range(heads):
            ds = (nn(v_ref[at, :], dt_of[h]) * s_scr[h, at, :].astype(F32)).astype(BF16)
            mine = pl.ds(h * DH, DH)
            dq_scr[mine, :] += nn(kt_ref[mine, at], ds)
            d_keys += nn(ds, q_of[h])
            d_values += nn(w_scr[h, at, :], d_of[h])
        d_keys = d_keys * (0.5 * DH ** (-0.5))
        gkv_ref[at, :width] = d_keys.astype(BF16)
        gkv_ref[at, width:] = d_values.astype(BF16)
        term_ref[at, :] = (d_keys * slope_ref[at, :]).astype(BF16)
        return carry

    lax.fori_loop(0, events // BLOCK, backward, 0)
    d_query = jnp.transpose(dq_scr[...] * (0.5 * DH ** (-0.5)))
    back_ref[...] = spread([d_query, normed]).astype(BF16)


def history_grads_kernel(core_ref, ev_ref, term_ref, gkv_ref, mine_ref, other_ref, scr):
    width = term_ref.shape[1]
    gk = tn(ev_ref[...], term_ref[...])
    gv = tn(ev_ref[...], gkv_ref[:, width:])
    rows = spread([gk, gv]).astype(BF16)
    half = rows.shape[0] // 2
    scr[0] = rows[:half]
    scr[1] = rows[half:]
    core = core_ref[0]
    mine_ref[...] = scr[core]
    other_ref[...] = scr[1 - core]


def post_kernel(core_ref, back_ref, place_ref, aux_ref, x_ref, w_ref, gy_ref, mine_ref, other_ref, gx_ref, scr):
    slots, rows = place_ref.shape
    width = back_ref.shape[1]
    got = back_ref[...].astype(F32).reshape(slots // CAP, 2 * CAP, width)
    d_query = got[:, :CAP].reshape(slots, width).astype(BF16)
    normed = got[:, CAP:].reshape(slots, width).astype(BF16)
    both = tn(place_ref[...], jnp.concatenate([d_query, normed], axis=1))
    d_query = both[:, :width]
    normed = both[:, width:]
    gates = aux_ref[2]
    gated = (normed * gates).astype(BF16)
    d_gate = (aux_ref[3] * normed).astype(BF16).astype(F32)
    q_term = (d_query * aux_ref[0]).astype(BF16)
    g_term = (d_gate * aux_ref[1]).astype(BF16)
    gx_ref[...] = (nt(q_term, w_ref[0]) + nt(g_term, w_ref[1])).astype(BF16)
    x = x_ref[...]
    gq = tn(x, q_term)
    gg = tn(x, g_term)
    go = tn(gated, gy_ref[...])
    go = jnp.concatenate([go[:, i * width : (i + 1) * width] for i in range(go.shape[1] // width)], axis=0)
    out = spread([gq, gg, go]).astype(BF16)
    half = out.shape[0] // 2
    scr[0] = out[:half]
    scr[1] = out[half:]
    core = core_ref[0]
    mine_ref[...] = scr[core]
    other_ref[...] = scr[1 - core]


def pair_kernel(a_ref, b_ref, c_ref, d_ref, out_ref):
    width = a_ref.shape[1]
    first = a_ref[...].astype(F32) + b_ref[...].astype(F32)
    second = c_ref[...].astype(F32) + d_ref[...].astype(F32)
    chunks = first.shape[0] // 16
    joined = jnp.concatenate(
        [first.reshape(chunks, 16, width), second.reshape(chunks, 24, width)], axis=1
    )
    out_ref[...] = joined.reshape(chunks * 40, width).astype(BF16)


def sum_kernel(factor, in_ref, out_ref):
    chunks = in_ref.shape[0] // 40
    total = jnp.sum(in_ref[...].astype(F32).reshape(chunks, 40, in_ref.shape[1]), axis=0)
    total = total * factor
    out_ref[...] = jnp.broadcast_to(total[None], (chunks, 40, total.shape[1])).reshape(out_ref.shape).astype(BF16)


def unfold_kernel(core_ref, mine_ref, other_ref, win_ref, wout_ref, scr):
    width = mine_ref.shape[1]
    core = core_ref[0]
    for ref, which in ((mine_ref, core), (other_ref, 1 - core)):
        got = ref[...].astype(F32)
        chunks = got.shape[0] // 40
        got = got.reshape(chunks, 5, 8, width)
        size = chunks * 8
        at = pl.ds(pl.multiple_of(which * size, size), size)
        for place, index in enumerate((2, 3, 0, 1)):
            win_ref[index, at, :] = got[:, place].reshape(size, width)
        scr[at, :] = got[:, 4].reshape(size, width)
    rows = wout_ref.shape[0]
    for i in range(wout_ref.shape[1] // width):
        wout_ref[:, i * width : (i + 1) * width] = scr[i * rows : (i + 1) * rows, :]


def call(kernel, outs, ins, specs=None, scratch=(), flops=0, moved=0):
    return pl.pallas_call(
        kernel,
        out_shape=[jax.ShapeDtypeStruct(s, d) for s, d in outs],
        in_specs=specs or [VMEM] * len(ins),
        out_specs=[VMEM] * len(outs),
        scratch_shapes=list(scratch),
        compiler_params=PARAMS,
        cost_estimate=pl.CostEstimate(flops=flops, bytes_accessed=moved, transcendentals=0),
    )(*ins)


def on_device(imp_x, imp_hist, imp_len, owner_map, hist_x, w_in, w_out, grad_y):
    owners = lax.axis_size("dp")
    planes = lax.axis_size("mp")
    rows, depth = imp_x.shape
    width = w_in.shape[2]
    slots = owners * CAP
    events = hist_x.shape[1]
    chips = owners // 2
    place_of = lax.axis_index("dp")
    core = (place_of % 2).reshape(1)
    hist = hist_x[0]
    pairs = [(i, i ^ 1) for i in range(owners)]
    same_core = [[2 * i + c for i in range(chips)] for c in range(2)]

    def swap(a):
        return lax.ppermute(a, "dp", pairs)

    def exchange(a):
        a = a.reshape(owners, a.shape[0] // owners, width)
        a = lax.all_to_all(a, "dp", 0, 0, tiled=True)
        return a.reshape(a.shape[0] * a.shape[1], width)

    def exchange_core(a):
        a = a.reshape(chips, a.shape[0] // chips, width)
        a = lax.all_to_all(a, "dp", 0, 0, axis_index_groups=same_core, tiled=True)
        return a.reshape(a.shape[0] * a.shape[1], width)

    send, aux, place = call(
        pre_kernel,
        [((3 * slots, width), BF16), ((4, rows, width), F32), ((slots, rows), BF16)],
        (imp_x, imp_hist, imp_len.reshape(1, rows), owner_map.reshape(1, owners), w_in, w_out, grad_y),
        flops=2 * rows * depth * width * 3,
        moved=1 << 20,
    )
    recv = exchange(send)
    keys, values, keys_t, values_t, key_slope = call(
        project_kernel,
        [((events, width), BF16)] * 2 + [((width, events), BF16)] * 2 + [((events, width), F32)],
        (hist, w_in),
        flops=4 * events * depth * width,
        moved=5 << 20,
    )
    back, gkv, term = call(
        attend_kernel,
        [((2 * slots, width), BF16), ((events, 2 * width), BF16), ((events, width), BF16)],
        (recv, keys, values, keys_t, values_t, key_slope),
        scratch=[
            pltpu.VMEM((width // DH, events, slots), BF16),
            pltpu.VMEM((width // DH, events, slots), BF16),
            pltpu.VMEM((width, slots), F32),
            pltpu.VMEM((width, slots), F32),
        ],
        flops=12 * events * slots * width,
        moved=4 << 20,
    )
    back = exchange(back)
    half = depth * width * 2 // 2 // width
    kv_mine, kv_other = call(
        history_grads_kernel,
        [((half, width), BF16)] * 2,
        (core, hist, term, gkv),
        specs=[SMEM, VMEM, VMEM, VMEM],
        scratch=[pltpu.VMEM((2, half, width), BF16)],
        flops=4 * events * depth * width,
        moved=4 << 20,
    )
    kv_other = swap(kv_other)
    half = depth * 3 // 2
    mine, other, gx = call(
        post_kernel,
        [((half, width), BF16)] * 2 + [((rows, depth), BF16)],
        (core, back, place, aux, imp_x, w_in, grad_y),
        specs=[SMEM] + [VMEM] * 6,
        scratch=[pltpu.VMEM((2, half, width), BF16)],
        flops=2 * rows * depth * width * 5,
        moved=2 << 20,
    )
    other = swap(other)
    (summed,) = call(
        pair_kernel, [((chips * 40, width), BF16)], (kv_mine, kv_other, mine, other), moved=1 << 20
    )
    plane = lax.axis_index("mp")
    share = rows // planes
    own = lax.dynamic_slice_in_dim(gx, plane * share, share, 0)
    total = own.astype(F32)
    for step in range(1, planes):
        target = (plane + step) % planes
        part = lax.dynamic_slice_in_dim(gx, target * share, share, 0)
        part = lax.ppermute(part, "mp", [(i, (i + step) % planes) for i in range(planes)])
        total = total + part.astype(F32)
    grad_x = total.astype(BF16)
    factor = (rows * owners) ** (-0.5)
    (piece,) = call(
        lambda i, o: sum_kernel(factor, i, o),
        [((chips * 40, width), BF16)],
        (exchange_core(summed),),
        moved=1 << 20,
    )
    mine = exchange_core(piece)
    other = swap(mine)
    grad_w_in, grad_w_out = call(
        unfold_kernel,
        [((4, depth, width), F32), ((width, depth), F32)],
        (core, mine, other),
        specs=[SMEM, VMEM, VMEM],
        scratch=[pltpu.VMEM((depth, width), F32)],
        moved=3 << 20,
    )
    grad_kv = gkv.reshape(1, events, 2, width)
    return (grad_x, grad_kv, grad_w_in, grad_w_out)


def solution(mesh):
    placed = (
        P("dp", None),
        P("dp", None),
        P("dp"),
        P(),
        P("dp", None, None),
        P(None, None, "mp"),
        P("mp", None),
        P("dp", None),
    )
    return jax.shard_map(
        on_device,
        mesh=mesh,
        in_specs=placed,
        out_specs=(
            P(("dp", "mp"), None),
            P("dp", None, None, "mp"),
            P(None, None, "mp"),
            P("mp", None),
        ),
        check_vma=False,
    )
```

```python
import jax
import jax.numpy as jnp
from jax import lax
from jax.experimental import pallas as pl
from jax.experimental.pallas import tpu as pltpu
from jax.sharding import PartitionSpec as P

DH = 64
EPSILON = 1e-05
CAP = 8
BLOCK = 1024
F32 = jnp.float32
BF16 = jnp.bfloat16
ANY = pl.BlockSpec(memory_space=pl.ANY)
SMEM = pl.BlockSpec(memory_space=pltpu.SMEM)
PARAMS = pltpu.CompilerParams(vmem_limit_bytes=62 * 1024 * 1024)


def nn(a, b):
    return lax.dot_general(a, b, (((1,), (0,)), ((), ())), preferred_element_type=F32)


def nt(a, b):
    return lax.dot_general(a, b, (((1,), (1,)), ((), ())), preferred_element_type=F32)


def tn(a, b):
    return lax.dot_general(a, b, (((0,), (0,)), ((), ())), preferred_element_type=F32)


def sigmoid(v):
    return 0.5 * jnp.tanh(0.5 * v) + 0.5


def silu_and_slope(v):
    s = sigmoid(v)
    return v * s, s * (1.0 + v * (1.0 - s))


def iota(shape, dim):
    return lax.broadcasted_iota(jnp.int32, shape, dim)


def spread(parts):
    count = parts[0].shape[0] // 8
    cut = [p.reshape(count, 8, p.shape[1]) for p in parts]
    joined = jnp.concatenate(cut, axis=1)
    return joined.reshape(count * 8 * len(parts), parts[0].shape[1])


def pre_kernel(x_in, hist_in, len_in, owner_in, w_in, wo_in, gy_in, send_out, aux_out, place_out):
    hist = hist_in.get()[...]
    owner = owner_in.get()[...]
    rows, owners = hist.shape[1], owner.shape[1]
    named = jnp.where(iota((owners, rows), 0) == hist, 1.0, 0.0).astype(BF16)
    owner = jnp.broadcast_to(owner.astype(F32), (8, owners)).astype(BF16)
    target = nn(owner, named)[:1]
    hit = jnp.where(iota((owners, rows), 0).astype(F32) == target, 1.0, 0.0)
    earlier = jnp.where(iota((rows, rows), 0) < iota((rows, rows), 1), 1.0, 0.0)
    before = nn(hit.astype(BF16), earlier.astype(BF16))
    rank = jnp.sum(before * hit, axis=0, keepdims=True)
    slot = target * float(CAP) + rank
    slots = owners * CAP
    place = jnp.where(iota((slots, rows), 0).astype(F32) == slot, 1.0, 0.0).astype(BF16)
    place_out.buffer[...] = place
    place_out.send()
    length = len_in.get()[...].astype(F32)
    high = jnp.floor(length * (1.0 / 256.0))
    low = length - 256.0 * high
    digits = jnp.transpose(jnp.where(iota((rows, rows), 0) == 0, high, low))
    x, w_ref = x_in.get()[...], w_in.get()
    queries, slope_q = silu_and_slope(nn(x, w_ref[0]))
    gates, slope_g = silu_and_slope(nn(x, w_ref[1]))
    cot = nt(gy_in.get()[...], wo_in.get()[...]).astype(BF16).astype(F32)
    gates = gates.astype(BF16).astype(F32)
    payload = jnp.concatenate(
        [queries.astype(BF16), (cot * gates).astype(BF16), digits.astype(BF16)], axis=1
    )
    packed = nn(place, payload)
    width = queries.shape[1]
    send_out.buffer[...] = spread(
        [packed[:, :width], packed[:, width : 2 * width], packed[:, 2 * width :]]
    ).astype(BF16)
    send_out.send()
    aux_out.buffer[0] = slope_q
    aux_out.buffer[1] = slope_g
    aux_out.buffer[2] = gates
    aux_out.buffer[3] = cot


def project_kernel(ev_in, w_in, k_out, v_out, kt_out, vt_out, slope_out):
    ev_ref, w_ref = ev_in.get(), w_in.get()

    def step(b, carry):
        at = pl.ds(pl.multiple_of(b * 512, 512), 512)
        ev = ev_ref[at, :]
        keys, slope = silu_and_slope(nn(ev, w_ref[2]))
        values = nn(ev, w_ref[3])
        k_out.buffer[at, :] = keys.astype(BF16)
        v_out.buffer[at, :] = values.astype(BF16)
        slope_out.buffer[at, :] = slope
        kt_out.buffer[:, at] = jnp.transpose(keys.astype(BF16))
        vt_out.buffer[:, at] = jnp.transpose(values.astype(BF16))
        return carry

    lax.fori_loop(0, ev_ref.shape[0] // 512, step, 0)


def attend_kernel(
    recv_in, k_in, vt_in, v_in, kt_in, slope_in,
    back_out, gkv_out, term_out,
    w_scr, s_scr, att_scr, dq_scr,
):
    gkv_ref, term_ref = gkv_out.buffer, term_out.buffer
    recv_ref = recv_in.get()
    slots, width = recv_ref.shape[0] // 3, recv_ref.shape[1]
    heads = width // DH
    got = recv_ref[...].astype(F32).reshape(slots // CAP, 3 * CAP, width)
    q = got[:, :CAP].reshape(slots, width)
    dn = got[:, CAP : 2 * CAP].reshape(slots, width)
    digits = got[:, 2 * CAP :].reshape(slots, width)
    digits = jnp.transpose(digits)
    length = digits[0:1] * 256.0 + digits[1:2]
    qt = jnp.transpose(q)
    head_row = iota((width, slots), 0) // DH
    head_col = iota((slots, width), 1) // DH
    qt_half = (qt * (0.5 * DH ** (-0.5))).astype(BF16)
    zero = jnp.zeros((), BF16)
    qt_of = [jnp.where(head_row == h, qt_half, zero) for h in range(heads)]
    att_scr[...] = jnp.zeros_like(att_scr)
    k_ref, vt_ref = k_in.get(), vt_in.get()
    events = k_ref.shape[0]

    def forward(b, carry):
        start = pl.multiple_of(b * BLOCK, BLOCK)
        at = pl.ds(start, BLOCK)
        visible = (iota((BLOCK, slots), 0) + start).astype(F32) < length
        for h in range(heads):
            half = nn(k_ref[at, :], qt_of[h])
            twice = jnp.where(visible, jnp.tanh(half) + 1.0, 0.0)
            weights = half * twice
            s_scr[h, at, :] = (twice + weights * (2.0 - twice)).astype(BF16)
            weights = weights.astype(BF16)
            w_scr[h, at, :] = weights
            mine = pl.ds(h * DH, DH)
            att_scr[mine, :] += nn(vt_ref[mine, at], weights)
        return carry

    lax.fori_loop(0, events // BLOCK, forward, 0)
    att = att_scr[...].reshape(heads, DH, slots)
    inverse = lax.rsqrt(jnp.mean(att * att, axis=1, keepdims=True) + EPSILON)
    normed = att * inverse
    dnt = jnp.transpose(dn).reshape(heads, DH, slots)
    d_att = inverse * (dnt - normed * jnp.mean(dnt * normed, axis=1, keepdims=True))
    d_att = d_att.reshape(width, slots)
    d_att_t = d_att.astype(BF16)
    d_att = jnp.transpose(d_att).astype(BF16)
    normed = jnp.transpose(normed.reshape(width, slots))
    q_bf = q.astype(BF16)
    dt_of = [jnp.where(head_row == h, d_att_t, zero) for h in range(heads)]
    d_of = [jnp.where(head_col == h, d_att, zero) for h in range(heads)]
    q_of = [jnp.where(head_col == h, q_bf, zero) for h in range(heads)]
    dq_scr[...] = jnp.zeros_like(dq_scr)
    v_ref, kt_ref, slope_ref = v_in.get(), kt_in.get(), slope_in.get()

    def backward(b, carry):
        at = pl.ds(pl.multiple_of(b * BLOCK, BLOCK), BLOCK)
        d_keys = jnp.zeros((BLOCK, width), F32)
        d_values = jnp.zeros((BLOCK, width), F32)
        for h in range(heads):
            ds = (nn(v_ref[at, :], dt_of[h]) * s_scr[h, at, :].astype(F32)).astype(BF16)
            mine = pl.ds(h * DH, DH)
            dq_scr[mine, :] += nn(kt_ref[mine, at], ds)
            d_keys += nn(ds, q_of[h])
            d_values += nn(w_scr[h, at, :], d_of[h])
        d_keys = d_keys * (0.5 * DH ** (-0.5))
        gkv_ref[at, :width] = d_keys.astype(BF16)
        gkv_ref[at, width:] = d_values.astype(BF16)
        term_ref[at, :] = (d_keys * slope_ref[at, :]).astype(BF16)
        return carry

    lax.fori_loop(0, events // BLOCK, backward, 0)
    d_query = jnp.transpose(dq_scr[...] * (0.5 * DH ** (-0.5)))
    back_out.buffer[...] = spread([d_query, normed]).astype(BF16)


def split_halves(core, rows, scr, mine_out, other_out):
    half = rows.shape[0] // 2
    scr[0] = rows[:half]
    scr[1] = rows[half:]
    other_out.buffer[...] = scr[1 - core]
    other_out.send()
    mine_out.buffer[...] = scr[core]


def history_grads_kernel(core_ref, ev_in, term_in, gkv_in, mine_out, other_out, scr):
    term_ref = term_in.get()
    width = term_ref.shape[1]
    gv = tn(ev_in.get()[...], gkv_in.get()[:, width:])
    gk = tn(ev_in.get()[...], term_ref[...])
    split_halves(core_ref[0], spread([gk, gv]).astype(BF16), scr, mine_out, other_out)


def post_kernel(core_ref, back_in, place_in, aux_in, x_in, w_in, gy_in, mine_out, other_out, gx_out, scr):
    place = place_in.get()[...]
    back_ref, aux_ref, w_ref = back_in.get(), aux_in.get(), w_in.get()
    slots = place.shape[0]
    width = back_ref.shape[1]
    got = back_ref[...].astype(F32).reshape(slots // CAP, 2 * CAP, width)
    d_query = got[:, :CAP].reshape(slots, width).astype(BF16)
    normed = got[:, CAP:].reshape(slots, width).astype(BF16)
    both = tn(place, jnp.concatenate([d_query, normed], axis=1))
    d_query = both[:, :width]
    normed = both[:, width:]
    gates = aux_ref[2]
    gated = (normed * gates).astype(BF16)
    d_gate = (aux_ref[3] * normed).astype(BF16).astype(F32)
    q_term = (d_query * aux_ref[0]).astype(BF16)
    g_term = (d_gate * aux_ref[1]).astype(BF16)
    gx_out.buffer[...] = (nt(q_term, w_ref[0]) + nt(g_term, w_ref[1])).astype(BF16)
    gx_out.send()
    x = x_in.get()[...]
    gq = tn(x, q_term)
    gg = tn(x, g_term)
    go = tn(gated, gy_in.get()[...])
    go = jnp.concatenate([go[:, i * width : (i + 1) * width] for i in range(go.shape[1] // width)], axis=0)
    split_halves(core_ref[0], spread([gq, gg, go]).astype(BF16), scr, mine_out, other_out)


def pair_kernel(a_in, b_in, c_in, d_in, out):
    width = a_in.buffer.shape[1]
    first = a_in.get()[...].astype(F32) + b_in.get()[...].astype(F32)
    second = c_in.get()[...].astype(F32) + d_in.get()[...].astype(F32)
    chunks = first.shape[0] // 16
    joined = jnp.concatenate(
        [first.reshape(chunks, 16, width), second.reshape(chunks, 24, width)], axis=1
    )
    out.buffer[...] = joined.reshape(chunks * 40, width).astype(BF16)


def sum_kernel(factor, rows_in, out):
    got = rows_in.get()[...]
    chunks = got.shape[0] // 40
    total = jnp.sum(got.astype(F32).reshape(chunks, 40, got.shape[1]), axis=0)
    total = total * factor
    shape = out.buffer.shape
    out.buffer[...] = jnp.broadcast_to(total[None], (chunks, 40, shape[1])).reshape(shape).astype(BF16)


def unfold_kernel(core_ref, mine_in, other_in, win_out, wout_out, scr):
    win_ref, wout_ref = win_out.buffer, wout_out.buffer
    width = mine_in.buffer.shape[1]
    core = core_ref[0]
    for source, which in ((mine_in, core), (other_in, 1 - core)):
        got = source.get()[...].astype(F32)
        chunks = got.shape[0] // 40
        got = got.reshape(chunks, 5, 8, width)
        size = chunks * 8
        at = pl.ds(pl.multiple_of(which * size, size), size)
        for place, index in enumerate((2, 3, 0, 1)):
            win_ref[index, at, :] = got[:, place].reshape(size, width)
        scr[at, :] = got[:, 4].reshape(size, width)
    rows = wout_ref.shape[0]
    for i in range(wout_ref.shape[1] // width):
        wout_ref[:, i * width : (i + 1) * width] = scr[i * rows : (i + 1) * rows, :]


class Load:
    def __init__(self, source, buffer, sem):
        self.buffer = buffer
        self.copy = pltpu.make_async_copy(source, buffer, sem)
        self.copy.start()
        self.done = False

    def get(self):
        if not self.done:
            self.copy.wait()
            self.done = True
        return self.buffer


class Store:
    def __init__(self, target, buffer, sem):
        self.buffer = buffer
        self.copy = pltpu.make_async_copy(buffer, target, sem)
        self.started = False

    def send(self):
        if not self.started:
            self.copy.start()
            self.started = True


def call(kernel, outs, ins, scalars=(), scratch=(), flops=0, moved=0):
    ns, ni, no = len(scalars), len(ins), len(outs)

    def body(*refs):
        given, refs = refs[:ns], refs[ns:]
        sources, refs = refs[:ni], refs[ni:]
        targets, refs = refs[:no], refs[no:]
        in_bufs, refs = refs[:ni], refs[ni:]
        out_bufs, refs = refs[:no], refs[no:]
        in_sems, out_sems, extra = refs[0], refs[1], refs[2:]
        loads = [Load(r, b, in_sems.at[i]) for i, (r, b) in enumerate(zip(sources, in_bufs))]
        stores = [Store(r, b, out_sems.at[i]) for i, (r, b) in enumerate(zip(targets, out_bufs))]
        kernel(*given, *loads, *stores, *extra)
        for load in loads:
            load.get()
        for store in stores:
            store.send()
        for store in stores:
            store.copy.wait()

    return pl.pallas_call(
        body,
        out_shape=[jax.ShapeDtypeStruct(s, d) for s, d in outs],
        in_specs=[SMEM] * ns + [ANY] * ni,
        out_specs=[ANY] * no,
        scratch_shapes=[pltpu.VMEM(a.shape, a.dtype) for a in ins]
        + [pltpu.VMEM(s, d) for s, d in outs]
        + [pltpu.SemaphoreType.DMA((ni,)), pltpu.SemaphoreType.DMA((no,))]
        + list(scratch),
        compiler_params=PARAMS,
        cost_estimate=pl.CostEstimate(flops=flops, bytes_accessed=moved, transcendentals=0),
    )(*scalars, *ins)


def on_device(imp_x, imp_hist, imp_len, owner_map, hist_x, w_in, w_out, grad_y):
    owners = lax.axis_size("dp")
    planes = lax.axis_size("mp")
    rows, depth = imp_x.shape
    width = w_in.shape[2]
    slots = owners * CAP
    events = hist_x.shape[1]
    chips = owners // 2
    place_of = lax.axis_index("dp")
    core = (place_of % 2).reshape(1)
    hist = hist_x[0]
    pairs = [(i, i ^ 1) for i in range(owners)]
    same_core = [[2 * i + c for i in range(chips)] for c in range(2)]

    def swap(a):
        return lax.ppermute(a, "dp", pairs)

    def exchange(a):
        a = a.reshape(owners, a.shape[0] // owners, width)
        a = lax.all_to_all(a, "dp", 0, 0, tiled=True)
        return a.reshape(a.shape[0] * a.shape[1], width)

    def exchange_core(a):
        a = a.reshape(chips, a.shape[0] // chips, width)
        a = lax.all_to_all(a, "dp", 0, 0, axis_index_groups=same_core, tiled=True)
        return a.reshape(a.shape[0] * a.shape[1], width)

    send, aux, place = call(
        pre_kernel,
        [((3 * slots, width), BF16), ((4, rows, width), F32), ((slots, rows), BF16)],
        (imp_x, imp_hist.reshape(1, rows), imp_len.reshape(1, rows), owner_map.reshape(1, owners), w_in, w_out, grad_y),
        flops=2 * rows * depth * width * 3,
        moved=1 << 20,
    )
    recv = exchange(send)
    keys, values, keys_t, values_t, key_slope = call(
        project_kernel,
        [((events, width), BF16)] * 2 + [((width, events), BF16)] * 2 + [((events, width), F32)],
        (hist, w_in),
        flops=4 * events * depth * width,
        moved=5 << 20,
    )
    back, gkv, term = call(
        attend_kernel,
        [((2 * slots, width), BF16), ((events, 2 * width), BF16), ((events, width), BF16)],
        (recv, keys, values_t, values, keys_t, key_slope),
        scratch=[
            pltpu.VMEM((width // DH, events, slots), BF16),
            pltpu.VMEM((width // DH, events, slots), BF16),
            pltpu.VMEM((width, slots), F32),
            pltpu.VMEM((width, slots), F32),
        ],
        flops=12 * events * slots * width,
        moved=4 << 20,
    )
    back = exchange(back)
    half = depth * width * 2 // 2 // width
    kv_mine, kv_other = call(
        history_grads_kernel,
        [((half, width), BF16)] * 2,
        (hist, term, gkv),
        (core,),
        scratch=[pltpu.VMEM((2, half, width), BF16)],
        flops=4 * events * depth * width,
        moved=4 << 20,
    )
    kv_other = swap(kv_other)
    back, kv_mine, kv_other = lax.optimization_barrier((back, kv_mine, kv_other))
    half = depth * 3 // 2
    mine, other, gx = call(
        post_kernel,
        [((half, width), BF16)] * 2 + [((rows, depth), BF16)],
        (back, place, aux, imp_x, w_in, grad_y),
        (core,),
        scratch=[pltpu.VMEM((2, half, width), BF16)],
        flops=2 * rows * depth * width * 5,
        moved=2 << 20,
    )
    other = swap(other)
    (summed,) = call(
        pair_kernel, [((chips * 40, width), BF16)], (kv_mine, kv_other, mine, other), moved=1 << 20
    )
    plane = lax.axis_index("mp")
    share = rows // planes
    parts = []
    for step in range(1, planes):
        part = lax.dynamic_slice_in_dim(gx, (plane + step) % planes * share, share, 0)
        parts.append(lax.ppermute(part, "mp", [(i, (i + step) % planes) for i in range(planes)]))
    factor = (rows * owners) ** (-0.5)
    summed, *parts = lax.optimization_barrier((exchange_core(summed), *parts))
    total = lax.dynamic_slice_in_dim(gx, plane * share, share, 0).astype(F32)
    for part in parts:
        total = total + part.astype(F32)
    grad_x = total.astype(BF16)
    (piece,) = call(
        lambda i, o: sum_kernel(factor, i, o),
        [((chips * 40, width), BF16)],
        (summed,),
        moved=1 << 20,
    )
    mine = exchange_core(piece)
    other = swap(mine)
    grad_w_in, grad_w_out = call(
        unfold_kernel,
        [((4, depth, width), F32), ((width, depth), F32)],
        (mine, other),
        (core,),
        scratch=[pltpu.VMEM((depth, width), F32)],
        moved=3 << 20,
    )
    grad_kv = gkv.reshape(1, events, 2, width)
    return (grad_x, grad_kv, grad_w_in, grad_w_out)


def solution(mesh):
    placed = (
        P("dp", None),
        P("dp", None),
        P("dp"),
        P(),
        P("dp", None, None),
        P(None, None, "mp"),
        P("mp", None),
        P("dp", None),
    )
    return jax.shard_map(
        on_device,
        mesh=mesh,
        in_specs=placed,
        out_specs=(
            P(("dp", "mp"), None),
            P("dp", None, None, "mp"),
            P(None, None, "mp"),
            P("mp", None),
        ),
        check_vma=False,
    )
```

```python
import jax
import jax.numpy as jnp
from jax import lax
from jax.experimental import pallas as pl
from jax.experimental.pallas import tpu as pltpu
from jax.sharding import PartitionSpec as P

DH = 64
EPSILON = 1e-05
CAP = 8
BLOCK = 1024
F32 = jnp.float32
BF16 = jnp.bfloat16
ANY = pl.BlockSpec(memory_space=pl.ANY)
VMEM = pl.BlockSpec(memory_space=pltpu.VMEM)
SMEM = pl.BlockSpec(memory_space=pltpu.SMEM)
PARAMS = pltpu.CompilerParams(vmem_limit_bytes=40 * 1024 * 1024)


def nn(a, b):
    return lax.dot_general(a, b, (((1,), (0,)), ((), ())), preferred_element_type=F32)


def nt(a, b):
    return lax.dot_general(a, b, (((1,), (1,)), ((), ())), preferred_element_type=F32)


def tn(a, b):
    return lax.dot_general(a, b, (((0,), (0,)), ((), ())), preferred_element_type=F32)


def sigmoid(v):
    return 0.5 * jnp.tanh(0.5 * v) + 0.5


def silu_and_slope(v):
    s = sigmoid(v)
    return v * s, s * (1.0 + v * (1.0 - s))


def iota(shape, dim):
    return lax.broadcasted_iota(jnp.int32, shape, dim)


def spread(parts):
    count = parts[0].shape[0] // 8
    cut = [p.reshape(count, 8, p.shape[1]) for p in parts]
    joined = jnp.concatenate(cut, axis=1)
    return joined.reshape(count * 8 * len(parts), parts[0].shape[1])


def pre_kernel(x_in, hist_in, len_in, owner_in, w_in, wo_in, gy_in, send_out, aux_out, place_out):
    hist = hist_in.get()[...]
    owner = owner_in.get()[...]
    rows, owners = hist.shape[1], owner.shape[1]
    named = jnp.where(iota((owners, rows), 0) == hist, 1.0, 0.0).astype(BF16)
    owner = jnp.broadcast_to(owner.astype(F32), (8, owners)).astype(BF16)
    target = nn(owner, named)[:1]
    hit = jnp.where(iota((owners, rows), 0).astype(F32) == target, 1.0, 0.0)
    earlier = jnp.where(iota((rows, rows), 0) < iota((rows, rows), 1), 1.0, 0.0)
    before = nn(hit.astype(BF16), earlier.astype(BF16))
    rank = jnp.sum(before * hit, axis=0, keepdims=True)
    slot = target * float(CAP) + rank
    slots = owners * CAP
    place = jnp.where(iota((slots, rows), 0).astype(F32) == slot, 1.0, 0.0).astype(BF16)
    place_out.buffer[...] = place
    place_out.send()
    length = len_in.get()[...].astype(F32)
    high = jnp.floor(length * (1.0 / 256.0))
    low = length - 256.0 * high
    digits = jnp.transpose(jnp.where(iota((rows, rows), 0) == 0, high, low))
    x, w_ref = x_in.get()[...], w_in.get()
    queries, slope_q = silu_and_slope(nn(x, w_ref[0]))
    gates, slope_g = silu_and_slope(nn(x, w_ref[1]))
    cot = nt(gy_in.get()[...], wo_in.get()[...]).astype(BF16).astype(F32)
    gates = gates.astype(BF16).astype(F32)
    payload = jnp.concatenate(
        [queries.astype(BF16), (cot * gates).astype(BF16), digits.astype(BF16)], axis=1
    )
    packed = nn(place, payload)
    width = queries.shape[1]
    send_out.buffer[...] = spread(
        [packed[:, :width], packed[:, width : 2 * width], packed[:, 2 * width :]]
    ).astype(BF16)
    send_out.send()
    aux_out.buffer[0] = slope_q
    aux_out.buffer[1] = slope_g
    aux_out.buffer[2] = gates
    aux_out.buffer[3] = cot


def project_kernel(ev_in, w_in, k_out, v_out, kt_out, vt_out, slope_out):
    ev_ref, w_ref = ev_in.get(), w_in.get()

    def step(b, carry):
        at = pl.ds(pl.multiple_of(b * 512, 512), 512)
        ev = ev_ref[at, :]
        keys, slope = silu_and_slope(nn(ev, w_ref[2]))
        values = nn(ev, w_ref[3])
        k_out.buffer[at, :] = keys.astype(BF16)
        v_out.buffer[at, :] = values.astype(BF16)
        slope_out.buffer[at, :] = slope
        kt_out.buffer[:, at] = jnp.transpose(keys.astype(BF16))
        vt_out.buffer[:, at] = jnp.transpose(values.astype(BF16))
        return carry

    lax.fori_loop(0, ev_ref.shape[0] // 512, step, 0)


def attend_kernel(
    recv_in, k_in, vt_in, v_in, kt_in, slope_in,
    back_out, gkv_out, term_out,
    w_scr, s_scr, att_scr, dq_scr,
):
    gkv_ref, term_ref = gkv_out.buffer, term_out.buffer
    recv_ref = recv_in.get()
    slots, width = recv_ref.shape[0] // 3, recv_ref.shape[1]
    heads = width // DH
    got = recv_ref[...].astype(F32).reshape(slots // CAP, 3 * CAP, width)
    q = got[:, :CAP].reshape(slots, width)
    dn = got[:, CAP : 2 * CAP].reshape(slots, width)
    digits = got[:, 2 * CAP :].reshape(slots, width)
    digits = jnp.transpose(digits)
    length = digits[0:1] * 256.0 + digits[1:2]
    qt = jnp.transpose(q)
    head_row = iota((width, slots), 0) // DH
    head_col = iota((slots, width), 1) // DH
    qt_half = (qt * (0.5 * DH ** (-0.5))).astype(BF16)
    zero = jnp.zeros((), BF16)
    qt_of = [jnp.where(head_row == h, qt_half, zero) for h in range(heads)]
    att_scr[...] = jnp.zeros_like(att_scr)
    k_ref, vt_ref = k_in.get(), vt_in.get()
    events = k_ref.shape[0]

    def forward(b, carry):
        start = pl.multiple_of(b * BLOCK, BLOCK)
        at = pl.ds(start, BLOCK)
        visible = (iota((BLOCK, slots), 0) + start).astype(F32) < length
        for h in range(heads):
            half = nn(k_ref[at, :], qt_of[h])
            twice = jnp.where(visible, jnp.tanh(half) + 1.0, 0.0)
            weights = half * twice
            s_scr[h, at, :] = (twice + weights * (2.0 - twice)).astype(BF16)
            weights = weights.astype(BF16)
            w_scr[h, at, :] = weights
            mine = pl.ds(h * DH, DH)
            att_scr[mine, :] += nn(vt_ref[mine, at], weights)
        return carry

    lax.fori_loop(0, events // BLOCK, forward, 0)
    att = att_scr[...].reshape(heads, DH, slots)
    inverse = lax.rsqrt(jnp.mean(att * att, axis=1, keepdims=True) + EPSILON)
    normed = att * inverse
    dnt = jnp.transpose(dn).reshape(heads, DH, slots)
    d_att = inverse * (dnt - normed * jnp.mean(dnt * normed, axis=1, keepdims=True))
    d_att = d_att.reshape(width, slots)
    d_att_t = d_att.astype(BF16)
    d_att = jnp.transpose(d_att).astype(BF16)
    normed = jnp.transpose(normed.reshape(width, slots))
    q_bf = q.astype(BF16)
    dt_of = [jnp.where(head_row == h, d_att_t, zero) for h in range(heads)]
    d_of = [jnp.where(head_col == h, d_att, zero) for h in range(heads)]
    q_of = [jnp.where(head_col == h, q_bf, zero) for h in range(heads)]
    dq_scr[...] = jnp.zeros_like(dq_scr)
    v_ref, kt_ref, slope_ref = v_in.get(), kt_in.get(), slope_in.get()

    def backward(b, carry):
        at = pl.ds(pl.multiple_of(b * BLOCK, BLOCK), BLOCK)
        d_keys = jnp.zeros((BLOCK, width), F32)
        d_values = jnp.zeros((BLOCK, width), F32)
        for h in range(heads):
            ds = (nn(v_ref[at, :], dt_of[h]) * s_scr[h, at, :].astype(F32)).astype(BF16)
            mine = pl.ds(h * DH, DH)
            dq_scr[mine, :] += nn(kt_ref[mine, at], ds)
            d_keys += nn(ds, q_of[h])
            d_values += nn(w_scr[h, at, :], d_of[h])
        d_keys = d_keys * (0.5 * DH ** (-0.5))
        gkv_ref[at, :width] = d_keys.astype(BF16)
        gkv_ref[at, width:] = d_values.astype(BF16)
        term_ref[at, :] = (d_keys * slope_ref[at, :]).astype(BF16)
        return carry

    lax.fori_loop(0, events // BLOCK, backward, 0)
    d_query = jnp.transpose(dq_scr[...] * (0.5 * DH ** (-0.5)))
    back_out.buffer[...] = spread([d_query, normed]).astype(BF16)


def split_halves(core, rows, scr, mine_out, other_out):
    half = rows.shape[0] // 2
    scr[0] = rows[:half]
    scr[1] = rows[half:]
    other_out.buffer[...] = scr[1 - core]
    other_out.send()
    mine_out.buffer[...] = scr[core]


def history_grads_kernel(core_ref, ev_in, term_in, gkv_in, mine_out, other_out, scr):
    term_ref = term_in.get()
    width = term_ref.shape[1]
    gv = tn(ev_in.get()[...], gkv_in.get()[:, width:])
    gk = tn(ev_in.get()[...], term_ref[...])
    split_halves(core_ref[0], spread([gk, gv]).astype(BF16), scr, mine_out, other_out)


def post_kernel(core_ref, back_in, place_in, aux_in, x_in, w_in, gy_in, mine_out, other_out, gx_out, scr):
    place = place_in.get()[...]
    back_ref, aux_ref, w_ref = back_in.get(), aux_in.get(), w_in.get()
    slots = place.shape[0]
    width = back_ref.shape[1]
    got = back_ref[...].astype(F32).reshape(slots // CAP, 2 * CAP, width)
    d_query = got[:, :CAP].reshape(slots, width).astype(BF16)
    normed = got[:, CAP:].reshape(slots, width).astype(BF16)
    both = tn(place, jnp.concatenate([d_query, normed], axis=1))
    d_query = both[:, :width]
    normed = both[:, width:]
    gates = aux_ref[2]
    gated = (normed * gates).astype(BF16)
    d_gate = (aux_ref[3] * normed).astype(BF16).astype(F32)
    q_term = (d_query * aux_ref[0]).astype(BF16)
    g_term = (d_gate * aux_ref[1]).astype(BF16)
    gx_out.buffer[...] = (nt(q_term, w_ref[0]) + nt(g_term, w_ref[1])).astype(BF16)
    gx_out.send()
    x = x_in.get()[...]
    gq = tn(x, q_term)
    gg = tn(x, g_term)
    go = tn(gated, gy_in.get()[...])
    go = jnp.concatenate([go[:, i * width : (i + 1) * width] for i in range(go.shape[1] // width)], axis=0)
    split_halves(core_ref[0], spread([gq, gg, go]).astype(BF16), scr, mine_out, other_out)


def pair_kernel(a_in, b_in, c_in, d_in, out):
    width = a_in.buffer.shape[1]
    first = a_in.get()[...].astype(F32) + b_in.get()[...].astype(F32)
    second = c_in.get()[...].astype(F32) + d_in.get()[...].astype(F32)
    chunks = first.shape[0] // 16
    joined = jnp.concatenate(
        [first.reshape(chunks, 16, width), second.reshape(chunks, 24, width)], axis=1
    )
    out.buffer[...] = joined.reshape(chunks * 40, width).astype(BF16)


def sum_kernel(factor, rows_in, out):
    got = rows_in.get()[...]
    chunks = got.shape[0] // 40
    total = jnp.sum(got.astype(F32).reshape(chunks, 40, got.shape[1]), axis=0)
    total = total * factor
    shape = out.buffer.shape
    out.buffer[...] = jnp.broadcast_to(total[None], (chunks, 40, shape[1])).reshape(shape).astype(BF16)


def unfold_kernel(core_ref, mine_in, other_in, win_out, wout_out, scr):
    win_ref, wout_ref = win_out.buffer, wout_out.buffer
    width = mine_in.buffer.shape[1]
    core = core_ref[0]
    for source, which in ((mine_in, core), (other_in, 1 - core)):
        got = source.get()[...].astype(F32)
        chunks = got.shape[0] // 40
        got = got.reshape(chunks, 5, 8, width)
        size = chunks * 8
        at = pl.ds(pl.multiple_of(which * size, size), size)
        for place, index in enumerate((2, 3, 0, 1)):
            win_ref[index, at, :] = got[:, place].reshape(size, width)
        scr[at, :] = got[:, 4].reshape(size, width)
    rows = wout_ref.shape[0]
    for i in range(wout_ref.shape[1] // width):
        wout_ref[:, i * width : (i + 1) * width] = scr[i * rows : (i + 1) * rows, :]


class Load:
    def __init__(self, source, buffer=None, sem=None):
        self.buffer, self.copy = source, None
        if buffer is not None:
            self.buffer = buffer
            self.copy = pltpu.make_async_copy(source, buffer, sem)
            self.copy.start()

    def get(self):
        if self.copy is not None:
            self.copy.wait()
            self.copy = None
        return self.buffer


class Store:
    def __init__(self, target, buffer=None, sem=None):
        self.buffer, self.copy, self.started = target, None, False
        if buffer is not None:
            self.buffer = buffer
            self.copy = pltpu.make_async_copy(buffer, target, sem)

    def send(self):
        if self.copy is not None and not self.started:
            self.copy.start()
            self.started = True

    def wait(self):
        if self.copy is not None:
            self.copy.wait()


def call(kernel, outs, ins, scalars=(), scratch=(), near_in=(), near_out=(), flops=0, moved=0):
    ns, ni, no = len(scalars), len(ins), len(outs)
    far_in = [i for i in range(ni) if i not in near_in]
    far_out = [i for i in range(no) if i not in near_out]

    ins = [
        a if i in near_in else pltpu.with_memory_space_constraint(a, pltpu.HBM) for i, a in enumerate(ins)
    ]

    def body(*refs):
        given, refs = refs[:ns], refs[ns:]
        sources, refs = refs[:ni], refs[ni:]
        targets, refs = refs[:no], refs[no:]
        in_bufs, refs = dict(zip(far_in, refs)), refs[len(far_in) :]
        out_bufs, refs = dict(zip(far_out, refs)), refs[len(far_out) :]
        sems, extra = refs[0], refs[1:]
        loads = [
            Load(r, in_bufs[i], sems.at[i]) if i in in_bufs else Load(r) for i, r in enumerate(sources)
        ]
        stores = [
            Store(r, out_bufs[i], sems.at[ni + i]) if i in out_bufs else Store(r)
            for i, r in enumerate(targets)
        ]
        kernel(*given, *loads, *stores, *extra)
        for load in loads:
            load.get()
        for store in stores:
            store.send()
        for store in stores:
            store.wait()

    return pl.pallas_call(
        body,
        out_shape=[
            jax.ShapeDtypeStruct(s, d) if i in near_out else pltpu.HBM(s, d) for i, (s, d) in enumerate(outs)
        ],
        in_specs=[SMEM] * ns + [VMEM if i in near_in else ANY for i in range(ni)],
        out_specs=[VMEM if i in near_out else ANY for i in range(no)],
        scratch_shapes=[pltpu.VMEM(ins[i].shape, ins[i].dtype) for i in far_in]
        + [pltpu.VMEM(*outs[i]) for i in far_out]
        + [pltpu.SemaphoreType.DMA((ni + no,))]
        + list(scratch),
        compiler_params=PARAMS,
        cost_estimate=pl.CostEstimate(flops=flops, bytes_accessed=moved, transcendentals=0),
    )(*scalars, *ins)


def on_device(imp_x, imp_hist, imp_len, owner_map, hist_x, w_in, w_out, grad_y):
    owners = lax.axis_size("dp")
    planes = lax.axis_size("mp")
    rows, depth = imp_x.shape
    width = w_in.shape[2]
    slots = owners * CAP
    events = hist_x.shape[1]
    chips = owners // 2
    place_of = lax.axis_index("dp")
    core = (place_of % 2).reshape(1)
    hist = hist_x[0]
    pairs = [(i, i ^ 1) for i in range(owners)]
    same_core = [[2 * i + c for i in range(chips)] for c in range(2)]

    def swap(a):
        return lax.ppermute(a, "dp", pairs)

    def exchange(a):
        a = a.reshape(owners, a.shape[0] // owners, width)
        a = lax.all_to_all(a, "dp", 0, 0, tiled=True)
        return a.reshape(a.shape[0] * a.shape[1], width)

    def exchange_core(a):
        a = a.reshape(chips, a.shape[0] // chips, width)
        a = lax.all_to_all(a, "dp", 0, 0, axis_index_groups=same_core, tiled=True)
        return a.reshape(a.shape[0] * a.shape[1], width)

    send, aux, place = call(
        pre_kernel,
        [((3 * slots, width), BF16), ((4, rows, width), F32), ((slots, rows), BF16)],
        (imp_x, imp_hist.reshape(1, rows), imp_len.reshape(1, rows), owner_map.reshape(1, owners), w_in, w_out, grad_y),
        near_out=(0,),
        flops=2 * rows * depth * width * 3,
        moved=1 << 20,
    )
    recv = exchange(send)
    keys, values, keys_t, values_t, key_slope = call(
        project_kernel,
        [((events, width), BF16)] * 2 + [((width, events), BF16)] * 2 + [((events, width), F32)],
        (hist, w_in),
        flops=4 * events * depth * width,
        moved=5 << 20,
    )
    back, gkv, term = call(
        attend_kernel,
        [((2 * slots, width), BF16), ((events, 2 * width), BF16), ((events, width), BF16)],
        (recv, keys, values_t, values, keys_t, key_slope),
        scratch=[
            pltpu.VMEM((width // DH, events, slots), BF16),
            pltpu.VMEM((width // DH, events, slots), BF16),
            pltpu.VMEM((width, slots), F32),
            pltpu.VMEM((width, slots), F32),
        ],
        near_in=(0,),
        near_out=(0,),
        flops=12 * events * slots * width,
        moved=4 << 20,
    )
    back = exchange(back)
    half = depth * width * 2 // 2 // width
    kv_mine, kv_other = call(
        history_grads_kernel,
        [((half, width), BF16)] * 2,
        (hist, term, gkv),
        (core,),
        scratch=[pltpu.VMEM((2, half, width), BF16)],
        near_out=(0, 1),
        flops=4 * events * depth * width,
        moved=4 << 20,
    )
    kv_other = swap(kv_other)
    back, kv_mine, kv_other = lax.optimization_barrier((back, kv_mine, kv_other))
    half = depth * 3 // 2
    mine, other, gx = call(
        post_kernel,
        [((half, width), BF16)] * 2 + [((rows, depth), BF16)],
        (back, place, aux, imp_x, w_in, grad_y),
        (core,),
        scratch=[pltpu.VMEM((2, half, width), BF16)],
        near_in=(0,),
        near_out=(0, 1, 2),
        flops=2 * rows * depth * width * 5,
        moved=2 << 20,
    )
    other = swap(other)
    (summed,) = call(
        pair_kernel,
        [((chips * 40, width), BF16)],
        (kv_mine, kv_other, mine, other),
        near_in=(0, 1, 2, 3),
        near_out=(0,),
        moved=1 << 20,
    )
    plane = lax.axis_index("mp")
    share = rows // planes
    parts = []
    for step in range(1, planes):
        part = lax.dynamic_slice_in_dim(gx, (plane + step) % planes * share, share, 0)
        parts.append(lax.ppermute(part, "mp", [(i, (i + step) % planes) for i in range(planes)]))
    factor = (rows * owners) ** (-0.5)
    summed, *parts = lax.optimization_barrier((exchange_core(summed), *parts))
    total = lax.dynamic_slice_in_dim(gx, plane * share, share, 0).astype(F32)
    for part in parts:
        total = total + part.astype(F32)
    grad_x = total.astype(BF16)
    (piece,) = call(
        lambda i, o: sum_kernel(factor, i, o),
        [((chips * 40, width), BF16)],
        (summed,),
        near_in=(0,),
        near_out=(0,),
        moved=1 << 20,
    )
    mine = exchange_core(piece)
    other = swap(mine)
    grad_w_in, grad_w_out = call(
        unfold_kernel,
        [((4, depth, width), F32), ((width, depth), F32)],
        (mine, other),
        (core,),
        scratch=[pltpu.VMEM((depth, width), F32)],
        near_in=(0, 1),
        moved=3 << 20,
    )
    grad_kv = gkv.reshape(1, events, 2, width)
    return (grad_x, grad_kv, grad_w_in, grad_w_out)


def solution(mesh):
    placed = (
        P("dp", None),
        P("dp", None),
        P("dp"),
        P(),
        P("dp", None, None),
        P(None, None, "mp"),
        P("mp", None),
        P("dp", None),
    )
    return jax.shard_map(
        on_device,
        mesh=mesh,
        in_specs=placed,
        out_specs=(
            P(("dp", "mp"), None),
            P("dp", None, None, "mp"),
            P(None, None, "mp"),
            P("mp", None),
        ),
        check_vma=False,
    )
```

```python
import jax
import jax.numpy as jnp
from jax import lax
from jax.experimental import pallas as pl
from jax.experimental.pallas import tpu as pltpu
from jax.sharding import PartitionSpec as P

DH = 64
EPSILON = 1e-05
CAP = 8
BLOCK = 1024
HISTORY_PARTS = 4
LATE = 5
F32 = jnp.float32
BF16 = jnp.bfloat16
ANY = pl.BlockSpec(memory_space=pl.ANY)
VMEM = pl.BlockSpec(memory_space=pltpu.VMEM)
SMEM = pl.BlockSpec(memory_space=pltpu.SMEM)
PARAMS = pltpu.CompilerParams(vmem_limit_bytes=40 * 1024 * 1024)


def nn(a, b):
    return lax.dot_general(a, b, (((1,), (0,)), ((), ())), preferred_element_type=F32)


def nt(a, b):
    return lax.dot_general(a, b, (((1,), (1,)), ((), ())), preferred_element_type=F32)


def tn(a, b):
    return lax.dot_general(a, b, (((0,), (0,)), ((), ())), preferred_element_type=F32)


def sigmoid(v):
    return 0.5 * jnp.tanh(0.5 * v) + 0.5


def silu_and_slope(v):
    s = sigmoid(v)
    return v * s, s * (1.0 + v * (1.0 - s))


def iota(shape, dim):
    return lax.broadcasted_iota(jnp.int32, shape, dim)


def spread(parts):
    count = parts[0].shape[0] // 8
    cut = [p.reshape(count, 8, p.shape[1]) for p in parts]
    joined = jnp.concatenate(cut, axis=1)
    return joined.reshape(count * 8 * len(parts), parts[0].shape[1])


def slot_table(hist, owner):
    rows, owners = hist.shape[1], owner.shape[1]
    named = jnp.where(iota((owners, rows), 0) == hist, 1.0, 0.0).astype(BF16)
    owner = jnp.broadcast_to(owner.astype(F32), (8, owners)).astype(BF16)
    target = nn(owner, named)[:1]
    hit = jnp.where(iota((owners, rows), 0).astype(F32) == target, 1.0, 0.0)
    earlier = jnp.where(iota((rows, rows), 0) < iota((rows, rows), 1), 1.0, 0.0)
    before = nn(hit.astype(BF16), earlier.astype(BF16))
    rank = jnp.sum(before * hit, axis=0, keepdims=True)
    slot = target * float(CAP) + rank
    return jnp.where(iota((owners * CAP, rows), 0).astype(F32) == slot, 1.0, 0.0).astype(BF16)


def pre_kernel(hist_in, len_in, owner_in, x_in, w_in, wo_in, gy_in, send_out):
    place = slot_table(hist_in.get()[...], owner_in.get()[...])
    length = len_in.get()[...].astype(F32)
    rows = length.shape[1]
    high = jnp.floor(length * (1.0 / 256.0))
    low = length - 256.0 * high
    digits = jnp.transpose(jnp.where(iota((rows, rows), 0) == 0, high, low))
    x, w_ref = x_in.get()[...], w_in.get()
    queries, _ = silu_and_slope(nn(x, w_ref[0]))
    gates, _ = silu_and_slope(nn(x, w_ref[1]))
    cot = nt(gy_in.get()[...], wo_in.get()[...]).astype(BF16).astype(F32)
    gates = gates.astype(BF16).astype(F32)
    payload = jnp.concatenate(
        [queries.astype(BF16), (cot * gates).astype(BF16), digits.astype(BF16)], axis=1
    )
    packed = nn(place, payload)
    width = queries.shape[1]
    send_out.buffer[...] = spread(
        [packed[:, :width], packed[:, width : 2 * width], packed[:, 2 * width :]]
    ).astype(BF16)


def project_kernel(
    w_in, ev_in, hist_in, owner_in, x_in, wo_in, gy_in,
    k_out, vt_out, v_out, kt_out, slope_out, aux_out, place_out,
):
    w_ref, ev_ref = w_in.get(), ev_in.get()
    count = ev_ref.shape[0] // 512
    for b in range(count):
        at = pl.ds(b * 512, 512)
        ev = ev_ref[at, :]
        keys, slope = silu_and_slope(nn(ev, w_ref[2]))
        values = nn(ev, w_ref[3])
        k_out.buffer[at, :] = keys.astype(BF16)
        v_out.buffer[at, :] = values.astype(BF16)
        slope_out.buffer[at, :] = slope
        kt_out.buffer[:, at] = jnp.transpose(keys.astype(BF16))
        vt_out.buffer[:, at] = jnp.transpose(values.astype(BF16))
    for out in (k_out, v_out, kt_out, vt_out, slope_out):
        out.send()
    place_out.buffer[...] = slot_table(hist_in.get()[...], owner_in.get()[...])
    x = x_in.get()[...]
    _, slope_q = silu_and_slope(nn(x, w_ref[0]))
    gates, slope_g = silu_and_slope(nn(x, w_ref[1]))
    aux_out.buffer[0] = slope_q
    aux_out.buffer[1] = slope_g
    aux_out.buffer[2] = gates.astype(BF16).astype(F32)
    aux_out.buffer[3] = nt(gy_in.get()[...], wo_in.get()[...]).astype(BF16).astype(F32)


def attend_kernel(
    recv_in, k_in, vt_in, v_in, kt_in,
    back_out, weights_out, d_keys_out, d_att_out,
    s_scr,
):
    recv_ref, k_ref, vt_ref = recv_in.get(), k_in.get(), vt_in.get()
    slots, width = recv_ref.shape[0] // 3, recv_ref.shape[1]
    heads = width // DH
    events = k_ref.shape[0]
    got = recv_ref[...].astype(F32).reshape(slots // CAP, 3 * CAP, width)
    q = got[:, :CAP].reshape(slots, width)
    dn = got[:, CAP : 2 * CAP].reshape(slots, width)
    digits = got[:, 2 * CAP :].reshape(slots, width)
    digits = jnp.transpose(digits)
    length = digits[0:1] * 256.0 + digits[1:2]
    head_row = iota((width, slots), 0) // DH
    head_col = iota((slots, width), 1) // DH
    qt_half = (jnp.transpose(q) * (0.5 * DH ** (-0.5))).astype(BF16)
    zero = jnp.zeros((), BF16)
    qt_of = [jnp.where(head_row == h, qt_half, zero) for h in range(heads)]
    att = [jnp.zeros((DH, slots), F32)] * heads
    for start in range(0, events, BLOCK):
        at = pl.ds(start, BLOCK)
        visible = (iota((BLOCK, slots), 0) + start).astype(F32) < length
        for h in range(heads):
            cols = slice(h * slots, (h + 1) * slots)
            half = nn(k_ref[at, :], qt_of[h])
            twice = jnp.where(visible, jnp.tanh(half) + 1.0, 0.0)
            weights = half * twice
            s_scr[at, cols] = (twice + weights * (2.0 - twice)).astype(BF16)
            weights = weights.astype(BF16)
            weights_out.buffer[at, cols] = weights
            att[h] += nn(vt_ref[h * DH : (h + 1) * DH, at], weights)
        weights_out.send_part((at,))
    att = jnp.concatenate(att, axis=0).reshape(heads, DH, slots)
    inverse = lax.rsqrt(jnp.mean(att * att, axis=1, keepdims=True) + EPSILON)
    normed = att * inverse
    dnt = jnp.transpose(dn).reshape(heads, DH, slots)
    d_att = inverse * (dnt - normed * jnp.mean(dnt * normed, axis=1, keepdims=True))
    d_att = d_att.reshape(width, slots)
    d_att_t = d_att.astype(BF16)
    d_att_out.buffer[...] = jnp.transpose(d_att).astype(BF16)
    d_att_out.send()
    normed = jnp.transpose(normed.reshape(width, slots))
    dt_of = [jnp.where(head_row == h, d_att_t, zero) for h in range(heads)]
    q_bf = q.astype(BF16)
    q_of = jnp.concatenate([jnp.where(head_col == h, q_bf, zero) for h in range(heads)], axis=0)
    v_ref, kt_ref = v_in.get(), kt_in.get()
    d_query = [jnp.zeros((DH, slots), F32)] * heads
    for start in range(0, events, BLOCK):
        at = pl.ds(start, BLOCK)
        for h in range(heads):
            cols = slice(h * slots, (h + 1) * slots)
            ds = (nn(v_ref[at, :], dt_of[h]) * s_scr[at, cols].astype(F32)).astype(BF16)
            s_scr[at, cols] = ds
            d_query[h] += nn(kt_ref[h * DH : (h + 1) * DH, at], ds)
        d_keys = nn(s_scr[at, :], q_of) * (0.5 * DH ** (-0.5))
        d_keys_out.buffer[at, :] = d_keys.astype(BF16)
        d_keys_out.send_part((at,))
    d_query = jnp.concatenate(d_query, axis=0) * (0.5 * DH ** (-0.5))
    back_out.buffer[...] = spread([jnp.transpose(d_query), normed]).astype(BF16)


def history_kernel(
    core_ref, d_att_in, d_keys_in, slope_in, weights_in, ev_in, *rest
):
    late, rest = rest[:LATE], rest[LATE:]
    gkv_out, mine_out, other_out, rest = rest[0], rest[1], rest[2], rest[3:]
    kept, (scr, w_scr, term_scr, sems, late_sems) = rest[:LATE], rest[LATE:]
    events = w_scr.shape[0]
    step = events // HISTORY_PARTS
    parts = [pl.ds(b * step, step) for b in range(HISTORY_PARTS)]
    copies = [
        pltpu.make_async_copy(weights_in.get().at[at], w_scr.at[at], sems.at[b])
        for b, at in enumerate(parts)
    ]
    for copy in copies:
        copy.start()
    moves = [
        pltpu.make_async_copy(src.get().at[: dst.buffer.shape[0]], dst.buffer, late_sems.at[i])
        for i, (src, dst) in enumerate(zip(late, kept))
    ]
    for move in moves:
        move.start()
    d_att = d_att_in.get()[...]
    slots, width = d_att.shape
    heads = width // DH
    head_col = iota((slots, width), 1) // DH
    zero = jnp.zeros((), BF16)
    d_of = jnp.concatenate([jnp.where(head_col == h, d_att, zero) for h in range(heads)], axis=0)
    d_keys_ref, slope_ref, gkv_ref = d_keys_in.get(), slope_in.get(), gkv_out.buffer
    for at, copy in zip(parts, copies):
        d_keys = d_keys_ref[at, :]
        gkv_ref[at, :width] = d_keys
        term_scr[at, :width] = (d_keys.astype(F32) * slope_ref[at, :]).astype(BF16)
        copy.wait()
        d_values = nn(w_scr[at, :], d_of).astype(BF16)
        gkv_ref[at, width:] = d_values
        gkv_out.send_part((at,))
        term_scr[at, width:] = d_values
    both = jnp.transpose(tn(term_scr[...], ev_in.get()[...]))
    rows = spread([both[:, :width], both[:, width:]]).astype(BF16)
    split_halves(core_ref[0], rows, scr, mine_out, other_out)
    for move in moves:
        move.wait()


def split_halves(core, rows, scr, mine_out, other_out):
    half = rows.shape[0] // 2
    scr[0] = rows[:half]
    scr[1] = rows[half:]
    other_out.buffer[...] = scr[1 - core]
    other_out.send()
    mine_out.buffer[...] = scr[core]


def post_kernel(core_ref, back_in, place_in, aux_in, x_in, w_in, gy_in, mine_out, other_out, gx_out, scr):
    place = place_in.get()[...]
    back_ref, aux_ref, w_ref = back_in.get(), aux_in.get(), w_in.get()
    slots = place.shape[0]
    width = back_ref.shape[1]
    got = back_ref[...].astype(F32).reshape(slots // CAP, 2 * CAP, width)
    d_query = got[:, :CAP].reshape(slots, width).astype(BF16)
    normed = got[:, CAP:].reshape(slots, width).astype(BF16)
    both = tn(place, jnp.concatenate([d_query, normed], axis=1))
    d_query = both[:, :width]
    normed = both[:, width:]
    gates = aux_ref[2]
    gated = (normed * gates).astype(BF16)
    d_gate = (aux_ref[3] * normed).astype(BF16).astype(F32)
    q_term = (d_query * aux_ref[0]).astype(BF16)
    g_term = (d_gate * aux_ref[1]).astype(BF16)
    gx_out.buffer[...] = (nt(q_term, w_ref[0]) + nt(g_term, w_ref[1])).astype(BF16)
    gx_out.send()
    x = x_in.get()[...]
    gq = tn(x, q_term)
    gg = tn(x, g_term)
    go = tn(gated, gy_in.get()[...])
    go = jnp.concatenate([go[:, i * width : (i + 1) * width] for i in range(go.shape[1] // width)], axis=0)
    split_halves(core_ref[0], spread([gq, gg, go]).astype(BF16), scr, mine_out, other_out)


def pair_kernel(a_in, b_in, c_in, d_in, out):
    width = a_in.buffer.shape[1]
    first = a_in.get()[...].astype(F32) + b_in.get()[...].astype(F32)
    second = c_in.get()[...].astype(F32) + d_in.get()[...].astype(F32)
    chunks = first.shape[0] // 16
    joined = jnp.concatenate(
        [first.reshape(chunks, 16, width), second.reshape(chunks, 24, width)], axis=1
    )
    out.buffer[...] = joined.reshape(chunks * 40, width).astype(BF16)


def sum_kernel(factor, rows_in, out):
    got = rows_in.get()[...]
    chunks = got.shape[0] // 40
    total = jnp.sum(got.astype(F32).reshape(chunks, 40, got.shape[1]), axis=0)
    total = total * factor
    shape = out.buffer.shape
    out.buffer[...] = jnp.broadcast_to(total[None], (chunks, 40, shape[1])).reshape(shape).astype(BF16)


def unfold_kernel(core_ref, mine_in, other_in, win_out, wout_out, scr):
    win_ref, wout_ref = win_out.buffer, wout_out.buffer
    width = mine_in.buffer.shape[1]
    core = core_ref[0]
    for source, which in ((mine_in, core), (other_in, 1 - core)):
        got = source.get()[...].astype(F32)
        chunks = got.shape[0] // 40
        got = got.reshape(chunks, 5, 8, width)
        size = chunks * 8
        at = pl.ds(pl.multiple_of(which * size, size), size)
        for place, index in enumerate((2, 3, 0, 1)):
            win_ref[index, at, :] = got[:, place].reshape(size, width)
        scr[at, :] = got[:, 4].reshape(size, width)
    rows = wout_ref.shape[0]
    for i in range(wout_ref.shape[1] // width):
        wout_ref[:, i * width : (i + 1) * width] = scr[i * rows : (i + 1) * rows, :]


class Load:
    def __init__(self, source, buffer=None, sem=None):
        self.buffer, self.copy = source, None
        if buffer is not None:
            self.buffer = buffer
            self.copy = pltpu.make_async_copy(source, buffer, sem)
            self.copy.start()

    def get(self):
        if self.copy is not None:
            self.copy.wait()
            self.copy = None
        return self.buffer


class Store:
    def __init__(self, target, buffer=None, sem=None):
        self.buffer, self.copy, self.started = target, None, False
        self.target, self.sem = target, sem
        if buffer is not None:
            self.buffer = buffer
            self.copy = pltpu.make_async_copy(buffer, target, sem)

    def send(self):
        if self.copy is not None and not self.started:
            self.copy.start()
            self.started = True

    def send_part(self, at):
        pltpu.make_async_copy(self.buffer.at[at], self.target.at[at], self.sem).start()
        self.started = True

    def wait(self):
        if self.copy is not None:
            self.copy.wait()


def call(kernel, outs, ins, scalars=(), scratch=(), near_in=(), raw_in=(), near_out=(), flops=0, moved=0):
    ns, ni, no = len(scalars), len(ins), len(outs)
    far_in = [i for i in range(ni) if i not in near_in and i not in raw_in]
    far_out = [i for i in range(no) if i not in near_out]

    ins = [
        a if i in near_in else pltpu.with_memory_space_constraint(a, pltpu.HBM) for i, a in enumerate(ins)
    ]

    def body(*refs):
        given, refs = refs[:ns], refs[ns:]
        sources, refs = refs[:ni], refs[ni:]
        targets, refs = refs[:no], refs[no:]
        in_bufs, refs = dict(zip(far_in, refs)), refs[len(far_in) :]
        out_bufs, refs = dict(zip(far_out, refs)), refs[len(far_out) :]
        sems, extra = refs[0], refs[1:]
        loads = [
            Load(r, in_bufs[i], sems.at[i]) if i in in_bufs else Load(r) for i, r in enumerate(sources)
        ]
        stores = [
            Store(r, out_bufs[i], sems.at[ni + i]) if i in out_bufs else Store(r)
            for i, r in enumerate(targets)
        ]
        kernel(*given, *loads, *stores, *extra)
        for load in loads:
            load.get()
        for store in stores:
            store.send()
        for store in stores:
            store.wait()

    return pl.pallas_call(
        body,
        out_shape=[
            jax.ShapeDtypeStruct(s, d) if i in near_out else pltpu.HBM(s, d) for i, (s, d) in enumerate(outs)
        ],
        in_specs=[SMEM] * ns + [VMEM if i in near_in else ANY for i in range(ni)],
        out_specs=[VMEM if i in near_out else ANY for i in range(no)],
        scratch_shapes=[pltpu.VMEM(ins[i].shape, ins[i].dtype) for i in far_in]
        + [pltpu.VMEM(*outs[i]) for i in far_out]
        + [pltpu.SemaphoreType.DMA((ni + no,))]
        + list(scratch),
        compiler_params=PARAMS,
        cost_estimate=pl.CostEstimate(flops=flops, bytes_accessed=moved, transcendentals=0),
    )(*scalars, *ins)


def on_device(imp_x, imp_hist, imp_len, owner_map, hist_x, w_in, w_out, grad_y):
    owners = lax.axis_size("dp")
    planes = lax.axis_size("mp")
    rows, depth = imp_x.shape
    width = w_in.shape[2]
    slots = owners * CAP
    events = hist_x.shape[1]
    chips = owners // 2
    place_of = lax.axis_index("dp")
    core = (place_of % 2).reshape(1)
    hist = hist_x[0]
    pairs = [(i, i ^ 1) for i in range(owners)]
    same_core = [[2 * i + c for i in range(chips)] for c in range(2)]

    def swap(a):
        return lax.ppermute(a, "dp", pairs)

    def exchange(a):
        a = a.reshape(owners, a.shape[0] // owners, width)
        a = lax.all_to_all(a, "dp", 0, 0, tiled=True)
        return a.reshape(a.shape[0] * a.shape[1], width)

    def exchange_core(a):
        a = a.reshape(chips, a.shape[0] // chips, width)
        a = lax.all_to_all(a, "dp", 0, 0, axis_index_groups=same_core, tiled=True)
        return a.reshape(a.shape[0] * a.shape[1], width)

    hist_rows = imp_hist.reshape(1, rows)
    owner_row = owner_map.reshape(1, owners)
    (send,) = call(
        pre_kernel,
        [((3 * slots, width), BF16)],
        (hist_rows, imp_len.reshape(1, rows), owner_row, imp_x, w_in, w_out, grad_y),
        near_out=(0,),
        flops=2 * rows * depth * width * 3,
        moved=1 << 20,
    )
    recv = exchange(send)
    keys, values_t, values, keys_t, key_slope, aux, place = call(
        project_kernel,
        [
            ((events, width), BF16),
            ((width, events), BF16),
            ((events, width), BF16),
            ((width, events), BF16),
            ((events, width), F32),
            ((4, rows, width), F32),
            ((slots, rows), BF16),
        ],
        (w_in, hist, hist_rows, owner_row, imp_x, w_out, grad_y),
        near_out=(0, 1),
        flops=4 * events * depth * width,
        moved=5 << 20,
    )
    heads = width // DH
    back, weights, d_keys, d_att = call(
        attend_kernel,
        [
            ((2 * slots, width), BF16),
            ((events, heads * slots), BF16),
            ((events, width), BF16),
            ((slots, width), BF16),
        ],
        (recv, keys, values_t, values, keys_t),
        scratch=[pltpu.VMEM((events, heads * slots), BF16)],
        near_in=(0, 1, 2),
        near_out=(0,),
        flops=10 * events * slots * width,
        moved=8 << 20,
    )
    back = exchange(back)
    half = depth * 2 // 2
    gkv, kv_mine, kv_other, place, aux, x_near, w_near, gy_near = call(
        history_kernel,
        [((events, 2 * width), BF16)]
        + [((half, width), BF16)] * 2
        + [(place.shape, BF16), (aux.shape, F32), (imp_x.shape, BF16)]
        + [((2,) + w_in.shape[1:], BF16), (grad_y.shape, BF16)],
        (d_att, d_keys, key_slope, weights, hist, place, aux, imp_x, w_in, grad_y),
        (core,),
        scratch=[
            pltpu.VMEM((2, half, width), BF16),
            pltpu.VMEM((events, heads * slots), BF16),
            pltpu.VMEM((events, 2 * width), BF16),
            pltpu.SemaphoreType.DMA((HISTORY_PARTS,)),
            pltpu.SemaphoreType.DMA((LATE,)),
        ],
        raw_in=(3, 5, 6, 7, 8, 9),
        near_out=(1, 2, 3, 4, 5, 6, 7),
        flops=4 * events * depth * width + 2 * events * slots * width,
        moved=10 << 20,
    )
    kv_other = swap(kv_other)
    back, kv_mine, kv_other = lax.optimization_barrier((back, kv_mine, kv_other))
    half = depth * 3 // 2
    mine, other, gx = call(
        post_kernel,
        [((half, width), BF16)] * 2 + [((rows, depth), BF16)],
        (back, place, aux, x_near, w_near, gy_near),
        (core,),
        scratch=[pltpu.VMEM((2, half, width), BF16)],
        near_in=(0, 1, 2, 3, 4, 5),
        near_out=(0, 1, 2),
        flops=2 * rows * depth * width * 5,
        moved=2 << 20,
    )
    other = swap(other)
    (summed,) = call(
        pair_kernel,
        [((chips * 40, width), BF16)],
        (kv_mine, kv_other, mine, other),
        near_in=(0, 1, 2, 3),
        near_out=(0,),
        moved=1 << 20,
    )
    plane = lax.axis_index("mp")
    share = rows // planes
    parts = []
    for step in range(1, planes):
        part = lax.dynamic_slice_in_dim(gx, (plane + step) % planes * share, share, 0)
        parts.append(lax.ppermute(part, "mp", [(i, (i + step) % planes) for i in range(planes)]))
    factor = (rows * owners) ** (-0.5)
    summed, *parts = lax.optimization_barrier((exchange_core(summed), *parts))
    total = lax.dynamic_slice_in_dim(gx, plane * share, share, 0).astype(F32)
    for part in parts:
        total = total + part.astype(F32)
    grad_x = total.astype(BF16)
    (piece,) = call(
        lambda i, o: sum_kernel(factor, i, o),
        [((chips * 40, width), BF16)],
        (summed,),
        near_in=(0,),
        near_out=(0,),
        moved=1 << 20,
    )
    mine = exchange_core(piece)
    other = swap(mine)
    grad_w_in, grad_w_out = call(
        unfold_kernel,
        [((4, depth, width), F32), ((width, depth), F32)],
        (mine, other),
        (core,),
        scratch=[pltpu.VMEM((depth, width), F32)],
        near_in=(0, 1),
        moved=3 << 20,
    )
    grad_kv = gkv.reshape(1, events, 2, width)
    return (grad_x, grad_kv, grad_w_in, grad_w_out)


def solution(mesh):
    placed = (
        P("dp", None),
        P("dp", None),
        P("dp"),
        P(),
        P("dp", None, None),
        P(None, None, "mp"),
        P("mp", None),
        P("dp", None),
    )
    return jax.shard_map(
        on_device,
        mesh=mesh,
        in_specs=placed,
        out_specs=(
            P(("dp", "mp"), None),
            P("dp", None, None, "mp"),
            P(None, None, "mp"),
            P("mp", None),
        ),
        check_vma=False,
    )
```

```python
import jax
import jax.numpy as jnp
from jax import lax
from jax.experimental import pallas as pl
from jax.experimental.pallas import tpu as pltpu
from jax.sharding import PartitionSpec as P

DH = 64
EPSILON = 1e-05
CAP = 8
BLOCK = 256
HISTORY_PARTS = 2
LATE = 5
F32 = jnp.float32
BF16 = jnp.bfloat16
ANY = pl.BlockSpec(memory_space=pl.ANY)
VMEM = pl.BlockSpec(memory_space=pltpu.VMEM)
SMEM = pl.BlockSpec(memory_space=pltpu.SMEM)
PARAMS = pltpu.CompilerParams(vmem_limit_bytes=40 * 1024 * 1024)


def nn(a, b):
    return lax.dot_general(a, b, (((1,), (0,)), ((), ())), preferred_element_type=F32)


def nt(a, b):
    return lax.dot_general(a, b, (((1,), (1,)), ((), ())), preferred_element_type=F32)


def tn(a, b):
    return lax.dot_general(a, b, (((0,), (0,)), ((), ())), preferred_element_type=F32)


def sigmoid(v):
    return 0.5 * jnp.tanh(0.5 * v) + 0.5


def silu_and_slope(v):
    s = sigmoid(v)
    return v * s, s * (1.0 + v * (1.0 - s))


def iota(shape, dim):
    return lax.broadcasted_iota(jnp.int32, shape, dim)


def spread(parts):
    count = parts[0].shape[0] // 8
    cut = [p.reshape(count, 8, p.shape[1]) for p in parts]
    joined = jnp.concatenate(cut, axis=1)
    return joined.reshape(count * 8 * len(parts), parts[0].shape[1])


def slot_table(hist, owner):
    rows, owners = hist.shape[1], owner.shape[1]
    named = jnp.where(iota((owners, rows), 0) == hist, 1.0, 0.0).astype(BF16)
    owner = jnp.broadcast_to(owner.astype(F32), (8, owners)).astype(BF16)
    target = nn(owner, named)[:1]
    hit = jnp.where(iota((owners, rows), 0).astype(F32) == target, 1.0, 0.0)
    earlier = jnp.where(iota((rows, rows), 0) < iota((rows, rows), 1), 1.0, 0.0)
    before = nn(hit.astype(BF16), earlier.astype(BF16))
    rank = jnp.sum(before * hit, axis=0, keepdims=True)
    slot = target * float(CAP) + rank
    return jnp.where(iota((owners * CAP, rows), 0).astype(F32) == slot, 1.0, 0.0).astype(BF16)


def pre_kernel(hist_in, len_in, owner_in, x_in, w_in, wo_in, gy_in, send_out, w_scr, w_sem):
    w_copy = pltpu.make_async_copy(w_in.get().at[:2], w_scr, w_sem)
    w_copy.start()
    place = slot_table(hist_in.get()[...], owner_in.get()[...])
    length = len_in.get()[...].astype(F32)
    rows = length.shape[1]
    high = jnp.floor(length * (1.0 / 256.0))
    low = length - 256.0 * high
    digits = jnp.transpose(jnp.where(iota((rows, rows), 0) == 0, high, low))
    cot = nt(gy_in.get()[...], wo_in.get()[...]).astype(BF16).astype(F32)
    x = x_in.get()[...]
    w_copy.wait()
    queries, _ = silu_and_slope(nn(x, w_scr[0]))
    gates, _ = silu_and_slope(nn(x, w_scr[1]))
    gates = gates.astype(BF16).astype(F32)
    payload = jnp.concatenate(
        [queries.astype(BF16), (cot * gates).astype(BF16), digits.astype(BF16)], axis=1
    )
    packed = nn(place, payload)
    width = queries.shape[1]
    send_out.buffer[...] = spread(
        [packed[:, :width], packed[:, width : 2 * width], packed[:, 2 * width :]]
    ).astype(BF16)


def project_kernel(
    w_in, ev_in, hist_in, owner_in, x_in, wo_in, gy_in,
    k_out, vt_out, v_out, kt_out, slope_out, aux_out, place_out,
):
    w_ref, ev_ref = w_in.get(), ev_in.get()
    count = ev_ref.shape[0] // 512
    for b in range(count):
        at = pl.ds(b * 512, 512)
        ev = ev_ref[at, :]
        keys, slope = silu_and_slope(nn(ev, w_ref[2]))
        values = nn(ev, w_ref[3])
        k_out.buffer[at, :] = keys.astype(BF16)
        v_out.buffer[at, :] = values.astype(BF16)
        slope_out.buffer[at, :] = slope.astype(BF16)
        kt_out.buffer[:, at] = jnp.transpose(keys.astype(BF16))
        vt_out.buffer[:, at] = jnp.transpose(values.astype(BF16))
    for out in (k_out, v_out, kt_out, vt_out, slope_out):
        out.send()
    place_out.buffer[...] = slot_table(hist_in.get()[...], owner_in.get()[...])
    x = x_in.get()[...]
    _, slope_q = silu_and_slope(nn(x, w_ref[0]))
    gates, slope_g = silu_and_slope(nn(x, w_ref[1]))
    aux_out.buffer[0] = slope_q
    aux_out.buffer[1] = slope_g
    aux_out.buffer[2] = gates.astype(BF16).astype(F32)
    aux_out.buffer[3] = nt(gy_in.get()[...], wo_in.get()[...]).astype(BF16).astype(F32)


def attend_kernel(
    recv_in, k_in, vt_in, v_in, kt_in,
    back_out, weights_out, d_keys_out, d_att_out,
    s_scr,
):
    recv_ref, k_ref, vt_ref = recv_in.get(), k_in.get(), vt_in.get()
    slots, width = recv_ref.shape[0] // 3, recv_ref.shape[1]
    heads = width // DH
    events = k_ref.shape[0]
    got = recv_ref[...].astype(F32).reshape(slots // CAP, 3 * CAP, width)
    q = got[:, :CAP].reshape(slots, width).astype(BF16)
    dn = got[:, CAP : 2 * CAP].reshape(slots, width).astype(BF16)
    digits = got[:, 2 * CAP :].reshape(slots, width).astype(BF16)
    digits = jnp.transpose(digits).astype(F32)
    length = digits[0:1] * 256.0 + digits[1:2]
    head_row = iota((width, slots), 0) // DH
    head_col = iota((slots, width), 1) // DH
    qt_half = (jnp.transpose(q).astype(F32) * (0.5 * DH ** (-0.5))).astype(BF16)
    zero = jnp.zeros((), BF16)
    qt_of = [jnp.where(head_row == h, qt_half, zero) for h in range(heads)]
    cols_of = [slice(h * slots, (h + 1) * slots) for h in range(heads)]
    mine_of = [slice(h * DH, (h + 1) * DH) for h in range(heads)]
    for start in range(0, events, BLOCK):
        at = pl.ds(start, BLOCK)
        visible = (iota((BLOCK, slots), 0) + start).astype(F32) < length
        for h in range(heads):
            half = nn(k_ref[at, :], qt_of[h])
            twice = jnp.where(visible, jnp.tanh(half) + 1.0, 0.0)
            weights = half * twice
            s_scr[at, cols_of[h]] = (twice + weights * (2.0 - twice)).astype(BF16)
            weights_out.buffer[at, cols_of[h]] = weights.astype(BF16)
        weights_out.send_part((at,))
    att = [nn(vt_ref[mine_of[h], :], weights_out.buffer[:, cols_of[h]]) for h in range(heads)]
    att = jnp.concatenate(att, axis=0).reshape(heads, DH, slots)
    inverse = lax.rsqrt(jnp.mean(att * att, axis=1, keepdims=True) + EPSILON)
    normed = att * inverse
    dnt = jnp.transpose(dn).astype(F32).reshape(heads, DH, slots)
    d_att = inverse * (dnt - normed * jnp.mean(dnt * normed, axis=1, keepdims=True))
    d_att = d_att.reshape(width, slots).astype(BF16)
    d_att_out.buffer[...] = jnp.transpose(d_att)
    d_att_out.send()
    normed = jnp.transpose(normed.reshape(width, slots).astype(BF16)).astype(F32)
    dt_of = [jnp.where(head_row == h, d_att, zero) for h in range(heads)]
    q_of = jnp.concatenate([jnp.where(head_col == h, q, zero) for h in range(heads)], axis=0)
    v_ref, kt_ref = v_in.get(), kt_in.get()
    for start in range(0, events, BLOCK):
        at = pl.ds(start, BLOCK)
        for h in range(heads):
            ds = nn(v_ref[at, :], dt_of[h]) * s_scr[at, cols_of[h]].astype(F32)
            s_scr[at, cols_of[h]] = ds.astype(BF16)
        d_keys = nn(s_scr[at, :], q_of) * (0.5 * DH ** (-0.5))
        d_keys_out.buffer[at, :] = d_keys.astype(BF16)
        d_keys_out.send_part((at,))
    d_query = [nn(kt_ref[mine_of[h], :], s_scr[:, cols_of[h]]) for h in range(heads)]
    d_query = (jnp.concatenate(d_query, axis=0) * (0.5 * DH ** (-0.5))).astype(BF16)
    back_out.buffer[...] = spread([jnp.transpose(d_query).astype(F32), normed]).astype(BF16)


def history_kernel(
    core_ref, d_att_in, d_keys_in, slope_in, weights_in, ev_in, *rest
):
    late, rest = rest[:LATE], rest[LATE:]
    gkv_out, mine_out, other_out, rest = rest[0], rest[1], rest[2], rest[3:]
    kept, (scr, w_scr, term_scr, ev_scr, sems, ev_sem, late_sems) = rest[:LATE], rest[LATE:]
    events = w_scr.shape[0]
    step = events // HISTORY_PARTS
    parts = [pl.ds(b * step, step) for b in range(HISTORY_PARTS)]
    copies = [
        pltpu.make_async_copy(weights_in.get().at[at], w_scr.at[at], sems.at[b])
        for b, at in enumerate(parts)
    ]
    for copy in copies:
        copy.start()
    ev_copy = pltpu.make_async_copy(ev_in.get(), ev_scr, ev_sem)
    ev_copy.start()
    moves = [
        pltpu.make_async_copy(src.get().at[: dst.buffer.shape[0]], dst.buffer, late_sems.at[i])
        for i, (src, dst) in enumerate(zip(late, kept))
    ]
    for move in moves:
        move.start()
    d_att = d_att_in.get()[...]
    slots, width = d_att.shape
    heads = width // DH
    head_col = iota((slots, width), 1) // DH
    zero = jnp.zeros((), BF16)
    d_of = jnp.concatenate([jnp.where(head_col == h, d_att, zero) for h in range(heads)], axis=0)
    d_keys_ref, slope_ref, gkv_ref = d_keys_in.get(), slope_in.get(), gkv_out.buffer
    for at, copy in zip(parts, copies):
        d_keys = d_keys_ref[at, :]
        gkv_ref[at, :width] = d_keys
        term_scr[at, :width] = (d_keys.astype(F32) * slope_ref[at, :].astype(F32)).astype(BF16)
        copy.wait()
        d_values = nn(w_scr[at, :], d_of).astype(BF16)
        gkv_ref[at, width:] = d_values
        gkv_out.send_part((at,))
        term_scr[at, width:] = d_values
    ev_copy.wait()
    both = jnp.transpose(tn(term_scr[...], ev_scr[...]))
    rows = spread([both[:, :width], both[:, width:]]).astype(BF16)
    split_halves(core_ref[0], rows, scr, mine_out, other_out)
    for move in moves:
        move.wait()


def split_halves(core, rows, scr, mine_out, other_out):
    half = rows.shape[0] // 2
    scr[0] = rows[:half]
    scr[1] = rows[half:]
    other_out.buffer[...] = scr[1 - core]
    other_out.send()
    mine_out.buffer[...] = scr[core]


def post_kernel(
    core_ref, back_in, kv_mine_in, kv_other_in, place_in, aux_in, x_in, w_in, gy_in,
    mine_out, other_out, gx_out, scr,
):
    place = place_in.get()[...]
    back_ref, aux_ref, w_ref = back_in.get(), aux_in.get(), w_in.get()
    slots = place.shape[0]
    width = back_ref.shape[1]
    got = back_ref[...].astype(F32).reshape(slots // CAP, 2 * CAP, width)
    d_query = got[:, :CAP].reshape(slots, width).astype(BF16)
    normed = got[:, CAP:].reshape(slots, width).astype(BF16)
    both = tn(place, jnp.concatenate([d_query, normed], axis=1))
    d_query = both[:, :width]
    normed = both[:, width:]
    gates = aux_ref[2]
    gated = (normed * gates).astype(BF16)
    d_gate = (aux_ref[3] * normed).astype(BF16).astype(F32)
    q_term = (d_query * aux_ref[0]).astype(BF16)
    g_term = (d_gate * aux_ref[1]).astype(BF16)
    gx_out.buffer[...] = (nt(q_term, w_ref[0]) + nt(g_term, w_ref[1])).astype(BF16)
    gx_out.send()
    x = x_in.get()[...]
    gq = tn(x, q_term)
    gg = tn(x, g_term)
    go = tn(gated, gy_in.get()[...])
    go = jnp.concatenate([go[:, i * width : (i + 1) * width] for i in range(go.shape[1] // width)], axis=0)
    out = spread([gq, gg, go])
    half = out.shape[0] // 2
    scr[0] = out[:half]
    scr[1] = out[half:]
    core = core_ref[0]
    other_out.buffer[...] = scr[1 - core].astype(BF16)
    chunks = half // 24
    pair = kv_mine_in.get()[...].astype(F32) + kv_other_in.get()[...].astype(F32)
    joined = jnp.concatenate(
        [pair.reshape(chunks, 16, width), scr[core].reshape(chunks, 24, width)], axis=1
    )
    mine_out.buffer[...] = joined.reshape(chunks * 40, width).astype(BF16)


def pair_kernel(mine_in, other_in, out):
    width = other_in.buffer.shape[1]
    other = other_in.get()[...].astype(F32)
    chunks = other.shape[0] // 24
    other = other.reshape(chunks, 24, width)
    other = jnp.concatenate([jnp.zeros((chunks, 16, width), F32), other], axis=1)
    total = mine_in.get()[...].astype(F32) + other.reshape(chunks * 40, width)
    out.buffer[...] = total.astype(BF16)


def sum_kernel(factor, rows_in, out):
    got = rows_in.get()[...]
    chunks = got.shape[0] // 40
    total = jnp.sum(got.astype(F32).reshape(chunks, 40, got.shape[1]), axis=0)
    total = total * factor
    shape = out.buffer.shape
    out.buffer[...] = jnp.broadcast_to(total[None], (chunks, 40, shape[1])).reshape(shape).astype(BF16)


def unfold_kernel(which_ref, source_ref, *refs):
    win_ref, wout_ref, win_scr, wout_scr, sems = refs[-5:]
    got = source_ref[...].astype(F32)
    width = got.shape[1]
    chunks = got.shape[0] // 40
    size = chunks * 8
    got = got.reshape(chunks, 5, 8, width)
    at = pl.ds(pl.multiple_of(which_ref[0] * size, size), size)
    copies = []
    for place, index in enumerate((2, 3, 0, 1)):
        win_scr[index] = got[:, place].reshape(size, width)
        copies.append(pltpu.make_async_copy(win_scr.at[index], win_ref.at[index, at], sems.at[place]))
        copies[-1].start()
    last = got[:, 4].reshape(size, width)
    rows = wout_scr.shape[0]
    for i in range(size // rows):
        wout_scr[:, i * width : (i + 1) * width] = last[i * rows : (i + 1) * rows]
    copies.append(pltpu.make_async_copy(wout_scr, wout_ref.at[:, at], sems.at[4]))
    copies[-1].start()
    for copy in copies:
        copy.wait()


def unfold(which, source, depth, filled=()):
    width = source.shape[1]
    return pl.pallas_call(
        unfold_kernel,
        out_shape=[pltpu.HBM((4, depth, width), F32), pltpu.HBM((width, depth), F32)],
        in_specs=[SMEM, VMEM] + [ANY] * len(filled),
        out_specs=[ANY, ANY],
        scratch_shapes=[
            pltpu.VMEM((4, depth // 2, width), F32),
            pltpu.VMEM((width, depth // 2), F32),
            pltpu.SemaphoreType.DMA((5,)),
        ],
        input_output_aliases={2 + i: i for i in range(len(filled))},
        compiler_params=PARAMS,
        cost_estimate=pl.CostEstimate(flops=0, bytes_accessed=1 << 20, transcendentals=0),
    )(which, source, *filled)


class Load:
    def __init__(self, source, buffer=None, sem=None):
        self.buffer, self.copy = source, None
        if buffer is not None:
            self.buffer = buffer
            self.copy = pltpu.make_async_copy(source, buffer, sem)
            self.copy.start()

    def get(self):
        if self.copy is not None:
            self.copy.wait()
            self.copy = None
        return self.buffer


class Store:
    def __init__(self, target, buffer=None, sem=None):
        self.buffer, self.copy, self.started = target, None, False
        self.target, self.sem = target, sem
        if buffer is not None:
            self.buffer = buffer
            self.copy = pltpu.make_async_copy(buffer, target, sem)

    def send(self):
        if self.copy is not None and not self.started:
            self.copy.start()
            self.started = True

    def send_part(self, at):
        pltpu.make_async_copy(self.buffer.at[at], self.target.at[at], self.sem).start()
        self.started = True

    def wait(self):
        if self.copy is not None:
            self.copy.wait()


def call(kernel, outs, ins, scalars=(), scratch=(), near_in=(), raw_in=(), near_out=(), flops=0, moved=0):
    ns, ni, no = len(scalars), len(ins), len(outs)
    far_in = [i for i in range(ni) if i not in near_in and i not in raw_in]
    far_out = [i for i in range(no) if i not in near_out]

    ins = [
        a if i in near_in else pltpu.with_memory_space_constraint(a, pltpu.HBM) for i, a in enumerate(ins)
    ]

    def body(*refs):
        given, refs = refs[:ns], refs[ns:]
        sources, refs = refs[:ni], refs[ni:]
        targets, refs = refs[:no], refs[no:]
        in_bufs, refs = dict(zip(far_in, refs)), refs[len(far_in) :]
        out_bufs, refs = dict(zip(far_out, refs)), refs[len(far_out) :]
        sems, extra = refs[0], refs[1:]
        loads = [
            Load(r, in_bufs[i], sems.at[i]) if i in in_bufs else Load(r) for i, r in enumerate(sources)
        ]
        stores = [
            Store(r, out_bufs[i], sems.at[ni + i]) if i in out_bufs else Store(r)
            for i, r in enumerate(targets)
        ]
        kernel(*given, *loads, *stores, *extra)
        for load in loads:
            load.get()
        for store in stores:
            store.send()
        for store in stores:
            store.wait()

    return pl.pallas_call(
        body,
        out_shape=[
            jax.ShapeDtypeStruct(s, d) if i in near_out else pltpu.HBM(s, d) for i, (s, d) in enumerate(outs)
        ],
        in_specs=[SMEM] * ns + [VMEM if i in near_in else ANY for i in range(ni)],
        out_specs=[VMEM if i in near_out else ANY for i in range(no)],
        scratch_shapes=[pltpu.VMEM(ins[i].shape, ins[i].dtype) for i in far_in]
        + [pltpu.VMEM(*outs[i]) for i in far_out]
        + [pltpu.SemaphoreType.DMA((ni + no,))]
        + list(scratch),
        compiler_params=PARAMS,
        cost_estimate=pl.CostEstimate(flops=flops, bytes_accessed=moved, transcendentals=0),
    )(*scalars, *ins)


def on_device(imp_x, imp_hist, imp_len, owner_map, hist_x, w_in, w_out, grad_y):
    owners = lax.axis_size("dp")
    planes = lax.axis_size("mp")
    rows, depth = imp_x.shape
    width = w_in.shape[2]
    slots = owners * CAP
    events = hist_x.shape[1]
    chips = owners // 2
    place_of = lax.axis_index("dp")
    core = (place_of % 2).reshape(1)
    hist = hist_x[0]
    pairs = [(i, i ^ 1) for i in range(owners)]
    same_core = [[2 * i + c for i in range(chips)] for c in range(2)]

    def swap(a):
        return lax.ppermute(a, "dp", pairs)

    def exchange(a):
        a = a.reshape(owners, a.shape[0] // owners, width)
        a = lax.all_to_all(a, "dp", 0, 0, tiled=True)
        return a.reshape(a.shape[0] * a.shape[1], width)

    def exchange_core(a):
        a = a.reshape(chips, a.shape[0] // chips, width)
        a = lax.all_to_all(a, "dp", 0, 0, axis_index_groups=same_core, tiled=True)
        return a.reshape(a.shape[0] * a.shape[1], width)

    hist_rows = imp_hist.reshape(1, rows)
    owner_row = owner_map.reshape(1, owners)
    (send,) = call(
        pre_kernel,
        [((3 * slots, width), BF16)],
        (hist_rows, imp_len.reshape(1, rows), owner_row, imp_x, w_in, w_out, grad_y),
        scratch=[pltpu.VMEM((2,) + w_in.shape[1:], BF16), pltpu.SemaphoreType.DMA(())],
        raw_in=(4,),
        near_out=(0,),
        flops=2 * rows * depth * width * 3,
        moved=1 << 20,
    )
    recv = exchange(send)
    keys, values_t, values, keys_t, key_slope, aux, place = call(
        project_kernel,
        [
            ((events, width), BF16),
            ((width, events), BF16),
            ((events, width), BF16),
            ((width, events), BF16),
            ((events, width), BF16),
            ((4, rows, width), F32),
            ((slots, rows), BF16),
        ],
        (w_in, hist, hist_rows, owner_row, imp_x, w_out, grad_y),
        near_out=(0, 1),
        flops=4 * events * depth * width,
        moved=5 << 20,
    )
    heads = width // DH
    back, weights, d_keys, d_att = call(
        attend_kernel,
        [
            ((2 * slots, width), BF16),
            ((events, heads * slots), BF16),
            ((events, width), BF16),
            ((slots, width), BF16),
        ],
        (recv, keys, values_t, values, keys_t),
        scratch=[pltpu.VMEM((events, heads * slots), BF16)],
        near_in=(0, 1, 2),
        near_out=(0,),
        flops=10 * events * slots * width,
        moved=8 << 20,
    )
    back = exchange(back)
    half = depth * 2 // 2
    gkv, kv_mine, kv_other, place, aux, x_near, w_near, gy_near = call(
        history_kernel,
        [((events, 2 * width), BF16)]
        + [((half, width), BF16)] * 2
        + [(place.shape, BF16), (aux.shape, F32), (imp_x.shape, BF16)]
        + [((2,) + w_in.shape[1:], BF16), (grad_y.shape, BF16)],
        (d_att, d_keys, key_slope, weights, hist, place, aux, imp_x, w_in, grad_y),
        (core,),
        scratch=[
            pltpu.VMEM((2, half, width), BF16),
            pltpu.VMEM((events, heads * slots), BF16),
            pltpu.VMEM((events, 2 * width), BF16),
            pltpu.VMEM((events, depth), BF16),
            pltpu.SemaphoreType.DMA((HISTORY_PARTS,)),
            pltpu.SemaphoreType.DMA(()),
            pltpu.SemaphoreType.DMA((LATE,)),
        ],
        raw_in=(3, 4, 5, 6, 7, 8, 9),
        near_out=(1, 2, 3, 4, 5, 6, 7),
        flops=4 * events * depth * width + 2 * events * slots * width,
        moved=10 << 20,
    )
    kv_other = swap(kv_other)
    back, kv_mine, kv_other = lax.optimization_barrier((back, kv_mine, kv_other))
    half = depth * 3 // 2
    mine, other, gx = call(
        post_kernel,
        [((chips * 40, width), BF16), ((half, width), BF16), ((rows, depth), BF16)],
        (back, kv_mine, kv_other, place, aux, x_near, w_near, gy_near),
        (core,),
        scratch=[pltpu.VMEM((2, half, width), F32)],
        near_in=(0, 1, 2, 3, 4, 5, 6, 7),
        near_out=(0, 1, 2),
        flops=2 * rows * depth * width * 5,
        moved=2 << 20,
    )
    other = swap(other)
    (summed,) = call(
        pair_kernel,
        [((chips * 40, width), BF16)],
        (mine, other),
        near_in=(0, 1),
        near_out=(0,),
        moved=1 << 20,
    )
    plane = lax.axis_index("mp")
    share = rows // planes
    parts = []
    for step in range(1, planes):
        part = lax.dynamic_slice_in_dim(gx, (plane + step) % planes * share, share, 0)
        parts.append(lax.ppermute(part, "mp", [(i, (i + step) % planes) for i in range(planes)]))
    factor = (rows * owners) ** (-0.5)
    grad_kv = gkv.reshape(1, events, 2, width)
    summed, grad_kv, *parts = lax.optimization_barrier((exchange_core(summed), grad_kv, *parts))
    total = lax.dynamic_slice_in_dim(gx, plane * share, share, 0).astype(F32)
    for part in parts:
        total = total + part.astype(F32)
    grad_x = total.astype(BF16)
    (piece,) = call(
        lambda i, o: sum_kernel(factor, i, o),
        [((chips * 40, width), BF16)],
        (summed,),
        near_in=(0,),
        near_out=(0,),
        moved=1 << 20,
    )
    piece, grad_x = lax.optimization_barrier((piece, grad_x))
    mine = exchange_core(piece)
    other = swap(mine)
    filled = unfold(core, mine, depth)
    grad_w_in, grad_w_out = unfold(1 - core, other, depth, filled)
    return (grad_x, grad_kv, grad_w_in, grad_w_out)


def solution(mesh):
    placed = (
        P("dp", None),
        P("dp", None),
        P("dp"),
        P(),
        P("dp", None, None),
        P(None, None, "mp"),
        P("mp", None),
        P("dp", None),
    )
    return jax.shard_map(
        on_device,
        mesh=mesh,
        in_specs=placed,
        out_specs=(
            P(("dp", "mp"), None),
            P("dp", None, None, "mp"),
            P(None, None, "mp"),
            P("mp", None),
        ),
        check_vma=False,
    )
```

```python
import functools

import jax
import jax.numpy as jnp
from jax import lax
from jax.experimental import pallas as pl
from jax.experimental.pallas import tpu as pltpu
from jax.sharding import PartitionSpec as P

DH = 64
EPSILON = 1e-05
CAP = 8
BLOCK = 256
HISTORY_PARTS = 2
LATE = 5
F32 = jnp.float32
BF16 = jnp.bfloat16
ANY = pl.BlockSpec(memory_space=pl.ANY)
VMEM = pl.BlockSpec(memory_space=pltpu.VMEM)
SMEM = pl.BlockSpec(memory_space=pltpu.SMEM)
PARAMS = pltpu.CompilerParams(vmem_limit_bytes=40 * 1024 * 1024)


def nn(a, b):
    return lax.dot_general(a, b, (((1,), (0,)), ((), ())), preferred_element_type=F32)


def nt(a, b):
    return lax.dot_general(a, b, (((1,), (1,)), ((), ())), preferred_element_type=F32)


def tn(a, b):
    return lax.dot_general(a, b, (((0,), (0,)), ((), ())), preferred_element_type=F32)


def sigmoid(v):
    return 0.5 * jnp.tanh(0.5 * v) + 0.5


def silu_and_slope(v):
    s = sigmoid(v)
    return v * s, s * (1.0 + v * (1.0 - s))


def iota(shape, dim):
    return lax.broadcasted_iota(jnp.int32, shape, dim)


def spread(parts):
    count = parts[0].shape[0] // 8
    cut = [p.reshape(count, 8, p.shape[1]) for p in parts]
    joined = jnp.concatenate(cut, axis=1)
    return joined.reshape(count * 8 * len(parts), parts[0].shape[1])


def slot_table(hist, owner):
    rows, owners = hist.shape[1], owner.shape[1]
    named = jnp.where(iota((owners, rows), 0) == hist, 1.0, 0.0).astype(BF16)
    owner = jnp.broadcast_to(owner.astype(F32), (8, owners)).astype(BF16)
    target = nn(owner, named)[:1]
    hit = jnp.where(iota((owners, rows), 0).astype(F32) == target, 1.0, 0.0)
    earlier = jnp.where(iota((rows, rows), 0) < iota((rows, rows), 1), 1.0, 0.0)
    before = nn(hit.astype(BF16), earlier.astype(BF16))
    rank = jnp.sum(before * hit, axis=0, keepdims=True)
    slot = target * float(CAP) + rank
    return jnp.where(iota((owners * CAP, rows), 0).astype(F32) == slot, 1.0, 0.0).astype(BF16)


def pre_kernel(hist_in, len_in, owner_in, x_in, w_in, wo_in, gy_in, send_out, w_scr, w_sem):
    w_copy = pltpu.make_async_copy(w_in.get().at[:2], w_scr, w_sem)
    w_copy.start()
    place = slot_table(hist_in.get()[...], owner_in.get()[...])
    length = len_in.get()[...].astype(F32)
    rows = length.shape[1]
    high = jnp.floor(length * (1.0 / 256.0))
    low = length - 256.0 * high
    digits = jnp.transpose(jnp.where(iota((rows, rows), 0) == 0, high, low))
    cot = nt(gy_in.get()[...], wo_in.get()[...]).astype(BF16).astype(F32)
    x = x_in.get()[...]
    w_copy.wait()
    queries, _ = silu_and_slope(nn(x, w_scr[0]))
    gates, _ = silu_and_slope(nn(x, w_scr[1]))
    gates = gates.astype(BF16).astype(F32)
    payload = jnp.concatenate(
        [queries.astype(BF16), (cot * gates).astype(BF16), digits.astype(BF16)], axis=1
    )
    packed = nn(place, payload)
    width = queries.shape[1]
    send_out.buffer[...] = spread(
        [packed[:, :width], packed[:, width : 2 * width], packed[:, 2 * width :]]
    ).astype(BF16)


def project_kernel(
    w_in, ev_in, hist_in, owner_in, x_in, wo_in, gy_in,
    k_out, vt_out, v_out, kt_out, slope_out, aux_out, place_out,
):
    w_ref, ev_ref = w_in.get(), ev_in.get()
    count = ev_ref.shape[0] // 512
    for b in range(count):
        at = pl.ds(b * 512, 512)
        ev = ev_ref[at, :]
        keys, slope = silu_and_slope(nn(ev, w_ref[2]))
        values = nn(ev, w_ref[3])
        k_out.buffer[at, :] = keys.astype(BF16)
        v_out.buffer[at, :] = values.astype(BF16)
        slope_out.buffer[at, :] = slope.astype(BF16)
        kt_out.buffer[:, at] = jnp.transpose(keys.astype(BF16))
        vt_out.buffer[:, at] = jnp.transpose(values.astype(BF16))
    for out in (k_out, v_out, kt_out, vt_out, slope_out):
        out.send()
    place_out.buffer[...] = slot_table(hist_in.get()[...], owner_in.get()[...])
    x = x_in.get()[...]
    _, slope_q = silu_and_slope(nn(x, w_ref[0]))
    gates, slope_g = silu_and_slope(nn(x, w_ref[1]))
    aux_out.buffer[0] = slope_q
    aux_out.buffer[1] = slope_g
    aux_out.buffer[2] = gates.astype(BF16).astype(F32)
    aux_out.buffer[3] = nt(gy_in.get()[...], wo_in.get()[...]).astype(BF16).astype(F32)


def attend_kernel(
    recv_in, k_in, vt_in, v_in, kt_in,
    back_out, weights_out, d_keys_out, d_att_out,
    s_scr,
):
    recv_ref, k_ref, vt_ref = recv_in.get(), k_in.get(), vt_in.get()
    slots, width = recv_ref.shape[0] // 3, recv_ref.shape[1]
    heads = width // DH
    events = k_ref.shape[0]
    got = recv_ref[...].astype(F32).reshape(slots // CAP, 3 * CAP, width)
    q = got[:, :CAP].reshape(slots, width).astype(BF16)
    dn = got[:, CAP : 2 * CAP].reshape(slots, width).astype(BF16)
    digits = got[:, 2 * CAP :].reshape(slots, width).astype(BF16)
    digits = jnp.transpose(digits).astype(F32)
    length = digits[0:1] * 256.0 + digits[1:2]
    head_row = iota((width, slots), 0) // DH
    head_col = iota((slots, width), 1) // DH
    qt_half = (jnp.transpose(q).astype(F32) * (0.5 * DH ** (-0.5))).astype(BF16)
    zero = jnp.zeros((), BF16)
    qt_of = [jnp.where(head_row == h, qt_half, zero) for h in range(heads)]
    cols_of = [slice(h * slots, (h + 1) * slots) for h in range(heads)]
    mine_of = [slice(h * DH, (h + 1) * DH) for h in range(heads)]
    for start in range(0, events, BLOCK):
        at = pl.ds(start, BLOCK)
        visible = (iota((BLOCK, slots), 0) + start).astype(F32) < length
        for h in range(heads):
            half = nn(k_ref[at, :], qt_of[h])
            twice = jnp.where(visible, jnp.tanh(half) + 1.0, 0.0)
            weights = half * twice
            s_scr[at, cols_of[h]] = (twice + weights * (2.0 - twice)).astype(BF16)
            weights_out.buffer[at, cols_of[h]] = weights.astype(BF16)
        weights_out.send_part((at,))
    att = [nn(vt_ref[mine_of[h], :], weights_out.buffer[:, cols_of[h]]) for h in range(heads)]
    att = jnp.concatenate(att, axis=0).reshape(heads, DH, slots)
    inverse = lax.rsqrt(jnp.mean(att * att, axis=1, keepdims=True) + EPSILON)
    normed = att * inverse
    dnt = jnp.transpose(dn).astype(F32).reshape(heads, DH, slots)
    d_att = inverse * (dnt - normed * jnp.mean(dnt * normed, axis=1, keepdims=True))
    d_att = d_att.reshape(width, slots).astype(BF16)
    d_att_out.buffer[...] = jnp.transpose(d_att)
    d_att_out.send()
    normed = jnp.transpose(normed.reshape(width, slots).astype(BF16)).astype(F32)
    dt_of = [jnp.where(head_row == h, d_att, zero) for h in range(heads)]
    q_of = jnp.concatenate([jnp.where(head_col == h, q, zero) for h in range(heads)], axis=0)
    v_ref, kt_ref = v_in.get(), kt_in.get()
    for start in range(0, events, BLOCK):
        at = pl.ds(start, BLOCK)
        for h in range(heads):
            ds = nn(v_ref[at, :], dt_of[h]) * s_scr[at, cols_of[h]].astype(F32)
            s_scr[at, cols_of[h]] = ds.astype(BF16)
        d_keys = nn(s_scr[at, :], q_of) * (0.5 * DH ** (-0.5))
        d_keys_out.buffer[at, :] = d_keys.astype(BF16)
        d_keys_out.send_part((at,))
    d_query = [nn(kt_ref[mine_of[h], :], s_scr[:, cols_of[h]]) for h in range(heads)]
    d_query = (jnp.concatenate(d_query, axis=0) * (0.5 * DH ** (-0.5))).astype(BF16)
    back_out.buffer[...] = spread([jnp.transpose(d_query).astype(F32), normed]).astype(BF16)


def history_kernel(
    core_ref, d_att_in, d_keys_in, slope_in, weights_in, ev_in, *rest
):
    late, rest = rest[:LATE], rest[LATE:]
    gkv_out, mine_out, other_out, rest = rest[0], rest[1], rest[2], rest[3:]
    kept, (scr, w_scr, term_scr, ev_scr, sems, ev_sem, late_sems) = rest[:LATE], rest[LATE:]
    events = w_scr.shape[0]
    step = events // HISTORY_PARTS
    parts = [pl.ds(b * step, step) for b in range(HISTORY_PARTS)]
    copies = [
        pltpu.make_async_copy(weights_in.get().at[at], w_scr.at[at], sems.at[b])
        for b, at in enumerate(parts)
    ]
    for copy in copies:
        copy.start()
    ev_copy = pltpu.make_async_copy(ev_in.get(), ev_scr, ev_sem)
    ev_copy.start()
    moves = [
        pltpu.make_async_copy(src.get().at[: dst.buffer.shape[0]], dst.buffer, late_sems.at[i])
        for i, (src, dst) in enumerate(zip(late, kept))
    ]
    for move in moves:
        move.start()
    d_att = d_att_in.get()[...]
    slots, width = d_att.shape
    heads = width // DH
    head_col = iota((slots, width), 1) // DH
    zero = jnp.zeros((), BF16)
    d_of = jnp.concatenate([jnp.where(head_col == h, d_att, zero) for h in range(heads)], axis=0)
    d_keys_ref, slope_ref, gkv_ref = d_keys_in.get(), slope_in.get(), gkv_out.buffer
    for at, copy in zip(parts, copies):
        d_keys = d_keys_ref[at, :]
        gkv_ref[at, :width] = d_keys
        term_scr[at, :width] = (d_keys.astype(F32) * slope_ref[at, :].astype(F32)).astype(BF16)
        copy.wait()
        d_values = nn(w_scr[at, :], d_of).astype(BF16)
        gkv_ref[at, width:] = d_values
        gkv_out.send_part((at,))
        term_scr[at, width:] = d_values
    ev_copy.wait()
    both = jnp.transpose(tn(term_scr[...], ev_scr[...]))
    rows = spread([both[:, :width], both[:, width:]]).astype(BF16)
    split_halves(core_ref[0], rows, scr, mine_out, other_out)
    for move in moves:
        move.wait()


def split_halves(core, rows, scr, mine_out, other_out):
    half = rows.shape[0] // 2
    scr[0] = rows[:half]
    scr[1] = rows[half:]
    other_out.buffer[...] = scr[1 - core]
    other_out.send()
    mine_out.buffer[...] = scr[core]


def post_kernel(
    core_ref, back_in, kv_mine_in, kv_other_in, place_in, aux_in, x_in, w_in, gy_in,
    mine_out, other_out, gx_out, scr,
):
    place = place_in.get()[...]
    back_ref, aux_ref, w_ref = back_in.get(), aux_in.get(), w_in.get()
    slots = place.shape[0]
    width = back_ref.shape[1]
    got = back_ref[...].astype(F32).reshape(slots // CAP, 2 * CAP, width)
    d_query = got[:, :CAP].reshape(slots, width).astype(BF16)
    normed = got[:, CAP:].reshape(slots, width).astype(BF16)
    both = tn(place, jnp.concatenate([d_query, normed], axis=1))
    d_query = both[:, :width]
    normed = both[:, width:]
    gates = aux_ref[2]
    gated = (normed * gates).astype(BF16)
    d_gate = (aux_ref[3] * normed).astype(BF16).astype(F32)
    q_term = (d_query * aux_ref[0]).astype(BF16)
    g_term = (d_gate * aux_ref[1]).astype(BF16)
    gx_out.buffer[...] = (nt(q_term, w_ref[0]) + nt(g_term, w_ref[1])).astype(BF16)
    gx_out.send()
    x = x_in.get()[...]
    gq = tn(x, q_term)
    gg = tn(x, g_term)
    go = tn(gated, gy_in.get()[...])
    go = jnp.concatenate([go[:, i * width : (i + 1) * width] for i in range(go.shape[1] // width)], axis=0)
    out = spread([gq, gg, go])
    half = out.shape[0] // 2
    scr[0] = out[:half]
    scr[1] = out[half:]
    core = core_ref[0]
    for kv_in, which, result in ((kv_other_in, 1 - core, other_out), (kv_mine_in, core, mine_out)):
        chunks = half // 24
        kv = kv_in.get()[...].astype(F32).reshape(chunks, 16, width)
        joined = jnp.concatenate([kv, scr[which].reshape(chunks, 24, width)], axis=1)
        result.buffer[...] = joined.reshape(chunks * 40, width).astype(BF16)


def pair_kernel(mine_in, other_in, out):
    out.buffer[...] = (mine_in.get()[...].astype(F32) + other_in.get()[...].astype(F32)).astype(BF16)


def sum_kernel(factor, rows_in, out):
    got = rows_in.get()[...]
    chunks = got.shape[0] // 40
    total = jnp.sum(got.astype(F32).reshape(chunks, 40, got.shape[1]), axis=0)
    total = total * factor
    shape = out.buffer.shape
    out.buffer[...] = jnp.broadcast_to(total[None], (chunks, 40, shape[1])).reshape(shape).astype(BF16)


def unfold_kernel(shares, which_ref, source_ref, *refs):
    if shares:
        share_refs, refs = refs[:shares], refs[shares:]
        gx_ref, win_ref, wout_ref, win_scr, wout_scr, sems, share_scr, gx_scr, gx_sems = refs
        loads = [
            pltpu.make_async_copy(share, share_scr.at[i], gx_sems.at[i]) for i, share in enumerate(share_refs)
        ]
        for load in loads:
            load.start()
    else:
        win_ref, wout_ref, win_scr, wout_scr, sems = refs[2:]
    got = source_ref[...].astype(F32)
    width = got.shape[1]
    chunks = got.shape[0] // 40
    size = chunks * 8
    got = got.reshape(chunks, 5, 8, width)
    at = pl.ds(pl.multiple_of(which_ref[0] * size, size), size)
    copies = []
    for place, index in enumerate((2, 3, 0, 1)):
        win_scr[index] = got[:, place].reshape(size, width)
        copies.append(pltpu.make_async_copy(win_scr.at[index], win_ref.at[index, at], sems.at[place]))
        copies[-1].start()
    last = got[:, 4].reshape(size, width)
    rows = wout_scr.shape[0]
    for i in range(size // rows):
        wout_scr[:, i * width : (i + 1) * width] = last[i * rows : (i + 1) * rows]
    copies.append(pltpu.make_async_copy(wout_scr, wout_ref.at[:, at], sems.at[4]))
    copies[-1].start()
    if shares:
        for load in loads:
            load.wait()
        gx_scr[...] = jnp.sum(share_scr[...].astype(F32), axis=0).astype(BF16)
        copies.append(pltpu.make_async_copy(gx_scr, gx_ref, gx_sems.at[shares]))
        copies[-1].start()
    for copy in copies:
        copy.wait()


def unfold(which, source, depth, shares=(), filled=()):
    width = source.shape[1]
    results = [pltpu.HBM((4, depth, width), F32), pltpu.HBM((width, depth), F32)]
    scratch = [
        pltpu.VMEM((4, depth // 2, width), F32),
        pltpu.VMEM((width, depth // 2), F32),
        pltpu.SemaphoreType.DMA((5,)),
    ]
    if shares:
        shape, count = shares[0].shape, len(shares)
        results = [pltpu.HBM(shape, BF16)] + results
        scratch += [
            pltpu.VMEM((count,) + shape, BF16),
            pltpu.VMEM(shape, BF16),
            pltpu.SemaphoreType.DMA((count + 1,)),
        ]
    return pl.pallas_call(
        functools.partial(unfold_kernel, len(shares)),
        out_shape=results,
        in_specs=[SMEM, VMEM] + [ANY] * (len(shares) + len(filled)),
        out_specs=[ANY] * len(results),
        scratch_shapes=scratch,
        input_output_aliases={2 + i: i for i in range(len(filled))},
        compiler_params=PARAMS,
        cost_estimate=pl.CostEstimate(flops=0, bytes_accessed=1 << 20, transcendentals=0),
    )(which, source, *shares, *filled)


class Load:
    def __init__(self, source, buffer=None, sem=None):
        self.buffer, self.copy = source, None
        if buffer is not None:
            self.buffer = buffer
            self.copy = pltpu.make_async_copy(source, buffer, sem)
            self.copy.start()

    def get(self):
        if self.copy is not None:
            self.copy.wait()
            self.copy = None
        return self.buffer


class Store:
    def __init__(self, target, buffer=None, sem=None):
        self.buffer, self.copy, self.started = target, None, False
        self.target, self.sem = target, sem
        if buffer is not None:
            self.buffer = buffer
            self.copy = pltpu.make_async_copy(buffer, target, sem)

    def send(self):
        if self.copy is not None and not self.started:
            self.copy.start()
            self.started = True

    def send_part(self, at):
        pltpu.make_async_copy(self.buffer.at[at], self.target.at[at], self.sem).start()
        self.started = True

    def wait(self):
        if self.copy is not None:
            self.copy.wait()


def call(kernel, outs, ins, scalars=(), scratch=(), near_in=(), raw_in=(), near_out=(), flops=0, moved=0):
    ns, ni, no = len(scalars), len(ins), len(outs)
    far_in = [i for i in range(ni) if i not in near_in and i not in raw_in]
    far_out = [i for i in range(no) if i not in near_out]

    ins = [
        a if i in near_in else pltpu.with_memory_space_constraint(a, pltpu.HBM) for i, a in enumerate(ins)
    ]

    def body(*refs):
        given, refs = refs[:ns], refs[ns:]
        sources, refs = refs[:ni], refs[ni:]
        targets, refs = refs[:no], refs[no:]
        in_bufs, refs = dict(zip(far_in, refs)), refs[len(far_in) :]
        out_bufs, refs = dict(zip(far_out, refs)), refs[len(far_out) :]
        sems, extra = refs[0], refs[1:]
        loads = [
            Load(r, in_bufs[i], sems.at[i]) if i in in_bufs else Load(r) for i, r in enumerate(sources)
        ]
        stores = [
            Store(r, out_bufs[i], sems.at[ni + i]) if i in out_bufs else Store(r)
            for i, r in enumerate(targets)
        ]
        kernel(*given, *loads, *stores, *extra)
        for load in loads:
            load.get()
        for store in stores:
            store.send()
        for store in stores:
            store.wait()

    return pl.pallas_call(
        body,
        out_shape=[
            jax.ShapeDtypeStruct(s, d) if i in near_out else pltpu.HBM(s, d) for i, (s, d) in enumerate(outs)
        ],
        in_specs=[SMEM] * ns + [VMEM if i in near_in else ANY for i in range(ni)],
        out_specs=[VMEM if i in near_out else ANY for i in range(no)],
        scratch_shapes=[pltpu.VMEM(ins[i].shape, ins[i].dtype) for i in far_in]
        + [pltpu.VMEM(*outs[i]) for i in far_out]
        + [pltpu.SemaphoreType.DMA((ni + no,))]
        + list(scratch),
        compiler_params=PARAMS,
        cost_estimate=pl.CostEstimate(flops=flops, bytes_accessed=moved, transcendentals=0),
    )(*scalars, *ins)


def on_device(imp_x, imp_hist, imp_len, owner_map, hist_x, w_in, w_out, grad_y):
    owners = lax.axis_size("dp")
    planes = lax.axis_size("mp")
    rows, depth = imp_x.shape
    width = w_in.shape[2]
    slots = owners * CAP
    events = hist_x.shape[1]
    chips = owners // 2
    place_of = lax.axis_index("dp")
    core = (place_of % 2).reshape(1)
    hist = hist_x[0]
    pairs = [(i, i ^ 1) for i in range(owners)]
    same_core = [[2 * i + c for i in range(chips)] for c in range(2)]

    def swap(a):
        return lax.ppermute(a, "dp", pairs)

    def exchange(a):
        a = a.reshape(owners, a.shape[0] // owners, width)
        a = lax.all_to_all(a, "dp", 0, 0, tiled=True)
        return a.reshape(a.shape[0] * a.shape[1], width)

    def exchange_core(a):
        a = a.reshape(chips, a.shape[0] // chips, width)
        a = lax.all_to_all(a, "dp", 0, 0, axis_index_groups=same_core, tiled=True)
        return a.reshape(a.shape[0] * a.shape[1], width)

    hist_rows = imp_hist.reshape(1, rows)
    owner_row = owner_map.reshape(1, owners)
    (send,) = call(
        pre_kernel,
        [((3 * slots, width), BF16)],
        (hist_rows, imp_len.reshape(1, rows), owner_row, imp_x, w_in, w_out, grad_y),
        scratch=[pltpu.VMEM((2,) + w_in.shape[1:], BF16), pltpu.SemaphoreType.DMA(())],
        raw_in=(4,),
        near_out=(0,),
        flops=2 * rows * depth * width * 3,
        moved=1 << 20,
    )
    recv = exchange(send)
    keys, values_t, values, keys_t, key_slope, aux, place = call(
        project_kernel,
        [
            ((events, width), BF16),
            ((width, events), BF16),
            ((events, width), BF16),
            ((width, events), BF16),
            ((events, width), BF16),
            ((4, rows, width), F32),
            ((slots, rows), BF16),
        ],
        (w_in, hist, hist_rows, owner_row, imp_x, w_out, grad_y),
        near_out=(0, 1),
        flops=4 * events * depth * width,
        moved=5 << 20,
    )
    heads = width // DH
    back, weights, d_keys, d_att = call(
        attend_kernel,
        [
            ((2 * slots, width), BF16),
            ((events, heads * slots), BF16),
            ((events, width), BF16),
            ((slots, width), BF16),
        ],
        (recv, keys, values_t, values, keys_t),
        scratch=[pltpu.VMEM((events, heads * slots), BF16)],
        near_in=(0, 1, 2),
        near_out=(0,),
        flops=10 * events * slots * width,
        moved=8 << 20,
    )
    back = exchange(back)
    half = depth * 2 // 2
    gkv, kv_mine, kv_other, place, aux, x_near, w_near, gy_near = call(
        history_kernel,
        [((events, 2 * width), BF16)]
        + [((half, width), BF16)] * 2
        + [(place.shape, BF16), (aux.shape, F32), (imp_x.shape, BF16)]
        + [((2,) + w_in.shape[1:], BF16), (grad_y.shape, BF16)],
        (d_att, d_keys, key_slope, weights, hist, place, aux, imp_x, w_in, grad_y),
        (core,),
        scratch=[
            pltpu.VMEM((2, half, width), BF16),
            pltpu.VMEM((events, heads * slots), BF16),
            pltpu.VMEM((events, 2 * width), BF16),
            pltpu.VMEM((events, depth), BF16),
            pltpu.SemaphoreType.DMA((HISTORY_PARTS,)),
            pltpu.SemaphoreType.DMA(()),
            pltpu.SemaphoreType.DMA((LATE,)),
        ],
        raw_in=(3, 4, 5, 6, 7, 8, 9),
        near_out=(1, 2, 3, 4, 5, 6, 7),
        flops=4 * events * depth * width + 2 * events * slots * width,
        moved=10 << 20,
    )
    back, kv_mine, kv_other = lax.optimization_barrier((back, kv_mine, kv_other))
    half = depth * 3 // 2
    mine, other, gx = call(
        post_kernel,
        [((chips * 40, width), BF16)] * 2 + [((rows, depth), BF16)],
        (back, kv_mine, kv_other, place, aux, x_near, w_near, gy_near),
        (core,),
        scratch=[pltpu.VMEM((2, half, width), F32)],
        near_in=(0, 1, 2, 3, 4, 5, 6, 7),
        near_out=(0, 1, 2),
        flops=2 * rows * depth * width * 5,
        moved=2 << 20,
    )
    other = swap(other)
    (summed,) = call(
        pair_kernel,
        [((chips * 40, width), BF16)],
        (mine, other),
        near_in=(0, 1),
        near_out=(0,),
        moved=1 << 20,
    )
    plane = lax.axis_index("mp")
    share = rows // planes
    parts = [lax.dynamic_slice_in_dim(gx, plane * share, share, 0)]
    for step in range(1, planes):
        part = lax.dynamic_slice_in_dim(gx, (plane + step) % planes * share, share, 0)
        parts.append(lax.ppermute(part, "mp", [(i, (i + step) % planes) for i in range(planes)]))
    factor = (rows * owners) ** (-0.5)
    grad_kv = gkv.reshape(1, events, 2, width)
    summed, grad_kv, *parts = lax.optimization_barrier((exchange_core(summed), grad_kv, *parts))
    (piece,) = call(
        lambda i, o: sum_kernel(factor, i, o),
        [((chips * 40, width), BF16)],
        (summed,),
        near_in=(0,),
        near_out=(0,),
        moved=1 << 20,
    )
    mine = exchange_core(piece)
    other = swap(mine)
    grad_x, *filled = unfold(core, mine, depth, shares=parts)
    grad_w_in, grad_w_out = unfold(1 - core, other, depth, filled=filled)
    return (grad_x, grad_kv, grad_w_in, grad_w_out)


def solution(mesh):
    placed = (
        P("dp", None),
        P("dp", None),
        P("dp"),
        P(),
        P("dp", None, None),
        P(None, None, "mp"),
        P("mp", None),
        P("dp", None),
    )
    return jax.shard_map(
        on_device,
        mesh=mesh,
        in_specs=placed,
        out_specs=(
            P(("dp", "mp"), None),
            P("dp", None, None, "mp"),
            P(None, None, "mp"),
            P("mp", None),
        ),
        check_vma=False,
    )
```

```python
import functools

import jax
import jax.numpy as jnp
from jax import lax
from jax.experimental import pallas as pl
from jax.experimental.pallas import tpu as pltpu
from jax.sharding import PartitionSpec as P

DH = 64
EPSILON = 1e-05
CAP = 8
BLOCK = 256
HISTORY_PARTS = 2
LATE = 5
ROWS = 2 * CAP + 2
F32 = jnp.float32
BF16 = jnp.bfloat16
ANY = pl.BlockSpec(memory_space=pl.ANY)
VMEM = pl.BlockSpec(memory_space=pltpu.VMEM)
SMEM = pl.BlockSpec(memory_space=pltpu.SMEM)
PARAMS = pltpu.CompilerParams(vmem_limit_bytes=40 * 1024 * 1024)


def nn(a, b):
    return lax.dot_general(a, b, (((1,), (0,)), ((), ())), preferred_element_type=F32)


def nt(a, b):
    return lax.dot_general(a, b, (((1,), (1,)), ((), ())), preferred_element_type=F32)


def tn(a, b):
    return lax.dot_general(a, b, (((0,), (0,)), ((), ())), preferred_element_type=F32)


def sigmoid(v):
    return 0.5 * jnp.tanh(0.5 * v) + 0.5


def silu_and_slope(v):
    s = sigmoid(v)
    return v * s, s * (1.0 + v * (1.0 - s))


def iota(shape, dim):
    return lax.broadcasted_iota(jnp.int32, shape, dim)


def spread(parts):
    count = parts[0].shape[0] // 8
    cut = [p.reshape(count, 8, p.shape[1]) for p in parts]
    joined = jnp.concatenate(cut, axis=1)
    return joined.reshape(count * 8 * len(parts), parts[0].shape[1])


def slot_parts(hist, owner):
    rows, owners = hist.shape[1], owner.shape[1]
    named = jnp.where(iota((owners, rows), 0) == hist, 1.0, 0.0).astype(BF16)
    owner = jnp.broadcast_to(owner.astype(F32), (8, owners)).astype(BF16)
    target = nn(owner, named)[:1]
    hit = jnp.where(iota((owners, rows), 0).astype(F32) == target, 1.0, 0.0)
    earlier = jnp.where(iota((rows, rows), 0) < iota((rows, rows), 1), 1.0, 0.0)
    before = nn(hit.astype(BF16), earlier.astype(BF16))
    rank = jnp.sum(before * hit, axis=0, keepdims=True)
    return target, rank, hit


def one_hot(slot, slots):
    return jnp.where(iota((slots, slot.shape[1]), 0).astype(F32) == slot, 1.0, 0.0).astype(BF16)


def every(first, count, step):
    return pl.ds(first, count, stride=step)


def column(row):
    return jnp.transpose(jnp.broadcast_to(row, (row.shape[1], row.shape[1])))


def pre_kernel(hist_in, len_in, owner_in, x_in, w_in, wo_in, gy_in, send_out, w_scr, w_sem, scr):
    w_copy = pltpu.make_async_copy(w_in.get().at[:2], w_scr, w_sem)
    w_copy.start()
    target, rank, hit = slot_parts(hist_in.get()[...], owner_in.get()[...])
    owners, rows = hit.shape
    place = one_hot(rank * float(owners) + target, owners * CAP)
    length = len_in.get()[...].astype(F32)
    high = jnp.floor(length * (1.0 / 256.0))
    low = length - 256.0 * high
    lane = iota((rows, rows), 1).astype(F32) == column(rank)
    hit = hit.astype(BF16)
    for i, digit in enumerate((high, low)):
        digit = jnp.where(lane, column(digit), 0.0).astype(BF16)
        scr[every(2 * CAP + i, owners, ROWS), :] = nn(hit, digit)
    cot = nt(gy_in.get()[...], wo_in.get()[...]).astype(BF16).astype(F32)
    x = x_in.get()[...]
    w_copy.wait()
    queries, _ = silu_and_slope(nn(x, w_scr[0]))
    gates, _ = silu_and_slope(nn(x, w_scr[1]))
    gates = gates.astype(BF16).astype(F32)
    payload = jnp.concatenate([queries.astype(BF16), (cot * gates).astype(BF16)], axis=1)
    packed = nn(place, payload)
    width = queries.shape[1]
    for j in range(CAP):
        some = packed[j * owners : (j + 1) * owners]
        scr[every(j, owners, ROWS), :] = some[:, :width]
        scr[every(CAP + j, owners, ROWS), :] = some[:, width:]
    send_out.buffer[...] = scr[...].astype(BF16)


def project_kernel(
    w_in, ev_in, hist_in, owner_in, x_in, wo_in, gy_in,
    k_out, vt_out, v_out, kt_out, slope_out, aux_out, place_out,
):
    w_ref, ev_ref = w_in.get(), ev_in.get()
    count = ev_ref.shape[0] // 512
    for b in range(count):
        at = pl.ds(b * 512, 512)
        ev = ev_ref[at, :]
        keys, slope = silu_and_slope(nn(ev, w_ref[2]))
        values = nn(ev, w_ref[3])
        k_out.buffer[at, :] = keys.astype(BF16)
        v_out.buffer[at, :] = values.astype(BF16)
        slope_out.buffer[at, :] = slope.astype(BF16)
        kt_out.buffer[:, at] = jnp.transpose(keys.astype(BF16))
        vt_out.buffer[:, at] = jnp.transpose(values.astype(BF16))
    for out in (k_out, v_out, kt_out, vt_out, slope_out):
        out.send()
    target, rank, hit = slot_parts(hist_in.get()[...], owner_in.get()[...])
    place_out.buffer[...] = one_hot(target * float(CAP) + rank, hit.shape[0] * CAP)
    x = x_in.get()[...]
    _, slope_q = silu_and_slope(nn(x, w_ref[0]))
    gates, slope_g = silu_and_slope(nn(x, w_ref[1]))
    aux_out.buffer[0] = slope_q
    aux_out.buffer[1] = slope_g
    aux_out.buffer[2] = gates.astype(BF16).astype(F32)
    aux_out.buffer[3] = nt(gy_in.get()[...], wo_in.get()[...]).astype(BF16).astype(F32)


def attend_kernel(
    recv_in, k_in, vt_in, v_in, kt_in,
    back_out, weights_out, d_keys_out, d_att_out,
    s_scr, in_scr, out_scr,
):
    recv_ref, k_ref, vt_ref = recv_in.get(), k_in.get(), vt_in.get()
    owners, width = recv_ref.shape[0] // ROWS, recv_ref.shape[1]
    slots = owners * CAP
    heads = width // DH
    events = k_ref.shape[0]
    in_scr[...] = recv_ref[...].astype(F32)
    q = jnp.concatenate([in_scr[every(j, owners, ROWS), :] for j in range(CAP)], axis=0).astype(BF16)
    dn = jnp.concatenate([in_scr[every(CAP + j, owners, ROWS), :] for j in range(CAP)], axis=0).astype(BF16)
    high, low = (in_scr[every(2 * CAP + i, owners, ROWS), :] for i in range(2))
    length = jnp.transpose(high * 256.0 + low)
    length = jnp.concatenate([length[j : j + 1] for j in range(CAP)], axis=1)
    head_row = iota((width, slots), 0) // DH
    head_col = iota((slots, width), 1) // DH
    qt_half = (jnp.transpose(q).astype(F32) * (0.5 * DH ** (-0.5))).astype(BF16)
    zero = jnp.zeros((), BF16)
    qt_of = [jnp.where(head_row == h, qt_half, zero) for h in range(heads)]
    cols_of = [slice(h * slots, (h + 1) * slots) for h in range(heads)]
    mine_of = [slice(h * DH, (h + 1) * DH) for h in range(heads)]
    for start in range(0, events, BLOCK):
        at = pl.ds(start, BLOCK)
        visible = (iota((BLOCK, slots), 0) + start).astype(F32) < length
        for h in range(heads):
            half = nn(k_ref[at, :], qt_of[h])
            twice = jnp.where(visible, jnp.tanh(half) + 1.0, 0.0)
            weights = half * twice
            s_scr[at, cols_of[h]] = (twice + weights * (2.0 - twice)).astype(BF16)
            weights_out.buffer[at, cols_of[h]] = weights.astype(BF16)
        weights_out.send_part((at,))
    att = [nn(vt_ref[mine_of[h], :], weights_out.buffer[:, cols_of[h]]) for h in range(heads)]
    att = jnp.concatenate(att, axis=0).reshape(heads, DH, slots)
    inverse = lax.rsqrt(jnp.mean(att * att, axis=1, keepdims=True) + EPSILON)
    normed = att * inverse
    dnt = jnp.transpose(dn).astype(F32).reshape(heads, DH, slots)
    d_att = inverse * (dnt - normed * jnp.mean(dnt * normed, axis=1, keepdims=True))
    d_att = d_att.reshape(width, slots).astype(BF16)
    d_att_out.buffer[...] = jnp.transpose(d_att)
    d_att_out.send()
    normed = jnp.transpose(normed.reshape(width, slots).astype(BF16)).astype(F32)
    dt_of = [jnp.where(head_row == h, d_att, zero) for h in range(heads)]
    q_of = jnp.concatenate([jnp.where(head_col == h, q, zero) for h in range(heads)], axis=0)
    v_ref, kt_ref = v_in.get(), kt_in.get()
    for start in range(0, events, BLOCK):
        at = pl.ds(start, BLOCK)
        for h in range(heads):
            ds = nn(v_ref[at, :], dt_of[h]) * s_scr[at, cols_of[h]].astype(F32)
            s_scr[at, cols_of[h]] = ds.astype(BF16)
        d_keys = nn(s_scr[at, :], q_of) * (0.5 * DH ** (-0.5))
        d_keys_out.buffer[at, :] = d_keys.astype(BF16)
        d_keys_out.send_part((at,))
    d_query = [nn(kt_ref[mine_of[h], :], s_scr[:, cols_of[h]]) for h in range(heads)]
    d_query = (jnp.concatenate(d_query, axis=0) * (0.5 * DH ** (-0.5))).astype(BF16)
    d_query = jnp.transpose(d_query).astype(F32)
    for j in range(CAP):
        some = slice(j * owners, (j + 1) * owners)
        out_scr[every(j, owners, 2 * CAP), :] = d_query[some]
        out_scr[every(CAP + j, owners, 2 * CAP), :] = normed[some]
    back_out.buffer[...] = out_scr[...].astype(BF16)


def history_kernel(
    core_ref, d_att_in, d_keys_in, slope_in, weights_in, ev_in, *rest
):
    late, rest = rest[:LATE], rest[LATE:]
    gkv_out, mine_out, other_out, rest = rest[0], rest[1], rest[2], rest[3:]
    kept, (scr, w_scr, term_scr, ev_scr, sems, ev_sem, late_sems) = rest[:LATE], rest[LATE:]
    events = w_scr.shape[0]
    step = events // HISTORY_PARTS
    parts = [pl.ds(b * step, step) for b in range(HISTORY_PARTS)]
    copies = [
        pltpu.make_async_copy(weights_in.get().at[at], w_scr.at[at], sems.at[b])
        for b, at in enumerate(parts)
    ]
    for copy in copies:
        copy.start()
    ev_copy = pltpu.make_async_copy(ev_in.get(), ev_scr, ev_sem)
    ev_copy.start()
    moves = [
        pltpu.make_async_copy(src.get().at[: dst.buffer.shape[0]], dst.buffer, late_sems.at[i])
        for i, (src, dst) in enumerate(zip(late, kept))
    ]
    for move in moves:
        move.start()
    d_att = d_att_in.get()[...]
    slots, width = d_att.shape
    heads = width // DH
    head_col = iota((slots, width), 1) // DH
    zero = jnp.zeros((), BF16)
    d_of = jnp.concatenate([jnp.where(head_col == h, d_att, zero) for h in range(heads)], axis=0)
    d_keys_ref, slope_ref, gkv_ref = d_keys_in.get(), slope_in.get(), gkv_out.buffer
    for at, copy in zip(parts, copies):
        d_keys = d_keys_ref[at, :]
        gkv_ref[at, :width] = d_keys
        term_scr[at, :width] = (d_keys.astype(F32) * slope_ref[at, :].astype(F32)).astype(BF16)
        copy.wait()
        d_values = nn(w_scr[at, :], d_of).astype(BF16)
        gkv_ref[at, width:] = d_values
        gkv_out.send_part((at,))
        term_scr[at, width:] = d_values
    ev_copy.wait()
    both = jnp.transpose(tn(term_scr[...], ev_scr[...]))
    rows = spread([both[:, :width], both[:, width:]]).astype(BF16)
    split_halves(core_ref[0], rows, scr, mine_out, other_out)
    for move in moves:
        move.wait()


def split_halves(core, rows, scr, mine_out, other_out):
    half = rows.shape[0] // 2
    scr[0] = rows[:half]
    scr[1] = rows[half:]
    other_out.buffer[...] = scr[1 - core]
    other_out.send()
    mine_out.buffer[...] = scr[core]


def post_kernel(
    core_ref, back_in, kv_mine_in, kv_other_in, place_in, aux_in, x_in, w_in, gy_in,
    mine_out, other_out, gx_out, scr,
):
    place = place_in.get()[...]
    back_ref, aux_ref, w_ref = back_in.get(), aux_in.get(), w_in.get()
    slots = place.shape[0]
    width = back_ref.shape[1]
    got = back_ref[...].astype(F32).reshape(slots // CAP, 2 * CAP, width)
    d_query = got[:, :CAP].reshape(slots, width).astype(BF16)
    normed = got[:, CAP:].reshape(slots, width).astype(BF16)
    both = tn(place, jnp.concatenate([d_query, normed], axis=1))
    d_query = both[:, :width]
    normed = both[:, width:]
    gates = aux_ref[2]
    gated = (normed * gates).astype(BF16)
    d_gate = (aux_ref[3] * normed).astype(BF16).astype(F32)
    q_term = (d_query * aux_ref[0]).astype(BF16)
    g_term = (d_gate * aux_ref[1]).astype(BF16)
    gx_out.buffer[...] = (nt(q_term, w_ref[0]) + nt(g_term, w_ref[1])).astype(BF16)
    gx_out.send()
    x = x_in.get()[...]
    gq = tn(x, q_term)
    gg = tn(x, g_term)
    go = tn(gated, gy_in.get()[...])
    go = jnp.concatenate([go[:, i * width : (i + 1) * width] for i in range(go.shape[1] // width)], axis=0)
    out = spread([gq, gg, go])
    half = out.shape[0] // 2
    scr[0] = out[:half]
    scr[1] = out[half:]
    core = core_ref[0]
    for kv_in, which, result in ((kv_other_in, 1 - core, other_out), (kv_mine_in, core, mine_out)):
        chunks = half // 24
        kv = kv_in.get()[...].astype(F32).reshape(chunks, 16, width)
        joined = jnp.concatenate([kv, scr[which].reshape(chunks, 24, width)], axis=1)
        result.buffer[...] = joined.reshape(chunks * 40, width).astype(BF16)


def pair_kernel(mine_in, other_in, out):
    out.buffer[...] = (mine_in.get()[...].astype(F32) + other_in.get()[...].astype(F32)).astype(BF16)


def sum_kernel(factor, rows_in, out):
    got = rows_in.get()[...]
    chunks = got.shape[0] // 40
    total = jnp.sum(got.astype(F32).reshape(chunks, 40, got.shape[1]), axis=0)
    total = total * factor
    shape = out.buffer.shape
    out.buffer[...] = jnp.broadcast_to(total[None], (chunks, 40, shape[1])).reshape(shape).astype(BF16)


def unfold_kernel(shares, which_ref, source_ref, *refs):
    if shares:
        share_refs, refs = refs[:shares], refs[shares:]
        gx_ref, win_ref, wout_ref, win_scr, wout_scr, sems, share_scr, gx_scr, gx_sems = refs
        loads = [
            pltpu.make_async_copy(share, share_scr.at[i], gx_sems.at[i]) for i, share in enumerate(share_refs)
        ]
        for load in loads:
            load.start()
    else:
        win_ref, wout_ref, win_scr, wout_scr, sems = refs[2:]
    got = source_ref[...].astype(F32)
    width = got.shape[1]
    chunks = got.shape[0] // 40
    size = chunks * 8
    got = got.reshape(chunks, 5, 8, width)
    at = pl.ds(pl.multiple_of(which_ref[0] * size, size), size)
    copies = []
    for place, index in enumerate((2, 3, 0, 1)):
        win_scr[index] = got[:, place].reshape(size, width)
        copies.append(pltpu.make_async_copy(win_scr.at[index], win_ref.at[index, at], sems.at[place]))
        copies[-1].start()
    last = got[:, 4].reshape(size, width)
    rows = wout_scr.shape[0]
    for i in range(size // rows):
        wout_scr[:, i * width : (i + 1) * width] = last[i * rows : (i + 1) * rows]
    copies.append(pltpu.make_async_copy(wout_scr, wout_ref.at[:, at], sems.at[4]))
    copies[-1].start()
    if shares:
        for load in loads:
            load.wait()
        gx_scr[...] = jnp.sum(share_scr[...].astype(F32), axis=0).astype(BF16)
        copies.append(pltpu.make_async_copy(gx_scr, gx_ref, gx_sems.at[shares]))
        copies[-1].start()
    for copy in copies:
        copy.wait()


def unfold(which, source, depth, shares=(), filled=()):
    width = source.shape[1]
    results = [pltpu.HBM((4, depth, width), F32), pltpu.HBM((width, depth), F32)]
    scratch = [
        pltpu.VMEM((4, depth // 2, width), F32),
        pltpu.VMEM((width, depth // 2), F32),
        pltpu.SemaphoreType.DMA((5,)),
    ]
    if shares:
        shape, count = shares[0].shape, len(shares)
        results = [pltpu.HBM(shape, BF16)] + results
        scratch += [
            pltpu.VMEM((count,) + shape, BF16),
            pltpu.VMEM(shape, BF16),
            pltpu.SemaphoreType.DMA((count + 1,)),
        ]
    return pl.pallas_call(
        functools.partial(unfold_kernel, len(shares)),
        out_shape=results,
        in_specs=[SMEM, VMEM] + [ANY] * (len(shares) + len(filled)),
        out_specs=[ANY] * len(results),
        scratch_shapes=scratch,
        input_output_aliases={2 + i: i for i in range(len(filled))},
        compiler_params=PARAMS,
        cost_estimate=pl.CostEstimate(flops=0, bytes_accessed=1 << 20, transcendentals=0),
    )(which, source, *shares, *filled)


class Load:
    def __init__(self, source, buffer=None, sem=None):
        self.buffer, self.copy = source, None
        if buffer is not None:
            self.buffer = buffer
            self.copy = pltpu.make_async_copy(source, buffer, sem)
            self.copy.start()

    def get(self):
        if self.copy is not None:
            self.copy.wait()
            self.copy = None
        return self.buffer


class Store:
    def __init__(self, target, buffer=None, sem=None):
        self.buffer, self.copy, self.started = target, None, False
        self.target, self.sem = target, sem
        if buffer is not None:
            self.buffer = buffer
            self.copy = pltpu.make_async_copy(buffer, target, sem)

    def send(self):
        if self.copy is not None and not self.started:
            self.copy.start()
            self.started = True

    def send_part(self, at):
        pltpu.make_async_copy(self.buffer.at[at], self.target.at[at], self.sem).start()
        self.started = True

    def wait(self):
        if self.copy is not None:
            self.copy.wait()


def call(kernel, outs, ins, scalars=(), scratch=(), near_in=(), raw_in=(), near_out=(), flops=0, moved=0):
    ns, ni, no = len(scalars), len(ins), len(outs)
    far_in = [i for i in range(ni) if i not in near_in and i not in raw_in]
    far_out = [i for i in range(no) if i not in near_out]

    ins = [
        a if i in near_in else pltpu.with_memory_space_constraint(a, pltpu.HBM) for i, a in enumerate(ins)
    ]

    def body(*refs):
        given, refs = refs[:ns], refs[ns:]
        sources, refs = refs[:ni], refs[ni:]
        targets, refs = refs[:no], refs[no:]
        in_bufs, refs = dict(zip(far_in, refs)), refs[len(far_in) :]
        out_bufs, refs = dict(zip(far_out, refs)), refs[len(far_out) :]
        sems, extra = refs[0], refs[1:]
        loads = [
            Load(r, in_bufs[i], sems.at[i]) if i in in_bufs else Load(r) for i, r in enumerate(sources)
        ]
        stores = [
            Store(r, out_bufs[i], sems.at[ni + i]) if i in out_bufs else Store(r)
            for i, r in enumerate(targets)
        ]
        kernel(*given, *loads, *stores, *extra)
        for load in loads:
            load.get()
        for store in stores:
            store.send()
        for store in stores:
            store.wait()

    return pl.pallas_call(
        body,
        out_shape=[
            jax.ShapeDtypeStruct(s, d) if i in near_out else pltpu.HBM(s, d) for i, (s, d) in enumerate(outs)
        ],
        in_specs=[SMEM] * ns + [VMEM if i in near_in else ANY for i in range(ni)],
        out_specs=[VMEM if i in near_out else ANY for i in range(no)],
        scratch_shapes=[pltpu.VMEM(ins[i].shape, ins[i].dtype) for i in far_in]
        + [pltpu.VMEM(*outs[i]) for i in far_out]
        + [pltpu.SemaphoreType.DMA((ni + no,))]
        + list(scratch),
        compiler_params=PARAMS,
        cost_estimate=pl.CostEstimate(flops=flops, bytes_accessed=moved, transcendentals=0),
    )(*scalars, *ins)


def on_device(imp_x, imp_hist, imp_len, owner_map, hist_x, w_in, w_out, grad_y):
    owners = lax.axis_size("dp")
    planes = lax.axis_size("mp")
    rows, depth = imp_x.shape
    width = w_in.shape[2]
    slots = owners * CAP
    events = hist_x.shape[1]
    chips = owners // 2
    place_of = lax.axis_index("dp")
    core = (place_of % 2).reshape(1)
    hist = hist_x[0]
    pairs = [(i, i ^ 1) for i in range(owners)]
    same_core = [[2 * i + c for i in range(chips)] for c in range(2)]

    def swap(a):
        return lax.ppermute(a, "dp", pairs)

    def exchange(a):
        shape = a.shape
        size = shape[0] // owners
        a = a.reshape((owners, size, width) if size % 8 == 0 else (owners, size // 2, 2, width))
        return lax.all_to_all(a, "dp", 0, 0, tiled=True).reshape(shape)

    def exchange_core(a):
        a = a.reshape(chips, a.shape[0] // chips, width)
        a = lax.all_to_all(a, "dp", 0, 0, axis_index_groups=same_core, tiled=True)
        return a.reshape(a.shape[0] * a.shape[1], width)

    hist_rows = imp_hist.reshape(1, rows)
    owner_row = owner_map.reshape(1, owners)
    (send,) = call(
        pre_kernel,
        [((owners * ROWS, width), BF16)],
        (hist_rows, imp_len.reshape(1, rows), owner_row, imp_x, w_in, w_out, grad_y),
        scratch=[
            pltpu.VMEM((2,) + w_in.shape[1:], BF16),
            pltpu.SemaphoreType.DMA(()),
            pltpu.VMEM((owners * ROWS, width), F32),
        ],
        raw_in=(4,),
        near_out=(0,),
        flops=2 * rows * depth * width * 3,
        moved=1 << 20,
    )
    recv = exchange(send)
    keys, values_t, values, keys_t, key_slope, aux, place = call(
        project_kernel,
        [
            ((events, width), BF16),
            ((width, events), BF16),
            ((events, width), BF16),
            ((width, events), BF16),
            ((events, width), BF16),
            ((4, rows, width), F32),
            ((slots, rows), BF16),
        ],
        (w_in, hist, hist_rows, owner_row, imp_x, w_out, grad_y),
        near_out=(0, 1),
        flops=4 * events * depth * width,
        moved=5 << 20,
    )
    heads = width // DH
    back, weights, d_keys, d_att = call(
        attend_kernel,
        [
            ((2 * slots, width), BF16),
            ((events, heads * slots), BF16),
            ((events, width), BF16),
            ((slots, width), BF16),
        ],
        (recv, keys, values_t, values, keys_t),
        scratch=[
            pltpu.VMEM((events, heads * slots), BF16),
            pltpu.VMEM((owners * ROWS, width), F32),
            pltpu.VMEM((2 * slots, width), F32),
        ],
        near_in=(0, 1, 2),
        near_out=(0,),
        flops=10 * events * slots * width,
        moved=8 << 20,
    )
    back = exchange(back)
    half = depth * 2 // 2
    gkv, kv_mine, kv_other, place, aux, x_near, w_near, gy_near = call(
        history_kernel,
        [((events, 2 * width), BF16)]
        + [((half, width), BF16)] * 2
        + [(place.shape, BF16), (aux.shape, F32), (imp_x.shape, BF16)]
        + [((2,) + w_in.shape[1:], BF16), (grad_y.shape, BF16)],
        (d_att, d_keys, key_slope, weights, hist, place, aux, imp_x, w_in, grad_y),
        (core,),
        scratch=[
            pltpu.VMEM((2, half, width), BF16),
            pltpu.VMEM((events, heads * slots), BF16),
            pltpu.VMEM((events, 2 * width), BF16),
            pltpu.VMEM((events, depth), BF16),
            pltpu.SemaphoreType.DMA((HISTORY_PARTS,)),
            pltpu.SemaphoreType.DMA(()),
            pltpu.SemaphoreType.DMA((LATE,)),
        ],
        raw_in=(3, 4, 5, 6, 7, 8, 9),
        near_out=(1, 2, 3, 4, 5, 6, 7),
        flops=4 * events * depth * width + 2 * events * slots * width,
        moved=10 << 20,
    )
    back, kv_mine, kv_other = lax.optimization_barrier((back, kv_mine, kv_other))
    half = depth * 3 // 2
    mine, other, gx = call(
        post_kernel,
        [((chips * 40, width), BF16)] * 2 + [((rows, depth), BF16)],
        (back, kv_mine, kv_other, place, aux, x_near, w_near, gy_near),
        (core,),
        scratch=[pltpu.VMEM((2, half, width), F32)],
        near_in=(0, 1, 2, 3, 4, 5, 6, 7),
        near_out=(0, 1, 2),
        flops=2 * rows * depth * width * 5,
        moved=2 << 20,
    )
    other = swap(other)
    (summed,) = call(
        pair_kernel,
        [((chips * 40, width), BF16)],
        (mine, other),
        near_in=(0, 1),
        near_out=(0,),
        moved=1 << 20,
    )
    plane = lax.axis_index("mp")
    share = rows // planes
    parts = [lax.dynamic_slice_in_dim(gx, plane * share, share, 0)]
    for step in range(1, planes):
        part = lax.dynamic_slice_in_dim(gx, (plane + step) % planes * share, share, 0)
        parts.append(lax.ppermute(part, "mp", [(i, (i + step) % planes) for i in range(planes)]))
    factor = (rows * owners) ** (-0.5)
    grad_kv = gkv.reshape(1, events, 2, width)
    summed, grad_kv, *parts = lax.optimization_barrier((exchange_core(summed), grad_kv, *parts))
    (piece,) = call(
        lambda i, o: sum_kernel(factor, i, o),
        [((chips * 40, width), BF16)],
        (summed,),
        near_in=(0,),
        near_out=(0,),
        moved=1 << 20,
    )
    mine = exchange_core(piece)
    other = swap(mine)
    grad_x, *filled = unfold(core, mine, depth, shares=parts)
    grad_w_in, grad_w_out = unfold(1 - core, other, depth, filled=filled)
    return (grad_x, grad_kv, grad_w_in, grad_w_out)


def solution(mesh):
    placed = (
        P("dp", None),
        P("dp", None),
        P("dp"),
        P(),
        P("dp", None, None),
        P(None, None, "mp"),
        P("mp", None),
        P("dp", None),
    )
    return jax.shard_map(
        on_device,
        mesh=mesh,
        in_specs=placed,
        out_specs=(
            P(("dp", "mp"), None),
            P("dp", None, None, "mp"),
            P(None, None, "mp"),
            P("mp", None),
        ),
        check_vma=False,
    )
```

```python
import functools

import jax
import jax.numpy as jnp
from jax import lax
from jax.experimental import pallas as pl
from jax.experimental.pallas import tpu as pltpu
from jax.sharding import PartitionSpec as P

DH = 64
EPSILON = 1e-05
CAP = 8
BLOCK = 256
HISTORY_PARTS = 2
LATE = 5
MOVED = 1024
ROWS = 2 * CAP + 2
F32 = jnp.float32
BF16 = jnp.bfloat16
ANY = pl.BlockSpec(memory_space=pl.ANY)
VMEM = pl.BlockSpec(memory_space=pltpu.VMEM)
SMEM = pl.BlockSpec(memory_space=pltpu.SMEM)
PARAMS = pltpu.CompilerParams(vmem_limit_bytes=40 * 1024 * 1024)


def nn(a, b):
    return lax.dot_general(a, b, (((1,), (0,)), ((), ())), preferred_element_type=F32)


def nt(a, b):
    return lax.dot_general(a, b, (((1,), (1,)), ((), ())), preferred_element_type=F32)


def tn(a, b):
    return lax.dot_general(a, b, (((0,), (0,)), ((), ())), preferred_element_type=F32)


def sigmoid(v):
    return 0.5 * jnp.tanh(0.5 * v) + 0.5


def silu_and_slope(v):
    s = sigmoid(v)
    return v * s, s * (1.0 + v * (1.0 - s))


def iota(shape, dim):
    return lax.broadcasted_iota(jnp.int32, shape, dim)


def spread(parts):
    count = parts[0].shape[0] // 8
    cut = [p.reshape(count, 8, p.shape[1]) for p in parts]
    joined = jnp.concatenate(cut, axis=1)
    return joined.reshape(count * 8 * len(parts), parts[0].shape[1])


def slot_parts(hist, owner):
    rows, owners = hist.shape[1], owner.shape[1]
    named = jnp.where(iota((owners, rows), 0) == hist, 1.0, 0.0).astype(BF16)
    owner = jnp.broadcast_to(owner.astype(F32), (8, owners)).astype(BF16)
    target = nn(owner, named)[:1]
    hit = jnp.where(iota((owners, rows), 0).astype(F32) == target, 1.0, 0.0)
    earlier = jnp.where(iota((rows, rows), 0) < iota((rows, rows), 1), 1.0, 0.0)
    before = nn(hit.astype(BF16), earlier.astype(BF16))
    rank = jnp.sum(before * hit, axis=0, keepdims=True)
    return target, rank, hit


def one_hot(slot, slots):
    return jnp.where(iota((slots, slot.shape[1]), 0).astype(F32) == slot, 1.0, 0.0).astype(BF16)


def every(first, count, step):
    return pl.ds(first, count, stride=step)


def column(row):
    return jnp.transpose(jnp.broadcast_to(row, (row.shape[1], row.shape[1])))


def pre_kernel(hist_in, len_in, owner_in, x_in, w_in, wo_in, gy_in, send_out, w_scr, w_sem, scr):
    w_copy = pltpu.make_async_copy(w_in.get().at[:2], w_scr, w_sem)
    w_copy.start()
    target, rank, hit = slot_parts(hist_in.get()[...], owner_in.get()[...])
    owners, rows = hit.shape
    place = one_hot(rank * float(owners) + target, owners * CAP)
    length = len_in.get()[...].astype(F32)
    high = jnp.floor(length * (1.0 / 256.0))
    low = length - 256.0 * high
    lane = iota((rows, rows), 1).astype(F32) == column(rank)
    hit = hit.astype(BF16)
    for i, digit in enumerate((high, low)):
        digit = jnp.where(lane, column(digit), 0.0).astype(BF16)
        scr[every(2 * CAP + i, owners, ROWS), :] = nn(hit, digit)
    cot = nt(gy_in.get()[...], wo_in.get()[...]).astype(BF16).astype(F32)
    x = x_in.get()[...]
    w_copy.wait()
    queries, _ = silu_and_slope(nn(x, w_scr[0]))
    gates, _ = silu_and_slope(nn(x, w_scr[1]))
    gates = gates.astype(BF16).astype(F32)
    payload = jnp.concatenate([queries.astype(BF16), (cot * gates).astype(BF16)], axis=1)
    packed = nn(place, payload)
    width = queries.shape[1]
    for j in range(CAP):
        some = packed[j * owners : (j + 1) * owners]
        scr[every(j, owners, ROWS), :] = some[:, :width]
        scr[every(CAP + j, owners, ROWS), :] = some[:, width:]
    send_out.buffer[...] = scr[...].astype(BF16)


def project_kernel(
    w_in, ev_in, hist_in, owner_in, x_in, wo_in, gy_in,
    k_out, vt_out, v_out, kt_out, slope_out, aux_out, place_out,
):
    w_ref, ev_ref = w_in.get(), ev_in.get()
    count = ev_ref.shape[0] // 512
    for b in range(count):
        at = pl.ds(b * 512, 512)
        ev = ev_ref[at, :]
        keys, slope = silu_and_slope(nn(ev, w_ref[2]))
        values = nn(ev, w_ref[3])
        k_out.buffer[at, :] = keys.astype(BF16)
        v_out.buffer[at, :] = values.astype(BF16)
        slope_out.buffer[at, :] = slope.astype(BF16)
        kt_out.buffer[:, at] = jnp.transpose(keys.astype(BF16))
        vt_out.buffer[:, at] = jnp.transpose(values.astype(BF16))
    for out in (k_out, v_out, kt_out, vt_out, slope_out):
        out.send()
    target, rank, hit = slot_parts(hist_in.get()[...], owner_in.get()[...])
    place_out.buffer[...] = one_hot(target * float(CAP) + rank, hit.shape[0] * CAP)
    x = x_in.get()[...]
    _, slope_q = silu_and_slope(nn(x, w_ref[0]))
    gates, slope_g = silu_and_slope(nn(x, w_ref[1]))
    aux_out.buffer[0] = slope_q
    aux_out.buffer[1] = slope_g
    aux_out.buffer[2] = gates.astype(BF16).astype(F32)
    aux_out.buffer[3] = nt(gy_in.get()[...], wo_in.get()[...]).astype(BF16).astype(F32)


def attend_kernel(
    recv_in, k_in, vt_in, v_in, kt_in,
    back_out, weights_out, d_keys_out, d_att_out, d_scores_out, q_out,
    s_scr, in_scr, out_scr,
):
    recv_ref, k_ref, vt_ref = recv_in.get(), k_in.get(), vt_in.get()
    owners, width = recv_ref.shape[0] // ROWS, recv_ref.shape[1]
    slots = owners * CAP
    heads = width // DH
    events = k_ref.shape[0]
    in_scr[...] = recv_ref[...].astype(F32)
    q = jnp.concatenate([in_scr[every(j, owners, ROWS), :] for j in range(CAP)], axis=0).astype(BF16)
    dn = jnp.concatenate([in_scr[every(CAP + j, owners, ROWS), :] for j in range(CAP)], axis=0).astype(BF16)
    q_out.buffer[...] = q
    q_out.send()
    high, low = (in_scr[every(2 * CAP + i, owners, ROWS), :] for i in range(2))
    length = jnp.transpose(high * 256.0 + low)
    length = jnp.concatenate([length[j : j + 1] for j in range(CAP)], axis=1)
    head_row = iota((width, slots), 0) // DH
    head_col = iota((slots, width), 1) // DH
    qt_half = (jnp.transpose(q).astype(F32) * (0.5 * DH ** (-0.5))).astype(BF16)
    zero = jnp.zeros((), BF16)
    qt_of = [jnp.where(head_row == h, qt_half, zero) for h in range(heads)]
    cols_of = [slice(h * slots, (h + 1) * slots) for h in range(heads)]
    mine_of = [slice(h * DH, (h + 1) * DH) for h in range(heads)]
    for start in range(0, events, BLOCK):
        at = pl.ds(start, BLOCK)
        visible = (iota((BLOCK, slots), 0) + start).astype(F32) < length
        for h in range(heads):
            half = nn(k_ref[at, :], qt_of[h])
            twice = jnp.where(visible, jnp.tanh(half) + 1.0, 0.0)
            weights = half * twice
            s_scr[at, cols_of[h]] = (twice + weights * (2.0 - twice)).astype(BF16)
            weights_out.buffer[at, cols_of[h]] = weights.astype(BF16)
        weights_out.send_part((at,))
    att = [nn(vt_ref[mine_of[h], :], weights_out.buffer[:, cols_of[h]]) for h in range(heads)]
    att = jnp.concatenate(att, axis=0).reshape(heads, DH, slots)
    inverse = lax.rsqrt(jnp.mean(att * att, axis=1, keepdims=True) + EPSILON)
    normed = att * inverse
    dnt = jnp.transpose(dn).astype(F32).reshape(heads, DH, slots)
    d_att = inverse * (dnt - normed * jnp.mean(dnt * normed, axis=1, keepdims=True))
    d_att = d_att.reshape(width, slots).astype(BF16)
    d_att_out.buffer[...] = jnp.transpose(d_att)
    d_att_out.send()
    normed = jnp.transpose(normed.reshape(width, slots).astype(BF16)).astype(F32)
    dt_of = [jnp.where(head_row == h, d_att, zero) for h in range(heads)]
    q_of = jnp.concatenate([jnp.where(head_col == h, q, zero) for h in range(heads)], axis=0)
    v_ref, kt_ref = v_in.get(), kt_in.get()
    for start in range(0, events, BLOCK):
        at = pl.ds(start, BLOCK)
        for h in range(heads):
            ds = nn(v_ref[at, :], dt_of[h]) * s_scr[at, cols_of[h]].astype(F32)
            s_scr[at, cols_of[h]] = ds.astype(BF16)
            if start < MOVED:
                d_scores_out.buffer[at, cols_of[h]] = ds.astype(BF16)
        if start < MOVED:
            d_scores_out.send_part((at,))
            continue
        d_keys = nn(s_scr[at, :], q_of) * (0.5 * DH ** (-0.5))
        left = pl.ds(start - MOVED, BLOCK)
        d_keys_out.buffer[left, :] = d_keys.astype(BF16)
        d_keys_out.send_part((left,))
    d_query = [nn(kt_ref[mine_of[h], :], s_scr[:, cols_of[h]]) for h in range(heads)]
    d_query = (jnp.concatenate(d_query, axis=0) * (0.5 * DH ** (-0.5))).astype(BF16)
    d_query = jnp.transpose(d_query).astype(F32)
    for j in range(CAP):
        some = slice(j * owners, (j + 1) * owners)
        out_scr[every(j, owners, 2 * CAP), :] = d_query[some]
        out_scr[every(CAP + j, owners, 2 * CAP), :] = normed[some]
    back_out.buffer[...] = out_scr[...].astype(BF16)


def history_kernel(
    core_ref, d_att_in, q_in, d_scores_in, d_keys_in, slope_in, weights_in, ev_in, *rest
):
    late, rest = rest[:LATE], rest[LATE:]
    gkv_out, mine_out, other_out, rest = rest[0], rest[1], rest[2], rest[3:]
    kept, (scr, w_scr, term_scr, ev_scr, sems, ev_sem, late_sems) = rest[:LATE], rest[LATE:]
    events = w_scr.shape[0]
    step = events // HISTORY_PARTS
    parts = [pl.ds(b * step, step) for b in range(HISTORY_PARTS)]
    copies = [
        pltpu.make_async_copy(weights_in.get().at[at], w_scr.at[at], sems.at[b])
        for b, at in enumerate(parts)
    ]
    for copy in copies:
        copy.start()
    ev_copy = pltpu.make_async_copy(ev_in.get(), ev_scr, ev_sem)
    ev_copy.start()
    moves = [
        pltpu.make_async_copy(src.get().at[: dst.buffer.shape[0]], dst.buffer, late_sems.at[i])
        for i, (src, dst) in enumerate(zip(late, kept))
    ]
    for move in moves:
        move.start()
    d_att = d_att_in.get()[...]
    slots, width = d_att.shape
    heads = width // DH
    head_col = iota((slots, width), 1) // DH
    zero = jnp.zeros((), BF16)
    d_of = jnp.concatenate([jnp.where(head_col == h, d_att, zero) for h in range(heads)], axis=0)
    q = q_in.get()[...]
    q_of = jnp.concatenate([jnp.where(head_col == h, q, zero) for h in range(heads)], axis=0)
    moved = (nn(d_scores_in.get()[...], q_of) * (0.5 * DH ** (-0.5))).astype(BF16)
    d_keys_ref, slope_ref, gkv_ref = d_keys_in.get(), slope_in.get(), gkv_out.buffer
    for b, (at, copy) in enumerate(zip(parts, copies)):
        if b == 0:
            d_keys = moved
            if step > MOVED:
                d_keys = jnp.concatenate([moved, d_keys_ref[: step - MOVED, :]], axis=0)
        else:
            d_keys = d_keys_ref[b * step - MOVED : (b + 1) * step - MOVED, :]
        gkv_ref[at, :width] = d_keys
        term_scr[at, :width] = (d_keys.astype(F32) * slope_ref[at, :].astype(F32)).astype(BF16)
        copy.wait()
        d_values = nn(w_scr[at, :], d_of).astype(BF16)
        gkv_ref[at, width:] = d_values
        gkv_out.send_part((at,))
        term_scr[at, width:] = d_values
    ev_copy.wait()
    both = jnp.transpose(tn(term_scr[...], ev_scr[...]))
    rows = spread([both[:, :width], both[:, width:]]).astype(BF16)
    split_halves(core_ref[0], rows, scr, mine_out, other_out)
    for move in moves:
        move.wait()


def split_halves(core, rows, scr, mine_out, other_out):
    half = rows.shape[0] // 2
    scr[0] = rows[:half]
    scr[1] = rows[half:]
    other_out.buffer[...] = scr[1 - core]
    other_out.send()
    mine_out.buffer[...] = scr[core]


def post_kernel(
    core_ref, back_in, kv_mine_in, kv_other_in, place_in, aux_in, x_in, w_in, gy_in,
    mine_out, other_out, gx_out, scr,
):
    place = place_in.get()[...]
    back_ref, aux_ref, w_ref = back_in.get(), aux_in.get(), w_in.get()
    slots = place.shape[0]
    width = back_ref.shape[1]
    got = back_ref[...].astype(F32).reshape(slots // CAP, 2 * CAP, width)
    d_query = got[:, :CAP].reshape(slots, width).astype(BF16)
    normed = got[:, CAP:].reshape(slots, width).astype(BF16)
    both = tn(place, jnp.concatenate([d_query, normed], axis=1))
    d_query = both[:, :width]
    normed = both[:, width:]
    gates = aux_ref[2]
    gated = (normed * gates).astype(BF16)
    d_gate = (aux_ref[3] * normed).astype(BF16).astype(F32)
    q_term = (d_query * aux_ref[0]).astype(BF16)
    g_term = (d_gate * aux_ref[1]).astype(BF16)
    gx_out.buffer[...] = (nt(q_term, w_ref[0]) + nt(g_term, w_ref[1])).astype(BF16)
    gx_out.send()
    x = x_in.get()[...]
    gq = tn(x, q_term)
    gg = tn(x, g_term)
    go = tn(gated, gy_in.get()[...])
    go = jnp.concatenate([go[:, i * width : (i + 1) * width] for i in range(go.shape[1] // width)], axis=0)
    out = spread([gq, gg, go])
    half = out.shape[0] // 2
    scr[0] = out[:half]
    scr[1] = out[half:]
    core = core_ref[0]
    for kv_in, which, result in ((kv_other_in, 1 - core, other_out), (kv_mine_in, core, mine_out)):
        chunks = half // 24
        kv = kv_in.get()[...].astype(F32).reshape(chunks, 16, width)
        joined = jnp.concatenate([kv, scr[which].reshape(chunks, 24, width)], axis=1)
        result.buffer[...] = joined.reshape(chunks * 40, width).astype(BF16)


def pair_kernel(mine_in, other_in, out):
    out.buffer[...] = (mine_in.get()[...].astype(F32) + other_in.get()[...].astype(F32)).astype(BF16)


def sum_kernel(factor, rows_in, out):
    got = rows_in.get()[...]
    chunks = got.shape[0] // 40
    total = jnp.sum(got.astype(F32).reshape(chunks, 40, got.shape[1]), axis=0)
    total = total * factor
    shape = out.buffer.shape
    out.buffer[...] = jnp.broadcast_to(total[None], (chunks, 40, shape[1])).reshape(shape).astype(BF16)


def unfold_kernel(shares, which_ref, source_ref, *refs):
    if shares:
        share_refs, refs = refs[:shares], refs[shares:]
        gx_ref, win_ref, wout_ref, win_scr, wout_scr, sems, share_scr, gx_scr, gx_sems = refs
        loads = [
            pltpu.make_async_copy(share, share_scr.at[i], gx_sems.at[i]) for i, share in enumerate(share_refs)
        ]
        for load in loads:
            load.start()
    else:
        win_ref, wout_ref, win_scr, wout_scr, sems = refs[2:]
    got = source_ref[...].astype(F32)
    width = got.shape[1]
    chunks = got.shape[0] // 40
    size = chunks * 8
    got = got.reshape(chunks, 5, 8, width)
    at = pl.ds(pl.multiple_of(which_ref[0] * size, size), size)
    copies = []
    for place, index in enumerate((2, 3, 0, 1)):
        win_scr[index] = got[:, place].reshape(size, width)
        copies.append(pltpu.make_async_copy(win_scr.at[index], win_ref.at[index, at], sems.at[place]))
        copies[-1].start()
    last = got[:, 4].reshape(size, width)
    rows = wout_scr.shape[0]
    for i in range(size // rows):
        wout_scr[:, i * width : (i + 1) * width] = last[i * rows : (i + 1) * rows]
    copies.append(pltpu.make_async_copy(wout_scr, wout_ref.at[:, at], sems.at[4]))
    copies[-1].start()
    if shares:
        for load in loads:
            load.wait()
        gx_scr[...] = jnp.sum(share_scr[...].astype(F32), axis=0).astype(BF16)
        copies.append(pltpu.make_async_copy(gx_scr, gx_ref, gx_sems.at[shares]))
        copies[-1].start()
    for copy in copies:
        copy.wait()


def unfold(which, source, depth, shares=(), filled=()):
    width = source.shape[1]
    results = [pltpu.HBM((4, depth, width), F32), pltpu.HBM((width, depth), F32)]
    scratch = [
        pltpu.VMEM((4, depth // 2, width), F32),
        pltpu.VMEM((width, depth // 2), F32),
        pltpu.SemaphoreType.DMA((5,)),
    ]
    if shares:
        shape, count = shares[0].shape, len(shares)
        results = [pltpu.HBM(shape, BF16)] + results
        scratch += [
            pltpu.VMEM((count,) + shape, BF16),
            pltpu.VMEM(shape, BF16),
            pltpu.SemaphoreType.DMA((count + 1,)),
        ]
    return pl.pallas_call(
        functools.partial(unfold_kernel, len(shares)),
        out_shape=results,
        in_specs=[SMEM, VMEM] + [ANY] * (len(shares) + len(filled)),
        out_specs=[ANY] * len(results),
        scratch_shapes=scratch,
        input_output_aliases={2 + i: i for i in range(len(filled))},
        compiler_params=PARAMS,
        cost_estimate=pl.CostEstimate(flops=0, bytes_accessed=1 << 20, transcendentals=0),
    )(which, source, *shares, *filled)


class Load:
    def __init__(self, source, buffer=None, sem=None):
        self.buffer, self.copy = source, None
        if buffer is not None:
            self.buffer = buffer
            self.copy = pltpu.make_async_copy(source, buffer, sem)
            self.copy.start()

    def get(self):
        if self.copy is not None:
            self.copy.wait()
            self.copy = None
        return self.buffer


class Store:
    def __init__(self, target, buffer=None, sem=None):
        self.buffer, self.copy, self.started = target, None, False
        self.target, self.sem = target, sem
        if buffer is not None:
            self.buffer = buffer
            self.copy = pltpu.make_async_copy(buffer, target, sem)

    def send(self):
        if self.copy is not None and not self.started:
            self.copy.start()
            self.started = True

    def send_part(self, at):
        pltpu.make_async_copy(self.buffer.at[at], self.target.at[at], self.sem).start()
        self.started = True

    def wait(self):
        if self.copy is not None:
            self.copy.wait()


def call(kernel, outs, ins, scalars=(), scratch=(), near_in=(), raw_in=(), near_out=(), flops=0, moved=0):
    ns, ni, no = len(scalars), len(ins), len(outs)
    far_in = [i for i in range(ni) if i not in near_in and i not in raw_in]
    far_out = [i for i in range(no) if i not in near_out]

    ins = [
        a if i in near_in else pltpu.with_memory_space_constraint(a, pltpu.HBM) for i, a in enumerate(ins)
    ]

    def body(*refs):
        given, refs = refs[:ns], refs[ns:]
        sources, refs = refs[:ni], refs[ni:]
        targets, refs = refs[:no], refs[no:]
        in_bufs, refs = dict(zip(far_in, refs)), refs[len(far_in) :]
        out_bufs, refs = dict(zip(far_out, refs)), refs[len(far_out) :]
        sems, extra = refs[0], refs[1:]
        loads = [
            Load(r, in_bufs[i], sems.at[i]) if i in in_bufs else Load(r) for i, r in enumerate(sources)
        ]
        stores = [
            Store(r, out_bufs[i], sems.at[ni + i]) if i in out_bufs else Store(r)
            for i, r in enumerate(targets)
        ]
        kernel(*given, *loads, *stores, *extra)
        for load in loads:
            load.get()
        for store in stores:
            store.send()
        for store in stores:
            store.wait()

    return pl.pallas_call(
        body,
        out_shape=[
            jax.ShapeDtypeStruct(s, d) if i in near_out else pltpu.HBM(s, d) for i, (s, d) in enumerate(outs)
        ],
        in_specs=[SMEM] * ns + [VMEM if i in near_in else ANY for i in range(ni)],
        out_specs=[VMEM if i in near_out else ANY for i in range(no)],
        scratch_shapes=[pltpu.VMEM(ins[i].shape, ins[i].dtype) for i in far_in]
        + [pltpu.VMEM(*outs[i]) for i in far_out]
        + [pltpu.SemaphoreType.DMA((ni + no,))]
        + list(scratch),
        compiler_params=PARAMS,
        cost_estimate=pl.CostEstimate(flops=flops, bytes_accessed=moved, transcendentals=0),
    )(*scalars, *ins)


def on_device(imp_x, imp_hist, imp_len, owner_map, hist_x, w_in, w_out, grad_y):
    owners = lax.axis_size("dp")
    planes = lax.axis_size("mp")
    rows, depth = imp_x.shape
    width = w_in.shape[2]
    slots = owners * CAP
    events = hist_x.shape[1]
    chips = owners // 2
    place_of = lax.axis_index("dp")
    core = (place_of % 2).reshape(1)
    hist = hist_x[0]
    pairs = [(i, i ^ 1) for i in range(owners)]
    same_core = [[2 * i + c for i in range(chips)] for c in range(2)]

    def swap(a):
        return lax.ppermute(a, "dp", pairs)

    def exchange(a):
        shape = a.shape
        size = shape[0] // owners
        a = a.reshape((owners, size, width) if size % 8 == 0 else (owners, size // 2, 2, width))
        return lax.all_to_all(a, "dp", 0, 0, tiled=True).reshape(shape)

    def exchange_core(a):
        a = a.reshape(chips, a.shape[0] // chips, width)
        a = lax.all_to_all(a, "dp", 0, 0, axis_index_groups=same_core, tiled=True)
        return a.reshape(a.shape[0] * a.shape[1], width)

    hist_rows = imp_hist.reshape(1, rows)
    owner_row = owner_map.reshape(1, owners)
    (send,) = call(
        pre_kernel,
        [((owners * ROWS, width), BF16)],
        (hist_rows, imp_len.reshape(1, rows), owner_row, imp_x, w_in, w_out, grad_y),
        scratch=[
            pltpu.VMEM((2,) + w_in.shape[1:], BF16),
            pltpu.SemaphoreType.DMA(()),
            pltpu.VMEM((owners * ROWS, width), F32),
        ],
        raw_in=(4,),
        near_out=(0,),
        flops=2 * rows * depth * width * 3,
        moved=1 << 20,
    )
    recv = exchange(send)
    keys, values_t, values, keys_t, key_slope, aux, place = call(
        project_kernel,
        [
            ((events, width), BF16),
            ((width, events), BF16),
            ((events, width), BF16),
            ((width, events), BF16),
            ((events, width), BF16),
            ((4, rows, width), F32),
            ((slots, rows), BF16),
        ],
        (w_in, hist, hist_rows, owner_row, imp_x, w_out, grad_y),
        near_out=(0, 1),
        flops=4 * events * depth * width,
        moved=5 << 20,
    )
    heads = width // DH
    back, weights, d_keys, d_att, d_scores, queries = call(
        attend_kernel,
        [
            ((2 * slots, width), BF16),
            ((events, heads * slots), BF16),
            ((events - MOVED, width), BF16),
            ((slots, width), BF16),
            ((MOVED, heads * slots), BF16),
            ((slots, width), BF16),
        ],
        (recv, keys, values_t, values, keys_t),
        scratch=[
            pltpu.VMEM((events, heads * slots), BF16),
            pltpu.VMEM((owners * ROWS, width), F32),
            pltpu.VMEM((2 * slots, width), F32),
        ],
        near_in=(0, 1, 2),
        near_out=(0,),
        flops=10 * events * slots * width,
        moved=8 << 20,
    )
    back = exchange(back)
    half = depth * 2 // 2
    gkv, kv_mine, kv_other, place, aux, x_near, w_near, gy_near = call(
        history_kernel,
        [((events, 2 * width), BF16)]
        + [((half, width), BF16)] * 2
        + [(place.shape, BF16), (aux.shape, F32), (imp_x.shape, BF16)]
        + [((2,) + w_in.shape[1:], BF16), (grad_y.shape, BF16)],
        (d_att, queries, d_scores, d_keys, key_slope, weights, hist, place, aux, imp_x, w_in, grad_y),
        (core,),
        scratch=[
            pltpu.VMEM((2, half, width), BF16),
            pltpu.VMEM((events, heads * slots), BF16),
            pltpu.VMEM((events, 2 * width), BF16),
            pltpu.VMEM((events, depth), BF16),
            pltpu.SemaphoreType.DMA((HISTORY_PARTS,)),
            pltpu.SemaphoreType.DMA(()),
            pltpu.SemaphoreType.DMA((LATE,)),
        ],
        raw_in=(5, 6, 7, 8, 9, 10, 11),
        near_out=(1, 2, 3, 4, 5, 6, 7),
        flops=4 * events * depth * width + 2 * events * slots * width,
        moved=10 << 20,
    )
    back, kv_mine, kv_other = lax.optimization_barrier((back, kv_mine, kv_other))
    half = depth * 3 // 2
    mine, other, gx = call(
        post_kernel,
        [((chips * 40, width), BF16)] * 2 + [((rows, depth), BF16)],
        (back, kv_mine, kv_other, place, aux, x_near, w_near, gy_near),
        (core,),
        scratch=[pltpu.VMEM((2, half, width), F32)],
        near_in=(0, 1, 2, 3, 4, 5, 6, 7),
        near_out=(0, 1, 2),
        flops=2 * rows * depth * width * 5,
        moved=2 << 20,
    )
    other = swap(other)
    (summed,) = call(
        pair_kernel,
        [((chips * 40, width), BF16)],
        (mine, other),
        near_in=(0, 1),
        near_out=(0,),
        moved=1 << 20,
    )
    plane = lax.axis_index("mp")
    share = rows // planes
    parts = [lax.dynamic_slice_in_dim(gx, plane * share, share, 0)]
    for step in range(1, planes):
        part = lax.dynamic_slice_in_dim(gx, (plane + step) % planes * share, share, 0)
        parts.append(lax.ppermute(part, "mp", [(i, (i + step) % planes) for i in range(planes)]))
    factor = (rows * owners) ** (-0.5)
    grad_kv = gkv.reshape(1, events, 2, width)
    summed, grad_kv, *parts = lax.optimization_barrier((exchange_core(summed), grad_kv, *parts))
    (piece,) = call(
        lambda i, o: sum_kernel(factor, i, o),
        [((chips * 40, width), BF16)],
        (summed,),
        near_in=(0,),
        near_out=(0,),
        moved=1 << 20,
    )
    mine = exchange_core(piece)
    other = swap(mine)
    grad_x, *filled = unfold(core, mine, depth, shares=parts)
    grad_w_in, grad_w_out = unfold(1 - core, other, depth, filled=filled)
    return (grad_x, grad_kv, grad_w_in, grad_w_out)


def solution(mesh):
    placed = (
        P("dp", None),
        P("dp", None),
        P("dp"),
        P(),
        P("dp", None, None),
        P(None, None, "mp"),
        P("mp", None),
        P("dp", None),
    )
    return jax.shard_map(
        on_device,
        mesh=mesh,
        in_specs=placed,
        out_specs=(
            P(("dp", "mp"), None),
            P("dp", None, None, "mp"),
            P(None, None, "mp"),
            P("mp", None),
        ),
        check_vma=False,
    )
```
